32 devices in a mesh: expert: 8 (over z, x), tensor: 4 (over y, core).
Axes of the slice: x: 2, y: 2, z: 4, core: 2. Of those that a mesh axis runs over, the one named last changes fastest.
Arguments:
- tokens: bfloat16 [1024, 3584], P('expert', 'tensor'), may hold values from -6 to 6
- routes: int32 [1024, 2], P('expert'), may hold values from 0 to 7, all different within a row; in each aligned block of 128 rows (0 to 127, 128 to 255, ...) at most 40 rows name the same one
- gate_values: float32 [1024, 2], P('expert'), may hold values from 0.05 to 0.5
- probe_rows: bfloat16 [128, 3584], P(None, 'tensor'), may hold values from -6 to 6
- gate_weight: bfloat16 [8, 3584, 2048], P('expert', None, 'tensor'), may hold values from -0.09375 to 0.09375
- up_weight: bfloat16 [8, 3584, 2048], P('expert', None, 'tensor'), may hold values from -0.09375 to 0.09375
- down_weight: bfloat16 [8, 2048, 3584], P('expert', 'tensor'), may hold values from -0.125 to 0.125
- hidden_perm: int32 [8, 2048], P('expert', 'tensor'), may hold values from 0 to 2047, each once within a row
- cluster: int32 [8], replicated, may hold values from 0 to 1, as said below
- owners: int32 [2], replicated, may hold values from 0 to 7, as said below
Outputs:
- mixed: bfloat16 [1024, 3584], P('expert', 'tensor')
- correlation: float32 [8, 2048, 2048], P('expert', 'tensor')
- merged_down: bfloat16 [8, 2048, 3584], P('expert', 'tensor')
The draws below stay inside these ranges and needn't reach their ends.
Inputs may be any that keep to these rules, and one draw needn't show every extreme that they name: `routes`: each row names 2 different experts. Within the rows of one index of the expert axis no expert is named more than 40 times, and in some such block one expert is named exactly 40 times. `hidden_perm`: each row is a permutation of the 2048 hidden units. Every cluster has at least one expert. owners[c] is an expert of cluster c; the owners are distinct.
All inputs are finite; a program needn't handle non-finite values.
Results may differ from the reference program's by a relative error of at most 0.012.
Values may be sent and summed in bfloat16 or wider, within the bound.
No kernel may reach another device: no remote copies, remote signals or barrier semaphores. Data moves between devices by JAX's collectives and lax.ppermute only.
A program may use at most 128 MiB of HBM per device.

```python
import math
import jax
import jax.numpy as jnp
import numpy as np
from jax import lax

D = 3584
FF = 2048
TOK_DEV = 128
PROBE = 128
EXPERTS = 8
TOP = 2
CAP = 40
CLUSTERS = 2
TOKENS = 1024
N_EXPERT = 8
N_TENSOR = 4


def assignment(key):
    middle = (jax.random.permutation(jax.random.fold_in(key, 11), EXPERTS - 2) + 1).astype(jnp.int32)
    ends = jnp.array([EXPERTS - 1, 0], dtype=jnp.int32)
    joined = jnp.concatenate([ends, middle]).astype(jnp.int32)
    head_order = jax.random.permutation(jax.random.fold_in(key, 13), CLUSTERS).astype(jnp.int32)
    head = joined[:CLUSTERS][head_order]
    ordering = jnp.concatenate([head, joined[CLUSTERS:]]).astype(jnp.int32)
    extras = jax.random.randint(jax.random.fold_in(key, 12), (EXPERTS,), 0, CLUSTERS).astype(jnp.int32)
    placing = jnp.arange(EXPERTS, dtype=jnp.int32)
    by_place = jnp.where(placing < CLUSTERS, placing, extras).astype(jnp.int32)
    grouping = jnp.zeros((EXPERTS,), jnp.int32).at[ordering].set(by_place)
    return (grouping, ordering[:CLUSTERS])


def draw_cluster(key, part):
    return assignment(key)[0]


def draw_owners(key, part):
    return assignment(key)[1]


def shard_levels(stream_key, extent, pieces, smallest, largest):
    def one(dim, shards_of):
        steps = jax.random.uniform(jax.random.fold_in(jax.random.fold_in(stream_key, 6), dim), (shards_of,), jnp.float32, smallest / len(pieces), largest / len(pieces))
        return jnp.repeat(jnp.exp(steps), extent[dim] // shards_of).reshape((-1,) + (1,) * (len(extent) - dim - 1))

    loudness = one(*pieces[0])
    for cut in pieces[1:]:
        loudness = loudness * one(*cut)
    return loudness


def deal_out(rng, own, number, rows, number_of, top, limit, slope):
    ranking = jax.random.permutation(rng, number_of)
    packed, ordinary = portions_of(number_of, rows * top, limit, slope, True), portions_of(number_of, rows * top, limit, slope, False)
    places = jnp.arange(number_of)

    def named(tallies, offset_by):
        used = int((tallies > 0).sum())
        fixed = max(1, used // 4)
        passed = fixed + (places - fixed + offset_by * (used - fixed)) % max(1, number_of - fixed)
        return jnp.zeros((number_of,), jnp.int32).at[ranking[jnp.where(places < fixed, places, passed)]].set(jnp.asarray(tallies, jnp.int32))

    tallies = jnp.where(number % 4 == 0, named(packed, number // 4), named(ordinary, number - number // 4 - 1))
    mixed = jax.random.permutation(jax.random.fold_in(own, 3), number_of)
    source_of, receiver = mixed[0:number_of // 2 * 2:2], mixed[1:number_of // 2 * 2:2]
    slack = jnp.minimum(tallies[source_of] - 1, limit - tallies[receiver]) // 2
    slack = jnp.where((source_of == ranking[0]) | (receiver == ranking[0]) | (tallies[receiver] == 0), 0, jnp.maximum(slack, 0))
    passed = jax.random.randint(jax.random.fold_in(own, 4), (number_of // 2,), 0, 1 << 20) % (slack + 1)
    tallies = tallies.at[source_of].add(-passed).at[receiver].add(passed)
    members = jnp.searchsorted(jnp.cumsum(tallies), jnp.arange(rows * top), side="right").astype(jnp.int32)
    table = members.reshape(top, rows).T
    table = table[jax.random.permutation(jax.random.fold_in(own, 1), rows)]
    offset_by = jax.random.randint(jax.random.fold_in(own, 2), (rows, 1), 0, top)
    return jnp.take_along_axis(table, (jnp.arange(top)[None, :] + offset_by) % top, axis=1)


def portions_of(amount, total, reach, slope, full):
    loads = [(1 << 20) // math.isqrt(rank ** slope) + 1 for rank in range(1, amount + 1)]
    largest = reach if full else min(reach, max(-(-total // amount), total * loads[0] // sum(loads)))
    least = 1 if total - largest >= amount - 1 else 0
    holding, spare = [largest] + [least] * (amount - 1), total - largest - least * (amount - 1)
    while spare > 0:
        free = [i for i in range(1, amount) if holding[i] < largest] or [i for i in range(1, amount) if holding[i] < reach]
        mass, remaining = sum([loads[i] for i in free]), spare
        for i in free:
            extra = min(reach - holding[i], max(1, remaining * loads[i] // mass), spare)
            holding[i] = holding[i] + extra
            spare = spare - extra
    return np.array(holding)


def scatter_about(own_key, extent, spread, bound, split=(), held_as=jnp.bfloat16):
    factor_of = shard_levels(own_key, extent, split, -0.22, 0.18) if split else 1.0
    values = jax.random.normal(own_key, extent, jnp.float32) * spread * factor_of
    return jnp.minimum(jnp.maximum(values, -bound), bound).astype(held_as)


def setup_inputs(seed: int = 0) -> dict:
    key_list = jax.random.split(jax.random.key(seed), 11)
    tokens = scatter_about(key_list[0], (TOKENS, D), 1.0, 6.0, ((0, 8), (1, 4)))
    routes_keys = jax.random.split(jax.random.fold_in(key_list[1], 1), TOKENS // TOK_DEV)
    routes_turns = jax.random.permutation(jax.random.fold_in(key_list[1], 3), TOKENS // TOK_DEV)
    routes = jax.vmap(lambda own, number: deal_out(jax.random.fold_in(key_list[1], 2), own, number, TOK_DEV, EXPERTS, TOP, CAP, 2))(routes_keys, routes_turns).reshape((TOKENS, TOP))
    gate_values = jnp.clip(jnp.exp(math.log(0.5) - 2.3025851 * jax.random.uniform(key_list[2], (TOKENS, TOP), jnp.float32) ** shard_levels(key_list[2], (TOKENS, TOP), ((0, 8),), -0.2, 0.2)), 0.05, 0.5)
    probe_rows = scatter_about(key_list[3], (PROBE, D), 1.0, 6.0, ((1, 4),))
    gate_weight = scatter_about(key_list[4], (EXPERTS, D, FF), D ** -0.5, 0.09375, ((0, 8), (2, 4)))
    up_weight = scatter_about(key_list[5], (EXPERTS, D, FF), D ** -0.5, 0.09375, ((0, 8), (2, 4)))
    down_weight = scatter_about(key_list[6], (EXPERTS, FF, D), FF ** -0.5, 0.125, ((0, 8), (1, 4)))
    hidden_perm = jax.vmap(lambda own: jax.random.permutation(own, FF))(jax.random.split(key_list[7], EXPERTS)).reshape((EXPERTS, FF)).astype(jnp.int32)
    cluster = draw_cluster(jax.random.fold_in(key_list[10], 71), 0)
    owners = draw_owners(jax.random.fold_in(key_list[10], 71), 0)
    return {"tokens": tokens, "routes": routes, "gate_values": gate_values, "probe_rows": probe_rows, "gate_weight": gate_weight, "up_weight": up_weight, "down_weight": down_weight, "hidden_perm": hidden_perm, "cluster": cluster, "owners": owners}


def reference(tokens, routes, gate_values, probe_rows, gate_weight, up_weight, down_weight, hidden_perm, cluster, owners):
    routed = EXPERTS * CAP
    width = FF // N_TENSOR
    flat_routes = routes.reshape(N_EXPERT, TOK_DEV * TOP)
    matches = (flat_routes[:, :, None] == jnp.arange(EXPERTS, dtype=jnp.int32)[None, None, :]).astype(jnp.int32)
    slot_rank = jnp.sum((jnp.cumsum(matches, axis=1) - matches) * matches, axis=2).astype(jnp.int32)
    slot_rank = slot_rank.reshape(TOKENS, TOP)
    source_block = (jnp.arange(TOKENS, dtype=jnp.int32) // TOK_DEV)[:, None]
    target_row = (source_block * CAP + slot_rank).astype(jnp.int32)
    spread_tokens = jnp.broadcast_to(tokens[:, None, :], (TOKENS, TOP, D))
    dispatched = jnp.zeros((EXPERTS, routed, D), jnp.bfloat16).at[routes, target_row].set(spread_tokens)

    def expert_pass(operands):
        rows_in, gate_mat, up_mat, down_mat = operands
        stacked = jnp.concatenate([rows_in, probe_rows], axis=0)
        gate_pre = jnp.dot(stacked, gate_mat, preferred_element_type=jnp.float32)
        up_pre = jnp.dot(stacked, up_mat, preferred_element_type=jnp.float32)
        hidden = (jax.nn.silu(gate_pre) * up_pre).astype(jnp.bfloat16)
        routed_hidden = hidden[:routed]
        expert_sum = jnp.zeros((routed, D), jnp.float32)
        for part_index in range(N_TENSOR):
            lower = part_index * width
            partial_sum = jnp.dot(routed_hidden[:, lower:lower + width], down_mat[lower:lower + width], preferred_element_type=jnp.float32).astype(jnp.bfloat16)
            partial_sum = lax.optimization_barrier(partial_sum)
            expert_sum = expert_sum + partial_sum.astype(jnp.float32)
        return expert_sum.astype(jnp.bfloat16), hidden[routed:]

    expert_out, probe_hidden = lax.map(expert_pass, (dispatched, gate_weight, up_weight, down_weight))
    picked = expert_out[routes, target_row]
    mixed = jnp.sum(gate_values[:, :, None] * picked.astype(jnp.float32), axis=1).astype(jnp.bfloat16)
    owner_of = owners[cluster]
    partner = probe_hidden[owner_of]
    correlation = jnp.einsum("epi,epj->eij", probe_hidden.astype(jnp.float32), partner.astype(jnp.float32), precision=lax.Precision.HIGHEST) / PROBE
    aligned = jax.vmap(lambda weights, order: weights[order])(down_weight, hidden_perm)
    cluster_total = jax.ops.segment_sum(aligned.astype(jnp.float32), cluster, num_segments=CLUSTERS)
    counts = jax.ops.segment_sum(jnp.ones((EXPERTS,), jnp.float32), cluster, num_segments=CLUSTERS)
    cluster_mean = (cluster_total * (1.0 / counts)[:, None, None]).astype(jnp.bfloat16)
    merged_down = jnp.zeros((EXPERTS, FF, D), jnp.bfloat16).at[owners].set(cluster_mean)
    return (mixed, correlation, merged_down)
```

```python
import functools

import jax
import jax.numpy as jnp
from jax import lax
from jax.experimental import pallas as pl
from jax.experimental.pallas import tpu as pltpu
from jax.sharding import PartitionSpec as P


def xor_permute(value, axis, size, k):
    return lax.ppermute(value, axis, [(i, i ^ k) for i in range(size)])


def gather_tensor(value, size):
    held = {0: value}
    bit = size // 2
    while bit:
        for k in sorted(held):
            held[k ^ bit] = xor_permute(held[k], "tensor", size, bit)
        bit //= 2
    return [held[k] for k in range(size)]


def scatter_tensor(parts, size):
    held = dict(enumerate(parts))
    bit = 1
    while bit < size:
        for k in sorted(held):
            if k & bit:
                arrived = xor_permute(
                    held.pop(k).astype(jnp.bfloat16), "tensor", size, bit
                )
                held[k ^ bit] = held[k ^ bit] + arrived.astype(jnp.float32)
        bit *= 2
    return held[0]


def ffn_kernel(count, where_ref, *refs):
    parts = refs[:count]
    gate_ref, up_ref, out_ref, gate_sum, up_sum = refs[count:]
    step = pl.program_id(0)

    @pl.when(step == 0)
    def _():
        gate_sum[...] = jnp.zeros_like(gate_sum)
        up_sum[...] = jnp.zeros_like(up_sum)

    for k in range(count):

        @pl.when(step == k)
        def _(k=k):
            rows = parts[k][...]
            gate_sum[...] += jnp.dot(rows, gate_ref[0], preferred_element_type=jnp.float32)
            up_sum[...] += jnp.dot(rows, up_ref[0], preferred_element_type=jnp.float32)

    @pl.when(step == count - 1)
    def _():
        gate = gate_sum[...]
        out_ref[...] = (gate / (1.0 + jnp.exp(-gate)) * up_sum[...]).astype(out_ref.dtype)


def ffn(parts, gate_weight, up_weight, t):
    count = len(parts)
    rows, width = parts[0].shape
    units = gate_weight.shape[2]
    weight_spec = pl.BlockSpec((1, width, units), lambda k, where: (0, where[0] ^ k, 0))
    return pl.pallas_call(
        functools.partial(ffn_kernel, count),
        out_shape=jax.ShapeDtypeStruct((rows, units), jnp.bfloat16),
        grid_spec=pltpu.PrefetchScalarGridSpec(
            num_scalar_prefetch=1,
            grid=(count,),
            in_specs=[pl.BlockSpec((rows, width), lambda k, where: (0, 0))] * count
            + [weight_spec, weight_spec],
            out_specs=pl.BlockSpec((rows, units), lambda k, where: (0, 0)),
            scratch_shapes=[pltpu.VMEM((rows, units), jnp.float32)] * 2,
        ),
        compiler_params=pltpu.CompilerParams(vmem_limit_bytes=48 * 1024 * 1024),
        cost_estimate=pl.CostEstimate(
            flops=4 * rows * width * count * units,
            bytes_accessed=2 * (2 * width * count * units + rows * width * count + rows * units),
            transcendentals=rows * units,
        ),
        name="ffn",
    )(t.reshape(1).astype(jnp.int32), *parts, gate_weight, up_weight)


def chunks_of(width):
    lanes = 128
    if width % lanes or width < 2 * lanes:
        return [(0, width)]
    first = (width // lanes + 1) // 2 * lanes
    return [(0, first), (first, width - first)]


def one_hot_rows(positions, source):
    rows = source.shape[0]
    selector = (positions[:, None] == jnp.arange(rows, dtype=jnp.int32)[None, :]).astype(
        jnp.bfloat16
    )
    return jnp.dot(selector, source, preferred_element_type=jnp.float32).astype(jnp.bfloat16)


def columns_to_device(own, t, nt, off, width):
    block = own.shape[1] // nt
    found = []
    for k in range(nt):
        piece = lax.dynamic_slice(own, (0, (t ^ k) * block + off), (own.shape[0], width))
        found.append(xor_permute(piece, "tensor", nt, k) if k else piece)
    return jnp.concatenate(found, axis=0)


def rows_to_device(pieces, t, nt):
    found = []
    for k in range(nt):
        piece = lax.dynamic_index_in_dim(pieces, t ^ k, 0, keepdims=False)
        found.append(xor_permute(piece, "tensor", nt, k) if k else piece)
    return found


def merge_two(own, perm, cluster, owners, e, t, ne, nt):
    rows, model = own.shape
    half = ne // 2
    block = model // nt
    sub = rows // half
    q, side = e % half, e // half
    placed = ((perm // rows) ^ t) * rows + perm % rows
    placed = placed.reshape(nt, half, sub)
    member = cluster[(e ^ jnp.arange(half, dtype=jnp.int32))]
    inverse = 1.0 / jnp.sum(
        (cluster[None, :] == jnp.arange(2, dtype=jnp.int32)[:, None]).astype(jnp.float32), axis=1
    )
    owner_side = owners // half
    keep = jnp.where(owner_side[0] == side, 0, 1)
    give = jnp.where(owner_side[0] != side, 0, 1)
    spans = chunks_of(block)

    partials = []
    for off, width in spans:
        source = columns_to_device(own, t, nt, off, width)
        arrived = []
        for k in range(half):
            positions = lax.dynamic_index_in_dim(placed, q ^ k, 1, keepdims=False).reshape(-1)
            aligned = one_hot_rows(positions, source)
            arrived.append(xor_permute(aligned, "expert", ne, k) if k else aligned)
        partials.append(arrived)

    def partial_of(arrived, which):
        total = jnp.zeros(arrived[0].shape, jnp.float32)
        for k in range(half):
            total = total + jnp.where(member[k] == which, arrived[k].astype(jnp.float32), 0.0)
        return total

    def finish(partials, kept, given):
        gathered = []
        for arrived, (off, width) in zip(partials, spans):
            sent = partial_of(arrived, given).astype(jnp.bfloat16)
            other = xor_permute(sent, "expert", ne, half)
            mean = (
                (partial_of(arrived, kept) + other.astype(jnp.float32)) * inverse[kept]
            ).astype(jnp.bfloat16)
            back = rows_to_device(mean.reshape(nt, sub, width), t, nt)
            lines = jnp.stack(back)
            gathered.append(
                [xor_permute(lines, "expert", ne, k) if k else lines for k in range(half)]
            )
        mine = owners[kept] == e
        order_t = jnp.arange(nt, dtype=jnp.int32) ^ t
        out = []
        for j in range(half):
            wide = []
            for group in gathered:
                chosen = group[0]
                for k in range(1, half):
                    chosen = jnp.where((q ^ j) == k, group[k], chosen)
                wide.append(chosen)
            out.append(jnp.concatenate(wide, axis=2))
        joined = jnp.stack(out)
        ordered = []
        for b in range(nt):
            chosen = joined[:, 0]
            for k in range(1, nt):
                chosen = jnp.where(order_t[b] == k, joined[:, k], chosen)
            ordered.append(chosen)
        whole = jnp.concatenate(ordered, axis=2).reshape(rows, model)
        return jnp.where(mine, whole, jnp.zeros_like(whole))

    first = finish(partials, keep, give)

    def second(args):
        first, partials = args
        return first + finish(partials, 1, 1)

    return lax.cond(
        owner_side[0] == owner_side[1], second, lambda args: args[0], (first, partials)
    )


def merge_any(own, perm, cluster, owners, e, t, ne, nt):
    rows, model = own.shape
    block = model // nt
    clusters = owners.shape[0]
    sub = rows // ne
    placed = ((perm // rows) ^ t) * rows + perm % rows
    placed = placed.reshape(nt, ne, sub).transpose(1, 0, 2).reshape(-1)
    aligned = one_hot_rows(placed, columns_to_device(own, t, nt, 0, block))
    arrived = lax.all_to_all(aligned, "expert", split_axis=0, concat_axis=0, tiled=True)
    arrived = arrived.reshape(ne, nt, sub, block)
    member = cluster[None, :] == jnp.arange(clusters, dtype=jnp.int32)[:, None]
    inverse = 1.0 / jnp.sum(member.astype(jnp.float32), axis=1)
    means = []
    for c in range(clusters):
        total = jnp.sum(
            jnp.where(member[c][:, None, None, None], arrived.astype(jnp.float32), 0.0), axis=0
        )
        means.append((total * inverse[c]).astype(jnp.bfloat16))
    means = jnp.stack(means, axis=1)
    back = lax.all_to_all(
        means.reshape(nt * clusters * sub, block), "tensor", split_axis=0, concat_axis=0, tiled=True
    ).reshape(nt, clusters, sub, block)
    lines = back.transpose(1, 2, 0, 3).reshape(clusters, sub, model)
    outgoing = jnp.zeros((ne, sub, model), jnp.bfloat16).at[owners].set(lines)
    return lax.all_to_all(
        outgoing.reshape(ne * sub, model), "expert", split_axis=0, concat_axis=0, tiled=True
    )


def on_device(
    tokens,
    routes,
    gate_values,
    probe_rows,
    gate_weight,
    up_weight,
    down_weight,
    hidden_perm,
    cluster,
    owners,
):
    ne = lax.axis_size("expert")
    nt = lax.axis_size("tensor")
    e = lax.axis_index("expert").astype(jnp.int32)
    t = lax.axis_index("tensor").astype(jnp.int32)
    tok_rows, top = routes.shape
    capacity = tok_rows * top * 5 // (4 * ne)
    own = down_weight[0]
    model = own.shape[1]
    block = model // nt

    perm = lax.all_gather(hidden_perm[0], "tensor", axis=0, tiled=True)
    merge = merge_two if ne == 8 and owners.shape[0] == 2 else merge_any
    merged = merge(own, perm, cluster, owners, e, t, ne, nt)

    flat = routes.reshape(-1)
    pairs = jnp.arange(flat.shape[0], dtype=jnp.int32)
    earlier = (flat[:, None] == flat[None, :]) & (pairs[None, :] < pairs[:, None])
    target = flat * capacity + jnp.sum(earlier.astype(jnp.int32), axis=1)
    target = target.reshape(tok_rows, top)
    slots = jnp.arange(ne * capacity, dtype=jnp.int32)
    selector = jnp.zeros((ne * capacity, tok_rows), jnp.bool_)
    for k in range(top):
        selector = selector | (slots[:, None] == target[:, k][None, :])
    outgoing = jnp.dot(
        selector.astype(jnp.bfloat16), tokens, preferred_element_type=jnp.float32
    ).astype(jnp.bfloat16)
    arrived = lax.all_to_all(outgoing, "expert", split_axis=0, concat_axis=0, tiled=True)
    routed = arrived.shape[0]
    stacked = jnp.concatenate([arrived, probe_rows], axis=0)
    hidden = ffn(gather_tensor(stacked, nt), gate_weight, up_weight, t)
    routed_hidden, probe_hidden = hidden[:routed], hidden[routed:]

    parts = [
        jnp.dot(
            routed_hidden,
            lax.dynamic_slice(own, (0, (t ^ k) * block), (own.shape[0], block)),
            preferred_element_type=jnp.float32,
        )
        for k in range(nt)
    ]
    returned = scatter_tensor(parts, nt).astype(jnp.bfloat16)
    home = lax.all_to_all(returned, "expert", split_axis=0, concat_axis=0, tiled=True)
    chooser = (target.T.reshape(-1)[:, None] == slots[None, :]).astype(jnp.bfloat16)
    picked = jnp.dot(chooser, home, preferred_element_type=jnp.float32)
    picked = picked.reshape(top, tok_rows, block)
    mixed = jnp.sum(gate_values.T[:, :, None] * picked, axis=0).astype(jnp.bfloat16)

    everyone = lax.all_gather(probe_hidden, "expert", axis=0)
    partner = lax.dynamic_index_in_dim(everyone, owners[cluster[e]], 0, keepdims=False)
    partner_full = lax.all_gather(partner, "tensor", axis=1, tiled=True)
    correlation = (
        lax.dot_general(
            probe_hidden, partner_full, (((0,), (0,)), ((), ())), preferred_element_type=jnp.float32
        )
        / probe_hidden.shape[0]
    )
    return (mixed, correlation[None], merged[None])


def solution(mesh):
    in_specs = (
        P("expert", "tensor"),
        P("expert", None),
        P("expert", None),
        P(None, "tensor"),
        P("expert", None, "tensor"),
        P("expert", None, "tensor"),
        P("expert", "tensor", None),
        P("expert", "tensor"),
        P(),
        P(),
    )
    out_specs = (P("expert", "tensor"), P("expert", "tensor", None), P("expert", "tensor", None))
    return jax.shard_map(
        on_device, mesh=mesh, in_specs=in_specs, out_specs=out_specs, check_vma=False
    )
```

```python
import functools

import jax
import jax.numpy as jnp
from jax import lax
from jax.experimental import pallas as pl
from jax.experimental.pallas import tpu as pltpu
from jax.sharding import PartitionSpec as P


def xor_permute(value, axis, size, k):
    return lax.ppermute(value, axis, [(i, i ^ k) for i in range(size)])


def gather_tensor(value, size):
    held = {0: value}
    bit = size // 2
    while bit:
        for k in sorted(held):
            held[k ^ bit] = xor_permute(held[k], "tensor", size, bit)
        bit //= 2
    return [held[k] for k in range(size)]


def scatter_tensor(parts, size):
    held = dict(enumerate(parts))
    bit = 1
    while bit < size:
        for k in sorted(held):
            if k & bit:
                arrived = xor_permute(
                    held.pop(k).astype(jnp.bfloat16), "tensor", size, bit
                )
                held[k ^ bit] = held[k ^ bit] + arrived.astype(jnp.float32)
        bit *= 2
    return held[0]


def ffn_kernel(count, where_ref, *refs):
    parts = refs[:count]
    gate_ref, up_ref, out_ref, gate_sum, up_sum = refs[count:]
    step = pl.program_id(0)

    @pl.when(step == 0)
    def _():
        gate_sum[...] = jnp.zeros_like(gate_sum)
        up_sum[...] = jnp.zeros_like(up_sum)

    for k in range(count):

        @pl.when(step == k)
        def _(k=k):
            rows = parts[k][...]
            gate_sum[...] += jnp.dot(rows, gate_ref[0], preferred_element_type=jnp.float32)
            up_sum[...] += jnp.dot(rows, up_ref[0], preferred_element_type=jnp.float32)

    @pl.when(step == count - 1)
    def _():
        gate = gate_sum[...]
        out_ref[...] = (gate / (1.0 + jnp.exp(-gate)) * up_sum[...]).astype(out_ref.dtype)


def ffn(parts, gate_weight, up_weight, t):
    count = len(parts)
    rows, width = parts[0].shape
    units = gate_weight.shape[2]
    weight_spec = pl.BlockSpec((1, width, units), lambda k, where: (0, where[0] ^ k, 0))
    return pl.pallas_call(
        functools.partial(ffn_kernel, count),
        out_shape=jax.ShapeDtypeStruct((rows, units), jnp.bfloat16),
        grid_spec=pltpu.PrefetchScalarGridSpec(
            num_scalar_prefetch=1,
            grid=(count,),
            in_specs=[pl.BlockSpec((rows, width), lambda k, where: (0, 0))] * count
            + [weight_spec, weight_spec],
            out_specs=pl.BlockSpec((rows, units), lambda k, where: (0, 0)),
            scratch_shapes=[pltpu.VMEM((rows, units), jnp.float32)] * 2,
        ),
        compiler_params=pltpu.CompilerParams(vmem_limit_bytes=48 * 1024 * 1024),
        cost_estimate=pl.CostEstimate(
            flops=4 * rows * width * count * units,
            bytes_accessed=2 * (2 * width * count * units + rows * width * count + rows * units),
            transcendentals=rows * units,
        ),
        name="ffn",
    )(t.reshape(1).astype(jnp.int32), *parts, gate_weight, up_weight)


def chunks_of(width):
    lanes = 128
    if width % lanes or width < 2 * lanes:
        return [(0, width)]
    first = (width // lanes + 1) // 2 * lanes
    return [(0, first), (first, width - first)]


def one_hot(positions, count):
    selector = (positions[:, None] == jnp.arange(count, dtype=jnp.int32)[None, :]).astype(
        jnp.bfloat16
    )
    return lax.optimization_barrier(selector)


def pick_rows(selector, source):
    return jnp.dot(selector, source, preferred_element_type=jnp.float32).astype(jnp.bfloat16)


def after(value, *others):
    return lax.optimization_barrier((value,) + others)[0]


def columns_to_device(own, t, nt, off, width):
    block = own.shape[1] // nt
    found = []
    for k in range(nt):
        piece = lax.dynamic_slice(own, (0, (t ^ k) * block + off), (own.shape[0], width))
        found.append(xor_permute(piece, "tensor", nt, k) if k else piece)
    return jnp.concatenate(found, axis=0)


def rows_to_device(pieces, nt):
    return [xor_permute(pieces[k], "tensor", nt, k) if k else pieces[k] for k in range(nt)]


def merge_two(own, perm, cluster, owners, e, t, ne, nt, beside):
    rows, model = own.shape
    half = ne // 2
    block = model // nt
    sub = rows // half
    q, side = e % half, e // half
    placed = ((perm // rows) ^ t) * rows + perm % rows
    placed = placed.reshape(nt, half, sub)
    member = cluster[(e ^ jnp.arange(half, dtype=jnp.int32))]
    inverse = 1.0 / jnp.sum(
        (cluster[None, :] == jnp.arange(2, dtype=jnp.int32)[:, None]).astype(jnp.float32), axis=1
    )
    owner_side = owners // half
    keep = jnp.where(owner_side[0] == side, 0, 1)
    give = jnp.where(owner_side[0] != side, 0, 1)
    spans = chunks_of(block)
    order = [(q ^ k) for k in range(half)]
    selectors = [
        one_hot(lax.dynamic_index_in_dim(placed, j, 1, keepdims=False).reshape(-1), rows * nt)
        for j in order
    ]

    partials = []
    for off, width in spans:
        source = columns_to_device(own, t, nt, off, width)
        arrived = [None] * half
        for k in list(range(1, half)) + [0]:
            aligned = pick_rows(selectors[k], source)
            arrived[k] = xor_permute(aligned, "expert", ne, k) if k else aligned
        partials.append(arrived)

    def partial_of(arrived, which):
        total = jnp.zeros(arrived[0].shape, jnp.float32)
        for k in range(half):
            total = total + jnp.where(member[k] == which, arrived[k].astype(jnp.float32), 0.0)
        return total

    def finish(partials, kept, given, beside=()):
        gathered = []
        for place, (arrived, (off, width)) in enumerate(zip(partials, spans)):
            sent = partial_of(arrived, given).astype(jnp.bfloat16)
            if place < len(beside):
                sent = after(sent, beside[place])
            other = xor_permute(sent, "expert", ne, half)
            mean = (
                (partial_of(arrived, kept) + other.astype(jnp.float32)) * inverse[kept]
            ).astype(jnp.bfloat16)
            lines = jnp.stack(rows_to_device(mean.reshape(nt, sub, width), nt))
            gathered.append(
                [xor_permute(lines, "expert", ne, k) if k else lines for k in range(half)]
            )
        mine = owners[kept] == e
        order_t = jnp.arange(nt, dtype=jnp.int32) ^ t
        out = []
        for j in range(half):
            wide = []
            for group in gathered:
                chosen = group[0]
                for k in range(1, half):
                    chosen = jnp.where((q ^ j) == k, group[k], chosen)
                wide.append(chosen)
            out.append(jnp.concatenate(wide, axis=2))
        joined = jnp.stack(out)
        ordered = []
        for b in range(nt):
            chosen = joined[:, 0]
            for k in range(1, nt):
                chosen = jnp.where(order_t[b] == k, joined[:, k], chosen)
            ordered.append(chosen)
        whole = jnp.concatenate(ordered, axis=2).reshape(rows, model)
        return jnp.where(mine, whole, jnp.zeros_like(whole))

    first = finish(partials, keep, give, beside)

    def second(args):
        first, partials = args
        return first + finish(partials, 1, 1)

    return lax.cond(
        owner_side[0] == owner_side[1], second, lambda args: args[0], (first, partials)
    )


def merge_any(own, perm, cluster, owners, e, t, ne, nt, beside):
    rows, model = own.shape
    block = model // nt
    clusters = owners.shape[0]
    sub = rows // ne
    placed = ((perm // rows) ^ t) * rows + perm % rows
    placed = placed.reshape(nt, ne, sub).transpose(1, 0, 2).reshape(-1)
    aligned = pick_rows(
        one_hot(placed, rows * nt), columns_to_device(own, t, nt, 0, block)
    )
    arrived = lax.all_to_all(aligned, "expert", split_axis=0, concat_axis=0, tiled=True)
    arrived = arrived.reshape(ne, nt, sub, block)
    member = cluster[None, :] == jnp.arange(clusters, dtype=jnp.int32)[:, None]
    inverse = 1.0 / jnp.sum(member.astype(jnp.float32), axis=1)
    means = []
    for c in range(clusters):
        total = jnp.sum(
            jnp.where(member[c][:, None, None, None], arrived.astype(jnp.float32), 0.0), axis=0
        )
        means.append((total * inverse[c]).astype(jnp.bfloat16))
    back = jnp.stack(rows_to_device(jnp.stack(means, axis=1), nt))
    back = jnp.take(back, jnp.arange(nt, dtype=jnp.int32) ^ t, axis=0)
    lines = back.transpose(1, 2, 0, 3).reshape(clusters, sub, model)
    outgoing = jnp.zeros((ne, sub, model), jnp.bfloat16).at[owners].set(lines)
    return lax.all_to_all(
        outgoing.reshape(ne * sub, model), "expert", split_axis=0, concat_axis=0, tiled=True
    )


def on_device(
    tokens,
    routes,
    gate_values,
    probe_rows,
    gate_weight,
    up_weight,
    down_weight,
    hidden_perm,
    cluster,
    owners,
):
    ne = lax.axis_size("expert")
    nt = lax.axis_size("tensor")
    e = lax.axis_index("expert").astype(jnp.int32)
    t = lax.axis_index("tensor").astype(jnp.int32)
    tok_rows, top = routes.shape
    capacity = tok_rows * top * 5 // (4 * ne)
    own = down_weight[0]
    model = own.shape[1]
    block = model // nt

    perm = jnp.concatenate(gather_tensor(hidden_perm[0], nt))

    flat = routes.reshape(-1)
    pairs = jnp.arange(flat.shape[0], dtype=jnp.int32)
    earlier = (flat[:, None] == flat[None, :]) & (pairs[None, :] < pairs[:, None])
    target = flat * capacity + jnp.sum(earlier.astype(jnp.int32), axis=1)
    target = target.reshape(tok_rows, top)
    slots = jnp.arange(ne * capacity, dtype=jnp.int32)
    selector = jnp.zeros((ne * capacity, tok_rows), jnp.bool_)
    for k in range(top):
        selector = selector | (slots[:, None] == target[:, k][None, :])
    outgoing = jnp.dot(
        selector.astype(jnp.bfloat16), tokens, preferred_element_type=jnp.float32
    ).astype(jnp.bfloat16)
    arrived = lax.all_to_all(outgoing, "expert", split_axis=0, concat_axis=0, tiled=True)
    routed = arrived.shape[0]
    stacked = jnp.concatenate([arrived, probe_rows], axis=0)
    hidden = ffn(gather_tensor(stacked, nt), gate_weight, up_weight, t)
    routed_hidden, probe_hidden = hidden[:routed], hidden[routed:]

    parts = [
        jnp.dot(
            routed_hidden,
            lax.dynamic_slice(own, (0, (t ^ k) * block), (own.shape[0], block)),
            preferred_element_type=jnp.float32,
        )
        for k in range(nt)
    ]
    returned = scatter_tensor(parts, nt).astype(jnp.bfloat16)
    home = lax.all_to_all(returned, "expert", split_axis=0, concat_axis=0, tiled=True)
    chooser = (target.T.reshape(-1)[:, None] == slots[None, :]).astype(jnp.bfloat16)
    picked = jnp.dot(chooser, home, preferred_element_type=jnp.float32)
    picked = picked.reshape(top, tok_rows, block)
    mixed = jnp.sum(gate_values.T[:, :, None] * picked, axis=0).astype(jnp.bfloat16)

    merge = merge_two if ne == 8 and owners.shape[0] == 2 else merge_any
    merged = merge(own, perm, cluster, owners, e, t, ne, nt, (hidden, returned))

    everyone = lax.all_gather(probe_hidden, "expert", axis=0)
    partner = lax.dynamic_index_in_dim(everyone, owners[cluster[e]], 0, keepdims=False)
    partner_full = lax.all_gather(partner, "tensor", axis=1, tiled=True)
    correlation = (
        lax.dot_general(
            probe_hidden, partner_full, (((0,), (0,)), ((), ())), preferred_element_type=jnp.float32
        )
        / probe_hidden.shape[0]
    )
    return (mixed, correlation[None], merged[None])


def solution(mesh):
    in_specs = (
        P("expert", "tensor"),
        P("expert", None),
        P("expert", None),
        P(None, "tensor"),
        P("expert", None, "tensor"),
        P("expert", None, "tensor"),
        P("expert", "tensor", None),
        P("expert", "tensor"),
        P(),
        P(),
    )
    out_specs = (P("expert", "tensor"), P("expert", "tensor", None), P("expert", "tensor", None))
    return jax.shard_map(
        on_device, mesh=mesh, in_specs=in_specs, out_specs=out_specs, check_vma=False
    )
```

```python
import functools

import jax
import jax.numpy as jnp
from jax import lax
from jax.experimental import pallas as pl
from jax.experimental.pallas import tpu as pltpu
from jax.sharding import PartitionSpec as P


def xor_permute(value, axis, size, k):
    return lax.ppermute(value, axis, [(i, i ^ k) for i in range(size)])


def gather_tensor(value, size):
    held = {0: value}
    bit = size // 2
    while bit:
        for k in sorted(held):
            held[k ^ bit] = xor_permute(held[k], "tensor", size, bit)
        bit //= 2
    return [held[k] for k in range(size)]


def scatter_tensor(parts, size):
    held = dict(enumerate(parts))
    bit = 1
    while bit < size:
        for k in sorted(held):
            if k & bit:
                arrived = xor_permute(
                    held.pop(k).astype(jnp.bfloat16), "tensor", size, bit
                )
                held[k ^ bit] = held[k ^ bit] + arrived.astype(jnp.float32)
        bit *= 2
    return held[0]


def ffn_kernel(count, where_ref, *refs):
    parts = refs[:count]
    gate_ref, up_ref, out_ref, gate_sum, up_sum = refs[count:]
    step = pl.program_id(0)

    @pl.when(step == 0)
    def _():
        gate_sum[...] = jnp.zeros_like(gate_sum)
        up_sum[...] = jnp.zeros_like(up_sum)

    for k in range(count):

        @pl.when(step == k)
        def _(k=k):
            rows = parts[k][...]
            gate_sum[...] += jnp.dot(rows, gate_ref[0], preferred_element_type=jnp.float32)
            up_sum[...] += jnp.dot(rows, up_ref[0], preferred_element_type=jnp.float32)

    @pl.when(step == count - 1)
    def _():
        gate = gate_sum[...]
        out_ref[...] = (gate / (1.0 + jnp.exp(-gate)) * up_sum[...]).astype(out_ref.dtype)


def ffn(parts, gate_weight, up_weight, t):
    count = len(parts)
    rows, width = parts[0].shape
    units = gate_weight.shape[2]
    weight_spec = pl.BlockSpec((1, width, units), lambda k, where: (0, where[0] ^ k, 0))
    return pl.pallas_call(
        functools.partial(ffn_kernel, count),
        out_shape=jax.ShapeDtypeStruct((rows, units), jnp.bfloat16),
        grid_spec=pltpu.PrefetchScalarGridSpec(
            num_scalar_prefetch=1,
            grid=(count,),
            in_specs=[pl.BlockSpec((rows, width), lambda k, where: (0, 0))] * count
            + [weight_spec, weight_spec],
            out_specs=pl.BlockSpec((rows, units), lambda k, where: (0, 0)),
            scratch_shapes=[pltpu.VMEM((rows, units), jnp.float32)] * 2,
        ),
        compiler_params=pltpu.CompilerParams(vmem_limit_bytes=48 * 1024 * 1024),
        cost_estimate=pl.CostEstimate(
            flops=4 * rows * width * count * units,
            bytes_accessed=2 * (2 * width * count * units + rows * width * count + rows * units),
            transcendentals=rows * units,
        ),
        name="ffn",
    )(t.reshape(1).astype(jnp.int32), *parts, gate_weight, up_weight)


def chunks_of(width):
    lanes = 128
    if width % lanes or width < 2 * lanes:
        return [(0, width)]
    first = (width // lanes + 1) // 2 * lanes
    return [(0, first), (first, width - first)]


def one_hot(positions, count):
    selector = (positions[:, None] == jnp.arange(count, dtype=jnp.int32)[None, :]).astype(
        jnp.bfloat16
    )
    return lax.optimization_barrier(selector)


def pick_rows(selector, source):
    return jnp.dot(selector, source, preferred_element_type=jnp.float32).astype(jnp.bfloat16)


def after(value, *others):
    return lax.optimization_barrier((value,) + others)[0]


def columns_to_device(own, t, nt, off, width):
    block = own.shape[1] // nt
    found = []
    for k in range(nt):
        piece = lax.dynamic_slice(own, (0, (t ^ k) * block + off), (own.shape[0], width))
        found.append(xor_permute(piece, "tensor", nt, k) if k else piece)
    return found


def rows_to_device(pieces, nt):
    return [xor_permute(pieces[k], "tensor", nt, k) if k else pieces[k] for k in range(nt)]


T_AT, Q_AT, KEEP_AT, GIVE_AT, MINE_AT, MEMBER_AT = range(6)
BIG_VMEM = 48 * 1024 * 1024


def full_spec(shape):
    return pl.BlockSpec(shape, memory_space=pltpu.VMEM)


def align_kernel(nt, half, sub, flags_ref, place_ref, *refs):
    sources, outs = refs[:nt], refs[nt:]
    rows, width = sources[0].shape
    lane = lax.broadcasted_iota(jnp.int32, (rows, rows), 1)
    q = flags_ref[Q_AT]
    for k in range(half):
        first = pl.multiple_of((q ^ k) * sub, sub)
        place = jnp.concatenate(
            [place_ref[pl.ds(first + b * half * sub, sub), :] for b in range(nt)], axis=0
        )
        total = jnp.zeros((rows, width), jnp.float32)
        for m in range(nt):
            selector = jnp.where(place - m * rows == lane, 1.0, 0.0).astype(jnp.bfloat16)
            total = total + jnp.dot(
                selector, sources[m][...], preferred_element_type=jnp.float32
            )
        outs[k][...] = total.astype(jnp.bfloat16)


def align(flags, place, sources, half, sub):
    nt = len(sources)
    rows, width = sources[0].shape
    piece = jax.ShapeDtypeStruct((rows, width), jnp.bfloat16)
    return pl.pallas_call(
        functools.partial(align_kernel, nt, half, sub),
        out_shape=[piece] * half,
        in_specs=[pl.BlockSpec(memory_space=pltpu.SMEM), full_spec(place.shape)]
        + [full_spec((rows, width))] * nt,
        out_specs=[full_spec((rows, width))] * half,
        compiler_params=pltpu.CompilerParams(vmem_limit_bytes=BIG_VMEM),
        cost_estimate=pl.CostEstimate(
            flops=2 * half * nt * rows * rows * width,
            bytes_accessed=2 * (half + nt) * rows * width,
            transcendentals=0,
        ),
        name="align",
    )(flags, place, *sources)


def sums_kernel(half, flags_ref, *refs):
    parts, sent_ref, kept_ref = refs[:half], refs[half], refs[half + 1]
    keep, give = flags_ref[KEEP_AT], flags_ref[GIVE_AT]
    sent = jnp.zeros(sent_ref.shape, jnp.float32)
    kept = jnp.zeros(kept_ref.shape, jnp.float32)
    for k in range(half):
        member = flags_ref[MEMBER_AT + k]
        part = parts[k][...].astype(jnp.float32)
        sent = sent + jnp.where(member == give, part, 0.0)
        kept = kept + jnp.where(member == keep, part, 0.0)
    sent_ref[...] = sent.astype(sent_ref.dtype)
    kept_ref[...] = kept


def sums(flags, parts, tile=64):
    rows, width = parts[0].shape
    tile = min(tile, rows)
    spec = pl.BlockSpec((tile, width), lambda i: (i, 0))
    return pl.pallas_call(
        functools.partial(sums_kernel, len(parts)),
        grid=(rows // tile,),
        out_shape=[
            jax.ShapeDtypeStruct((rows, width), jnp.bfloat16),
            jax.ShapeDtypeStruct((rows, width), jnp.float32),
        ],
        in_specs=[pl.BlockSpec(memory_space=pltpu.SMEM)] + [spec] * len(parts),
        out_specs=[spec, spec],
        cost_estimate=pl.CostEstimate(
            flops=2 * len(parts) * rows * width,
            bytes_accessed=2 * (len(parts) + 3) * rows * width,
            transcendentals=0,
        ),
        name="sums",
    )(flags, *parts)


def mean_kernel(scale_ref, kept_ref, other_ref, *outs):
    sub = outs[0].shape[0]
    scale = scale_ref[0]
    for m, out in enumerate(outs):
        at = pl.ds(m * sub, sub)
        total = kept_ref[at, :] + other_ref[at, :].astype(jnp.float32)
        out[...] = (total * scale).astype(out.dtype)


def mean_of(scale, kept, other, nt):
    rows, width = kept.shape
    sub = rows // nt
    return pl.pallas_call(
        mean_kernel,
        out_shape=[jax.ShapeDtypeStruct((sub, width), jnp.bfloat16)] * nt,
        in_specs=[pl.BlockSpec(memory_space=pltpu.SMEM)] + [full_spec((rows, width))] * 2,
        out_specs=[full_spec((sub, width))] * nt,
        compiler_params=pltpu.CompilerParams(vmem_limit_bytes=BIG_VMEM),
        cost_estimate=pl.CostEstimate(
            flops=2 * rows * width, bytes_accessed=8 * rows * width, transcendentals=0
        ),
        name="mean",
    )(scale, kept, other)


def assemble_kernel(half, nt, spans, flags_ref, *refs):
    count = half * len(spans)
    groups, out_ref, blank, sems, blank_sems = refs[:count], *refs[count:]
    sub = blank.shape[0]
    block = out_ref.shape[1] // nt
    mine = flags_ref[MINE_AT] != 0

    @pl.when(mine)
    def _():
        copies = []
        for k in range(half):
            at = pl.multiple_of((flags_ref[Q_AT] ^ k) * sub, sub)
            for m in range(nt):
                left = pl.multiple_of((flags_ref[T_AT] ^ m) * block, 128)
                for c, (off, width) in enumerate(spans):
                    copies.append(
                        pltpu.make_async_copy(
                            groups[c * half + k].at[m],
                            out_ref.at[pl.ds(at, sub), pl.ds(left + off, width)],
                            sems.at[len(copies)],
                        )
                    )
        for copy in copies:
            copy.start()
        for copy in copies:
            copy.wait()

    @pl.when(jnp.logical_not(mine))
    def _():
        blank[...] = jnp.zeros_like(blank)
        copies = [
            pltpu.make_async_copy(
                blank, out_ref.at[pl.ds(j * sub, sub), :], blank_sems.at[j]
            )
            for j in range(half)
        ]
        for copy in copies:
            copy.start()
        for copy in copies:
            copy.wait()


def assemble(flags, gathered, spans, rows, model):
    half = len(gathered[0])
    nt, sub = gathered[0][0].shape[:2]
    anywhere = pl.BlockSpec(memory_space=pl.ANY)
    groups = [piece for group in gathered for piece in group]
    return pl.pallas_call(
        functools.partial(assemble_kernel, half, nt, spans),
        out_shape=jax.ShapeDtypeStruct((rows, model), jnp.bfloat16),
        in_specs=[pl.BlockSpec(memory_space=pltpu.SMEM)] + [anywhere] * len(groups),
        out_specs=anywhere,
        scratch_shapes=[
            pltpu.VMEM((sub, model), jnp.bfloat16),
            pltpu.SemaphoreType.DMA((half * nt * len(spans),)),
            pltpu.SemaphoreType.DMA((half,)),
        ],
        cost_estimate=pl.CostEstimate(
            flops=0, bytes_accessed=4 * rows * model, transcendentals=0
        ),
        name="assemble",
    )(flags, *groups)


class TwoClusters:
    def __init__(self, own, perm, cluster, owners, e, t, ne, nt):
        self.own, self.t, self.ne, self.nt = own, t, ne, nt
        rows, model = own.shape
        half = self.half = ne // 2
        self.sub = rows // half
        self.spans = chunks_of(model // nt)
        self.cluster, self.owners, self.e = cluster, owners, e
        q, side = e % half, e // half
        self.place = (((perm // rows) ^ t) * rows + perm % rows).reshape(-1, 1)
        experts = jnp.arange(ne, dtype=jnp.int32)
        near = (e ^ jnp.arange(half, dtype=jnp.int32))[:, None] == experts[None, :]
        member = jnp.sum(jnp.where(near, cluster[None, :], 0), axis=1)
        sides = owners // half
        keep = jnp.where(sides[0:1] == side, 0, 1)
        give = jnp.where(sides[0:1] != side, 0, 1)
        mine = jnp.where(jnp.where(keep == 0, owners[0:1], owners[1:2]) == e, 1, 0)
        self.flags = jnp.concatenate(
            [t.reshape(1), q.reshape(1), keep, give, mine, member]
        ).astype(jnp.int32)
        self.sizes = jnp.sum(
            (cluster[None, :] == jnp.arange(2, dtype=jnp.int32)[:, None]).astype(jnp.float32),
            axis=1,
        )
        self.scale = 1.0 / jnp.where(keep == 0, self.sizes[0:1], self.sizes[1:2])
        self.sources = [
            columns_to_device(own, t, nt, off, width) for off, width in self.spans
        ]

    def send_aligned(self, c):
        pieces = align(self.flags, self.place, self.sources[c], self.half, self.sub)
        sent = [
            xor_permute(piece, "expert", self.ne, k) if k else piece
            for k, piece in enumerate(pieces)
        ]
        return pieces[0], sent

    def back_and_out(self, pieces, *others):
        lines = jnp.stack(rows_to_device(pieces, self.nt))
        if others:
            lines = after(lines, *others)
        return [
            xor_permute(lines, "expert", self.ne, k) if k else lines for k in range(self.half)
        ]

    def finish(self, gathered, arrived):
        rows, model = self.own.shape
        first = assemble(self.flags, gathered, self.spans, rows, model)
        sides = self.owners // self.half

        def second(args):
            first, arrived = args
            near = self.cluster[self.e ^ jnp.arange(self.half, dtype=jnp.int32)]
            again = []
            for parts in arrived:
                total = jnp.zeros(parts[0].shape, jnp.float32)
                for k in range(self.half):
                    total = total + jnp.where(near[k] == 1, parts[k].astype(jnp.float32), 0.0)
                other = xor_permute(total.astype(jnp.bfloat16), "expert", self.ne, self.half)
                scale = (1.0 / self.sizes[1]).reshape(1)
                again.append(self.back_and_out(mean_of(scale, total, other, self.nt)))
            mine = jnp.where(self.owners[1:2] == self.e, 1, 0).astype(jnp.int32)
            flags = jnp.concatenate(
                [self.flags[:MINE_AT], mine, self.flags[MINE_AT + 1 :]]
            )
            return first + assemble(flags, again, self.spans, rows, model)

        return lax.cond(
            sides[0] == sides[1], second, lambda args: args[0], (first, arrived)
        )


def merge_any(own, perm, cluster, owners, e, t, ne, nt):
    rows, model = own.shape
    block = model // nt
    clusters = owners.shape[0]
    sub = rows // ne
    placed = ((perm // rows) ^ t) * rows + perm % rows
    placed = placed.reshape(nt, ne, sub).transpose(1, 0, 2).reshape(-1)
    aligned = pick_rows(
        one_hot(placed, rows * nt), jnp.concatenate(columns_to_device(own, t, nt, 0, block))
    )
    arrived = lax.all_to_all(aligned, "expert", split_axis=0, concat_axis=0, tiled=True)
    arrived = arrived.reshape(ne, nt, sub, block)
    member = cluster[None, :] == jnp.arange(clusters, dtype=jnp.int32)[:, None]
    inverse = 1.0 / jnp.sum(member.astype(jnp.float32), axis=1)
    means = []
    for c in range(clusters):
        total = jnp.sum(
            jnp.where(member[c][:, None, None, None], arrived.astype(jnp.float32), 0.0), axis=0
        )
        means.append((total * inverse[c]).astype(jnp.bfloat16))
    back = jnp.stack(rows_to_device(jnp.stack(means, axis=1), nt))
    back = jnp.take(back, jnp.arange(nt, dtype=jnp.int32) ^ t, axis=0)
    lines = back.transpose(1, 2, 0, 3).reshape(clusters, sub, model)
    outgoing = jnp.zeros((ne, sub, model), jnp.bfloat16).at[owners].set(lines)
    return lax.all_to_all(
        outgoing.reshape(ne * sub, model), "expert", split_axis=0, concat_axis=0, tiled=True
    )


def on_device(
    tokens,
    routes,
    gate_values,
    probe_rows,
    gate_weight,
    up_weight,
    down_weight,
    hidden_perm,
    cluster,
    owners,
):
    ne = lax.axis_size("expert")
    nt = lax.axis_size("tensor")
    e = lax.axis_index("expert").astype(jnp.int32)
    t = lax.axis_index("tensor").astype(jnp.int32)
    tok_rows, top = routes.shape
    capacity = tok_rows * top * 5 // (4 * ne)
    own = down_weight[0]
    model = own.shape[1]
    block = model // nt

    perm = jnp.concatenate(gather_tensor(hidden_perm[0], nt))
    two = None
    if ne == 8 and owners.shape[0] == 2:
        two = TwoClusters(own, perm, cluster, owners, e, t, ne, nt)

    flat = routes.reshape(-1)
    pairs = jnp.arange(flat.shape[0], dtype=jnp.int32)
    earlier = (flat[:, None] == flat[None, :]) & (pairs[None, :] < pairs[:, None])
    target = flat * capacity + jnp.sum(earlier.astype(jnp.int32), axis=1)
    target = target.reshape(tok_rows, top)
    slots = jnp.arange(ne * capacity, dtype=jnp.int32)
    selector = jnp.zeros((ne * capacity, tok_rows), jnp.bool_)
    for k in range(top):
        selector = selector | (slots[:, None] == target[:, k][None, :])
    outgoing = jnp.dot(
        selector.astype(jnp.bfloat16), tokens, preferred_element_type=jnp.float32
    ).astype(jnp.bfloat16)
    arrived = lax.all_to_all(outgoing, "expert", split_axis=0, concat_axis=0, tiled=True)
    routed = arrived.shape[0]
    stacked = gather_tensor(jnp.concatenate([arrived, probe_rows], axis=0), nt)

    if two is not None:
        parts, others, kept, marks = [], [], [], []
        for c in range(len(two.spans)):
            mark, sent = two.send_aligned(c)
            marks.append(mark)
            parts.append(sent)
        stacked = list(lax.optimization_barrier((*stacked, *marks))[:nt])
    hidden = ffn(stacked, gate_weight, up_weight, t)
    routed_hidden, probe_hidden = hidden[:routed], hidden[routed:]
    if two is not None:
        for c in range(len(two.spans)):
            given, own_sum = sums(two.flags, parts[c])
            if c == 0:
                given = after(given, hidden)
            others.append(xor_permute(given, "expert", ne, two.half))
            kept.append(own_sum)

    partials = [
        jnp.dot(
            routed_hidden,
            lax.dynamic_slice(own, (0, (t ^ k) * block), (own.shape[0], block)),
            preferred_element_type=jnp.float32,
        )
        for k in range(nt)
    ]
    returned = scatter_tensor(partials, nt).astype(jnp.bfloat16)
    home = lax.all_to_all(returned, "expert", split_axis=0, concat_axis=0, tiled=True)
    chooser = (target.T.reshape(-1)[:, None] == slots[None, :]).astype(jnp.bfloat16)
    picked = jnp.dot(chooser, home, preferred_element_type=jnp.float32)
    picked = picked.reshape(top, tok_rows, block)
    mixed = jnp.sum(gate_values.T[:, :, None] * picked, axis=0).astype(jnp.bfloat16)

    everyone = lax.all_gather(probe_hidden, "expert", axis=0)
    at_owner = jnp.arange(ne, dtype=jnp.int32) == owners[cluster[e]]
    partner = jnp.sum(
        jnp.where(at_owner[:, None, None], everyone.astype(jnp.float32), 0.0), axis=0
    ).astype(jnp.bfloat16)
    partner_full = lax.all_gather(partner, "tensor", axis=1, tiled=True)
    correlation = (
        lax.dot_general(
            probe_hidden, partner_full, (((0,), (0,)), ((), ())), preferred_element_type=jnp.float32
        )
        / probe_hidden.shape[0]
    )
    if two is not None:
        gathered = []
        for c in range(len(two.spans)):
            means = mean_of(two.scale, kept[c], others[c], nt)
            gathered.append(two.back_and_out(means, *((returned,) if c == 0 else ())))
        gathered[-1][0] = after(gathered[-1][0], mixed, correlation)
        merged = two.finish(gathered, parts)
    else:
        merged = merge_any(own, perm, cluster, owners, e, t, ne, nt)
    return (mixed, correlation[None], merged[None])


def solution(mesh):
    in_specs = (
        P("expert", "tensor"),
        P("expert", None),
        P("expert", None),
        P(None, "tensor"),
        P("expert", None, "tensor"),
        P("expert", None, "tensor"),
        P("expert", "tensor", None),
        P("expert", "tensor"),
        P(),
        P(),
    )
    out_specs = (P("expert", "tensor"), P("expert", "tensor", None), P("expert", "tensor", None))
    return jax.shard_map(
        on_device, mesh=mesh, in_specs=in_specs, out_specs=out_specs, check_vma=False
    )
```

```python
import functools

import jax
import jax.numpy as jnp
from jax import lax
from jax.experimental import pallas as pl
from jax.experimental.pallas import tpu as pltpu
from jax.sharding import PartitionSpec as P


def xor_permute(value, axis, size, k):
    return lax.ppermute(value, axis, [(i, i ^ k) for i in range(size)])


def gather_small(value, size):
    held = {0: value}
    bit = size // 2
    while bit:
        for k in sorted(held):
            held[k ^ bit] = xor_permute(held[k], "tensor", size, bit)
        bit //= 2
    return [held[k] for k in range(size)]


def gather_even(value, size):
    stack, order = value[None], [0]
    bit = size // 2
    while bit > 1:
        stack = jnp.concatenate([stack, xor_permute(stack, "tensor", size, bit)])
        order = order + [k ^ bit for k in order]
        bit //= 2
    return stack, order


def down_kernel(count, where_ref, rows_ref, weight_ref, send_ref, keep_ref):
    step = pl.program_id(0)
    part = jnp.dot(rows_ref[...], weight_ref[...], preferred_element_type=jnp.float32)

    @pl.when(step < count // 2)
    def _():
        send_ref[0] = part.astype(send_ref.dtype)

    @pl.when(step >= count // 2)
    def _():
        keep_ref[0] = part.astype(keep_ref.dtype)


def down(hidden, routed, own, t, count):
    units, model = own.shape
    block = model // count
    half = count // 2

    def column(i, where):
        return (0, where[0] ^ jnp.where(i < half, 2 * i + 1, 2 * (i - half)))

    shape = jax.ShapeDtypeStruct((half, routed, block), jnp.bfloat16)
    return pl.pallas_call(
        functools.partial(down_kernel, count),
        out_shape=[shape, shape],
        grid_spec=pltpu.PrefetchScalarGridSpec(
            num_scalar_prefetch=1,
            grid=(count,),
            in_specs=[
                pl.BlockSpec((routed, units), lambda i, where: (0, 0)),
                pl.BlockSpec((units, block), column),
            ],
            out_specs=[
                pl.BlockSpec(
                    (1, routed, block), lambda i, where: (jnp.minimum(i, half - 1), 0, 0)
                ),
                pl.BlockSpec(
                    (1, routed, block), lambda i, where: (jnp.maximum(i - half, 0), 0, 0)
                ),
            ],
        ),
        compiler_params=pltpu.CompilerParams(vmem_limit_bytes=BIG_VMEM),
        cost_estimate=SMALL_COST,
        name="down",
    )(t.reshape(1).astype(jnp.int32), hidden, own)


def sum_tensor(send, keep, size):
    bit = 1
    while bit < size:
        if send.shape[0] == 1:
            send, keep = send[0], keep[0]
        arrived = xor_permute(send, "tensor", size, bit)
        total = keep.astype(jnp.float32) + arrived.astype(jnp.float32)
        bit *= 2
        if bit < size:
            send, keep = total[1::2].astype(jnp.bfloat16), total[0::2]
    return total.astype(jnp.bfloat16)


SMALL_COST = pl.CostEstimate(flops=1024, bytes_accessed=1024, transcendentals=0)
BIG_VMEM = 48 * 1024 * 1024


def all_after(values, *others):
    return list(lax.optimization_barrier((*values, *others))[: len(values)])


def ffn_kernel(order, where_ref, even_ref, odd_ref, gate_ref, up_ref, out_ref, gate_sum, up_sum):
    step = pl.program_id(0)
    count = 2 * len(order)

    @pl.when(step == 0)
    def _():
        gate_sum[...] = jnp.zeros_like(gate_sum)
        up_sum[...] = jnp.zeros_like(up_sum)

    for place, k in enumerate(order):
        for odd, stack in enumerate((even_ref, odd_ref)):

            @pl.when(step == k + odd)
            def _(place=place, stack=stack):
                rows = stack[place]
                gate_sum[...] += jnp.dot(rows, gate_ref[0], preferred_element_type=jnp.float32)
                up_sum[...] += jnp.dot(rows, up_ref[0], preferred_element_type=jnp.float32)

    @pl.when(step == count - 1)
    def _():
        gate = gate_sum[...]
        out_ref[...] = (gate / (1.0 + jnp.exp(-gate)) * up_sum[...]).astype(out_ref.dtype)


def ffn(stacks, order, gate_weight, up_weight, t):
    n, rows, width = stacks[0].shape
    units = gate_weight.shape[2]
    weight_spec = pl.BlockSpec((1, width, units), lambda k, where: (0, where[0] ^ k, 0))
    return pl.pallas_call(
        functools.partial(ffn_kernel, order),
        out_shape=jax.ShapeDtypeStruct((rows, units), jnp.bfloat16),
        grid_spec=pltpu.PrefetchScalarGridSpec(
            num_scalar_prefetch=1,
            grid=(2 * n,),
            in_specs=[pl.BlockSpec((n, rows, width), lambda k, where: (0, 0, 0))] * 2
            + [weight_spec, weight_spec],
            out_specs=pl.BlockSpec((rows, units), lambda k, where: (0, 0)),
            scratch_shapes=[pltpu.VMEM((rows, units), jnp.float32)] * 2,
        ),
        compiler_params=pltpu.CompilerParams(vmem_limit_bytes=BIG_VMEM),
        cost_estimate=SMALL_COST,
        name="ffn",
    )(t.reshape(1).astype(jnp.int32), *stacks, gate_weight, up_weight)


def chunks_of(width):
    lanes = 128
    if width % lanes or width < 2 * lanes:
        return [(0, width)]
    first = (width // lanes + 1) // 2 * lanes
    return [(0, first), (first, width - first)]


def one_hot(positions, count):
    selector = (positions[:, None] == jnp.arange(count, dtype=jnp.int32)[None, :]).astype(
        jnp.bfloat16
    )
    return lax.optimization_barrier(selector)


def pick_rows(selector, source):
    return jnp.dot(selector, source, preferred_element_type=jnp.float32).astype(jnp.bfloat16)


def after(value, *others):
    if not others:
        return value
    return lax.optimization_barrier((value,) + others)[0]


def columns_to_device(own, t, nt, off, width):
    block = own.shape[1] // nt
    found = []
    for k in range(nt):
        piece = lax.dynamic_slice(own, (0, (t ^ k) * block + off), (own.shape[0], width))
        found.append(xor_permute(piece, "tensor", nt, k) if k else piece)
    return found


def columns_in_two(own, t, off, width, *earlier):
    block = own.shape[1] // 4
    mine, near, far, both = [
        lax.dynamic_slice(own, (0, (t ^ k) * block + off), (own.shape[0], width)) for k in range(4)
    ]
    before_far, before_near = earlier or ((), ())
    first = xor_permute(after(jnp.stack([far, both]), *before_far), "tensor", 4, 2)
    pair = after(jnp.stack([near, first[1]]), *before_near)
    return [mine, first, xor_permute(pair, "tensor", 4, 1)]


def rows_to_device(pieces, nt):
    return [xor_permute(pieces[k], "tensor", nt, k) if k else pieces[k] for k in range(nt)]


T_AT, Q_AT, KEEP_AT, GIVE_AT, MINE_AT, MEMBER_AT = range(6)


def full_spec(shape):
    return pl.BlockSpec(shape, memory_space=pltpu.VMEM)


def align_kernel(nt, half, sub, flags_ref, place_ref, *refs):
    mine, first, second = refs[:3]
    outs = refs[3:]
    rows, width = mine.shape
    lane = lax.broadcasted_iota(jnp.int32, (rows, rows), 1)
    q = flags_ref[Q_AT]
    for k in range(half):
        start = pl.multiple_of((q ^ k) * sub, sub)
        place = jnp.concatenate(
            [place_ref[pl.ds(start + b * half * sub, sub), :] for b in range(nt)], axis=0
        )
        total = jnp.zeros((rows, width), jnp.float32)
        for m in range(nt):
            selector = jnp.where(place - m * rows == lane, 1.0, 0.0).astype(jnp.bfloat16)
            source = (mine[...], second[0], first[0], second[1])[m]
            total = total + jnp.dot(selector, source, preferred_element_type=jnp.float32)
        outs[k][...] = total.astype(jnp.bfloat16)


def align(flags, place, sources, half, sub):
    nt = 4
    rows, width = sources[0].shape
    piece = jax.ShapeDtypeStruct((rows, width), jnp.bfloat16)
    return pl.pallas_call(
        functools.partial(align_kernel, nt, half, sub),
        out_shape=[piece] * half,
        in_specs=[pl.BlockSpec(memory_space=pltpu.SMEM), full_spec(place.shape)]
        + [full_spec(source.shape) for source in sources],
        out_specs=[full_spec((rows, width))] * half,
        compiler_params=pltpu.CompilerParams(vmem_limit_bytes=BIG_VMEM),
        cost_estimate=SMALL_COST,
        name="align",
    )(flags, place, *sources)


def sums_kernel(half, tile, flags_ref, *refs):
    parts, sent_ref, kept_ref = refs[:half], refs[half], refs[half + 1]
    gives = [jnp.where(flags_ref[MEMBER_AT + k] == flags_ref[GIVE_AT], 1.0, 0.0) for k in range(half)]
    keeps = [jnp.where(flags_ref[MEMBER_AT + k] == flags_ref[KEEP_AT], 1.0, 0.0) for k in range(half)]

    @pl.loop(0, sent_ref.shape[0] // tile)
    def _(i):
        at = pl.ds(pl.multiple_of(i * tile, tile), tile)
        sent = kept = None
        for k in range(half):
            part = parts[k][at, :].astype(jnp.float32)
            sent = part * gives[k] if k == 0 else sent + part * gives[k]
            kept = part * keeps[k] if k == 0 else kept + part * keeps[k]
        sent_ref[at, :] = sent.astype(sent_ref.dtype)
        kept_ref[at, :] = kept


def sums(flags, parts):
    rows, width = parts[0].shape
    tile = min(32, rows)
    spec = full_spec((rows, width))
    return pl.pallas_call(
        functools.partial(sums_kernel, len(parts), tile),
        out_shape=[
            jax.ShapeDtypeStruct((rows, width), jnp.bfloat16),
            jax.ShapeDtypeStruct((rows, width), jnp.float32),
        ],
        in_specs=[pl.BlockSpec(memory_space=pltpu.SMEM)] + [spec] * len(parts),
        out_specs=[spec, spec],
        compiler_params=pltpu.CompilerParams(vmem_limit_bytes=BIG_VMEM),
        cost_estimate=SMALL_COST,
        name="sums",
    )(flags, *parts)


def mean_kernel(scale_ref, kept_ref, other_ref, *outs):
    sub = outs[0].shape[0]
    scale = scale_ref[0]
    for m, out in enumerate(outs):
        at = pl.ds(m * sub, sub)
        total = kept_ref[at, :] + other_ref[at, :].astype(jnp.float32)
        out[...] = (total * scale).astype(out.dtype)


def mean_of(scale, kept, other, nt):
    rows, width = kept.shape
    sub = rows // nt
    return pl.pallas_call(
        mean_kernel,
        out_shape=[jax.ShapeDtypeStruct((sub, width), jnp.bfloat16)] * nt,
        in_specs=[pl.BlockSpec(memory_space=pltpu.SMEM)] + [full_spec((rows, width))] * 2,
        out_specs=[full_spec((sub, width))] * nt,
        compiler_params=pltpu.CompilerParams(vmem_limit_bytes=BIG_VMEM),
        cost_estimate=SMALL_COST,
        name="mean",
    )(scale, kept, other)


def assemble_kernel(half, nt, spans, flags_ref, *refs):
    groups, out_ref = refs[:-1], refs[-1]
    sub = groups[0].shape[1]
    block = out_ref.shape[1] // nt
    mine = flags_ref[MINE_AT] != 0

    @pl.when(mine)
    def _():
        for k in range(half):
            at = pl.multiple_of((flags_ref[Q_AT] ^ k) * sub, sub)
            for m in range(nt):
                left = pl.multiple_of((flags_ref[T_AT] ^ m) * block, 128)
                for c, (off, width) in enumerate(spans):
                    out_ref[pl.ds(at, sub), pl.ds(left + off, width)] = groups[c * half + k][m]

    @pl.when(jnp.logical_not(mine))
    def _():
        out_ref[...] = jnp.zeros_like(out_ref)


def assemble(flags, gathered, spans, rows, model):
    half = len(gathered[0])
    nt = gathered[0][0].shape[0]
    groups = [piece for group in gathered for piece in group]
    return pl.pallas_call(
        functools.partial(assemble_kernel, half, nt, spans),
        out_shape=jax.ShapeDtypeStruct((rows, model), jnp.bfloat16),
        in_specs=[pl.BlockSpec(memory_space=pltpu.SMEM)]
        + [full_spec(piece.shape) for piece in groups],
        out_specs=full_spec((rows, model)),
        compiler_params=pltpu.CompilerParams(vmem_limit_bytes=BIG_VMEM),
        cost_estimate=SMALL_COST,
        name="assemble",
    )(flags, *groups)


class TwoClusters:
    def __init__(self, own, perm, cluster, owners, e, t, ne, nt):
        self.own, self.t, self.ne, self.nt = own, t, ne, nt
        rows, model = own.shape
        half = self.half = ne // 2
        self.sub = rows // half
        self.spans = chunks_of(model // nt)
        self.cluster, self.owners, self.e = cluster, owners, e
        q, side = e % half, e // half
        self.place = (((perm // rows) ^ t) * rows + perm % rows).reshape(-1, 1)
        experts = jnp.arange(ne, dtype=jnp.int32)
        near = (e ^ jnp.arange(half, dtype=jnp.int32))[:, None] == experts[None, :]
        member = jnp.sum(jnp.where(near, cluster[None, :], 0), axis=1)
        sides = owners // half
        keep = jnp.where(sides[0:1] == side, 0, 1)
        give = jnp.where(sides[0:1] != side, 0, 1)
        mine = jnp.where(jnp.where(keep == 0, owners[0:1], owners[1:2]) == e, 1, 0)
        self.flags = jnp.concatenate(
            [t.reshape(1), q.reshape(1), keep, give, mine, member]
        ).astype(jnp.int32)
        self.sizes = jnp.sum(
            (cluster[None, :] == jnp.arange(2, dtype=jnp.int32)[:, None]).astype(jnp.float32),
            axis=1,
        )
        self.scale = 1.0 / jnp.where(keep == 0, self.sizes[0:1], self.sizes[1:2])

    def columns(self, c, *earlier):
        return columns_in_two(self.own, self.t, *self.spans[c], *earlier)

    def send_aligned(self, sources, *earlier):
        sources = all_after(sources, *earlier)
        pieces = align(self.flags, self.place, sources, self.half, self.sub)
        sent = [
            xor_permute(piece, "expert", self.ne, k) if k else piece
            for k, piece in enumerate(pieces)
        ]
        return pieces[0], sent

    def back(self, pieces):
        return jnp.stack(rows_to_device(pieces, self.nt))

    def out(self, lines):
        return [
            xor_permute(lines, "expert", self.ne, k) if k else lines for k in range(self.half)
        ]

    def finish(self, gathered, arrived):
        rows, model = self.own.shape
        first = assemble(self.flags, gathered, self.spans, rows, model)
        sides = self.owners // self.half

        def second(args):
            first, arrived = args
            near = self.cluster[self.e ^ jnp.arange(self.half, dtype=jnp.int32)]
            again = []
            for parts in arrived:
                total = jnp.zeros(parts[0].shape, jnp.float32)
                for k in range(self.half):
                    total = total + jnp.where(near[k] == 1, parts[k].astype(jnp.float32), 0.0)
                other = xor_permute(total.astype(jnp.bfloat16), "expert", self.ne, self.half)
                scale = (1.0 / self.sizes[1]).reshape(1)
                again.append(self.out(self.back(mean_of(scale, total, other, self.nt))))
            mine = jnp.where(self.owners[1:2] == self.e, 1, 0).astype(jnp.int32)
            flags = jnp.concatenate(
                [self.flags[:MINE_AT], mine, self.flags[MINE_AT + 1 :]]
            )
            return first + assemble(flags, again, self.spans, rows, model)

        return lax.cond(
            sides[0] == sides[1], second, lambda args: args[0], (first, arrived)
        )


def merge_any(own, perm, cluster, owners, e, t, ne, nt):
    rows, model = own.shape
    block = model // nt
    clusters = owners.shape[0]
    sub = rows // ne
    placed = ((perm // rows) ^ t) * rows + perm % rows
    placed = placed.reshape(nt, ne, sub).transpose(1, 0, 2).reshape(-1)
    aligned = pick_rows(
        one_hot(placed, rows * nt), jnp.concatenate(columns_to_device(own, t, nt, 0, block))
    )
    arrived = lax.all_to_all(aligned, "expert", split_axis=0, concat_axis=0, tiled=True)
    arrived = arrived.reshape(ne, nt, sub, block)
    member = cluster[None, :] == jnp.arange(clusters, dtype=jnp.int32)[:, None]
    inverse = 1.0 / jnp.sum(member.astype(jnp.float32), axis=1)
    means = []
    for c in range(clusters):
        total = jnp.sum(
            jnp.where(member[c][:, None, None, None], arrived.astype(jnp.float32), 0.0), axis=0
        )
        means.append((total * inverse[c]).astype(jnp.bfloat16))
    back = jnp.stack(rows_to_device(jnp.stack(means, axis=1), nt))
    back = jnp.take(back, jnp.arange(nt, dtype=jnp.int32) ^ t, axis=0)
    lines = back.transpose(1, 2, 0, 3).reshape(clusters, sub, model)
    outgoing = jnp.zeros((ne, sub, model), jnp.bfloat16).at[owners].set(lines)
    return lax.all_to_all(
        outgoing.reshape(ne * sub, model), "expert", split_axis=0, concat_axis=0, tiled=True
    )


def on_device(
    tokens,
    routes,
    gate_values,
    probe_rows,
    gate_weight,
    up_weight,
    down_weight,
    hidden_perm,
    cluster,
    owners,
):
    ne = lax.axis_size("expert")
    nt = lax.axis_size("tensor")
    e = lax.axis_index("expert").astype(jnp.int32)
    t = lax.axis_index("tensor").astype(jnp.int32)
    tok_rows, top = routes.shape
    capacity = tok_rows * top * 5 // (4 * ne)
    own = down_weight[0]
    model = own.shape[1]
    block = model // nt

    perm = jnp.concatenate(gather_small(hidden_perm[0], nt))
    two = None
    if ne == 8 and nt == 4 and owners.shape[0] == 2:
        two = TwoClusters(own, perm, cluster, owners, e, t, ne, nt)

    flat = routes.reshape(-1)
    pairs = jnp.arange(flat.shape[0], dtype=jnp.int32)
    earlier = (flat[:, None] == flat[None, :]) & (pairs[None, :] < pairs[:, None])
    target = flat * capacity + jnp.sum(earlier.astype(jnp.int32), axis=1)
    target = target.reshape(tok_rows, top)
    slots = jnp.arange(ne * capacity, dtype=jnp.int32)
    selector = jnp.zeros((ne * capacity, tok_rows), jnp.bool_)
    for k in range(top):
        selector = selector | (slots[:, None] == target[:, k][None, :])
    outgoing = jnp.dot(
        selector.astype(jnp.bfloat16), tokens, preferred_element_type=jnp.float32
    ).astype(jnp.bfloat16)
    arrived = lax.all_to_all(outgoing, "expert", split_axis=0, concat_axis=0, tiled=True)
    routed = arrived.shape[0]
    stacked = jnp.concatenate([arrived, probe_rows], axis=0)
    if two is not None:
        last = len(two.spans) - 1
        sources, marks, parts = [], [], []
        for c in range(last + 1):
            earlier = ((sources[-1][1],), parts[-1][1:]) if c else ()
            sources.append(two.columns(c, *earlier))
            mark, sent = two.send_aligned(sources[c], *marks[-1:])
            marks.append(mark)
            parts.append(sent)
        stacked = after(stacked, sources[-1][1])
        given, own_sum = sums(two.flags, all_after(parts[0], marks[-1]))
        others, kept = [xor_permute(given, "expert", ne, two.half)], [own_sum]
    even, order = gather_even(stacked, nt)
    if two is not None:
        even = after(even, kept[0])
    odd = xor_permute(even, "tensor", nt, 1)
    if two is not None:
        for c in range(1, last + 1):
            given, own_sum = sums(two.flags, all_after(parts[c], kept[-1]))
            others.append(xor_permute(given, "expert", ne, two.half))
            kept.append(own_sum)
        odd = after(odd, kept[-1])
    hidden = ffn((even, odd), order, gate_weight, up_weight, t)
    probe_hidden = hidden[routed:]
    send, keep = down(hidden, routed, own, t, nt)
    if two is not None:
        keep = after(keep, others[0])
    returned = sum_tensor(send, keep, nt)
    home = lax.all_to_all(returned, "expert", split_axis=0, concat_axis=0, tiled=True)
    chooser = (target.T.reshape(-1)[:, None] == slots[None, :]).astype(jnp.bfloat16)
    picked = jnp.dot(chooser, home, preferred_element_type=jnp.float32)
    picked = picked.reshape(top, tok_rows, block)
    mixed = jnp.sum(gate_values.T[:, :, None] * picked, axis=0).astype(jnp.bfloat16)

    everyone = lax.all_gather(probe_hidden, "expert", axis=0)
    at_owner = jnp.arange(ne, dtype=jnp.int32) == owners[cluster[e]]
    partner = jnp.sum(
        jnp.where(at_owner[:, None, None], everyone.astype(jnp.float32), 0.0), axis=0
    ).astype(jnp.bfloat16)
    partner_full = lax.all_gather(partner, "tensor", axis=1, tiled=True)
    correlation = (
        lax.dot_general(
            probe_hidden, partner_full, (((0,), (0,)), ((), ())), preferred_element_type=jnp.float32
        )
        / probe_hidden.shape[0]
    )
    if two is not None:
        gathered = []
        for c in range(len(two.spans)):
            other = after(others[c], lines) if c else others[c]
            means = mean_of(two.scale, kept[c], other, nt)
            lines = two.back(means)
            if c == len(two.spans) - 1:
                lines = after(lines, returned)
            gathered.append(two.out(lines))
        gathered[-1][0] = after(gathered[-1][0], mixed, correlation)
        merged = two.finish(gathered, parts)
    else:
        merged = merge_any(own, perm, cluster, owners, e, t, ne, nt)
    return (mixed, correlation[None], merged[None])


def solution(mesh):
    in_specs = (
        P("expert", "tensor"),
        P("expert", None),
        P("expert", None),
        P(None, "tensor"),
        P("expert", None, "tensor"),
        P("expert", None, "tensor"),
        P("expert", "tensor", None),
        P("expert", "tensor"),
        P(),
        P(),
    )
    out_specs = (P("expert", "tensor"), P("expert", "tensor", None), P("expert", "tensor", None))
    return jax.shard_map(
        on_device, mesh=mesh, in_specs=in_specs, out_specs=out_specs, check_vma=False
    )
```

```python
import functools

import jax
import jax.numpy as jnp
from jax import lax
from jax.experimental import pallas as pl
from jax.experimental.pallas import tpu as pltpu
from jax.sharding import PartitionSpec as P


def xor_permute(value, axis, size, k):
    return lax.ppermute(value, axis, [(i, i ^ k) for i in range(size)])


def gather_small(value, size):
    held = {0: value}
    bit = size // 2
    while bit:
        for k in sorted(held):
            held[k ^ bit] = xor_permute(held[k], "tensor", size, bit)
        bit //= 2
    return [held[k] for k in range(size)]


def gather_even(value, size, *others):
    stack, order = value[None], [0]
    bit = size // 2
    while bit > 1:
        arrived = after(xor_permute(stack, "tensor", size, bit), *others)
        stack = jnp.concatenate([stack, arrived])
        order = order + [k ^ bit for k in order]
        bit //= 2
    return stack, order


def down_kernel(count, where_ref, rows_ref, weight_ref, send_ref, keep_ref):
    step = pl.program_id(0)
    part = jnp.dot(rows_ref[...], weight_ref[...], preferred_element_type=jnp.float32)

    @pl.when(step < count // 2)
    def _():
        send_ref[0] = part.astype(send_ref.dtype)

    @pl.when(step >= count // 2)
    def _():
        keep_ref[0] = part.astype(keep_ref.dtype)


def down(hidden, routed, own, t, count):
    units, model = own.shape
    block = model // count
    half = count // 2

    def column(i, where):
        return (0, where[0] ^ jnp.where(i < half, 2 * i + 1, 2 * (i - half)))

    shape = jax.ShapeDtypeStruct((half, routed, block), jnp.bfloat16)
    return pl.pallas_call(
        functools.partial(down_kernel, count),
        out_shape=[shape, shape],
        grid_spec=pltpu.PrefetchScalarGridSpec(
            num_scalar_prefetch=1,
            grid=(count,),
            in_specs=[
                pl.BlockSpec((routed, units), lambda i, where: (0, 0)),
                pl.BlockSpec((units, block), column),
            ],
            out_specs=[
                pl.BlockSpec(
                    (1, routed, block), lambda i, where: (jnp.minimum(i, half - 1), 0, 0)
                ),
                pl.BlockSpec(
                    (1, routed, block), lambda i, where: (jnp.maximum(i - half, 0), 0, 0)
                ),
            ],
        ),
        compiler_params=pltpu.CompilerParams(vmem_limit_bytes=BIG_VMEM),
        cost_estimate=SMALL_COST,
        name="down",
    )(t.reshape(1).astype(jnp.int32), hidden, own)


def sum_tensor(send, keep, size):
    bit = 1
    while bit < size:
        if send.shape[0] == 1:
            send, keep = send[0], keep[0]
        arrived = xor_permute(send, "tensor", size, bit)
        total = keep.astype(jnp.float32) + arrived.astype(jnp.float32)
        bit *= 2
        if bit < size:
            send, keep = total[1::2].astype(jnp.bfloat16), total[0::2]
    return total.astype(jnp.bfloat16)


SMALL_COST = pl.CostEstimate(flops=1024, bytes_accessed=1024, transcendentals=0)
BIG_VMEM = 48 * 1024 * 1024


def all_after(values, *others):
    return list(lax.optimization_barrier((*values, *others))[: len(values)])


def ffn_kernel(order, where_ref, even_ref, odd_ref, gate_ref, up_ref, out_ref, gate_sum, up_sum):
    step = pl.program_id(0)
    count = 2 * len(order)

    @pl.when(step == 0)
    def _():
        gate_sum[...] = jnp.zeros_like(gate_sum)
        up_sum[...] = jnp.zeros_like(up_sum)

    for place, k in enumerate(order):
        for odd, stack in enumerate((even_ref, odd_ref)):

            @pl.when(step == k + odd)
            def _(place=place, stack=stack):
                rows = stack[place]
                gate_sum[...] += jnp.dot(rows, gate_ref[0], preferred_element_type=jnp.float32)
                up_sum[...] += jnp.dot(rows, up_ref[0], preferred_element_type=jnp.float32)

    @pl.when(step == count - 1)
    def _():
        gate = gate_sum[...]
        out_ref[...] = (gate / (1.0 + jnp.exp(-gate)) * up_sum[...]).astype(out_ref.dtype)


def ffn(stacks, order, gate_weight, up_weight, t):
    n, rows, width = stacks[0].shape
    units = gate_weight.shape[2]
    weight_spec = pl.BlockSpec((1, width, units), lambda k, where: (0, where[0] ^ k, 0))
    return pl.pallas_call(
        functools.partial(ffn_kernel, order),
        out_shape=jax.ShapeDtypeStruct((rows, units), jnp.bfloat16),
        grid_spec=pltpu.PrefetchScalarGridSpec(
            num_scalar_prefetch=1,
            grid=(2 * n,),
            in_specs=[pl.BlockSpec((n, rows, width), lambda k, where: (0, 0, 0))] * 2
            + [weight_spec, weight_spec],
            out_specs=pl.BlockSpec((rows, units), lambda k, where: (0, 0)),
            scratch_shapes=[pltpu.VMEM((rows, units), jnp.float32)] * 2,
        ),
        compiler_params=pltpu.CompilerParams(vmem_limit_bytes=BIG_VMEM),
        cost_estimate=SMALL_COST,
        name="ffn",
    )(t.reshape(1).astype(jnp.int32), *stacks, gate_weight, up_weight)


def chunks_of(width):
    lanes = 128
    if width % lanes or width < 2 * lanes:
        return [(0, width)]
    first = (width // lanes + 1) // 2 * lanes
    return [(0, first), (first, width - first)]


def one_hot(positions, count):
    selector = (positions[:, None] == jnp.arange(count, dtype=jnp.int32)[None, :]).astype(
        jnp.bfloat16
    )
    return lax.optimization_barrier(selector)


def pick_rows(selector, source):
    return jnp.dot(selector, source, preferred_element_type=jnp.float32).astype(jnp.bfloat16)


def after(value, *others):
    if not others:
        return value
    return lax.optimization_barrier((value,) + others)[0]


def columns_to_device(own, t, nt, off, width):
    block = own.shape[1] // nt
    found = []
    for k in range(nt):
        piece = lax.dynamic_slice(own, (0, (t ^ k) * block + off), (own.shape[0], width))
        found.append(xor_permute(piece, "tensor", nt, k) if k else piece)
    return found


def columns_in_two(own, t, off, width, *earlier):
    block = own.shape[1] // 4
    mine, near, far, both = [
        lax.dynamic_slice(own, (0, (t ^ k) * block + off), (own.shape[0], width)) for k in range(4)
    ]
    before_far, before_near = earlier or ((), ())
    first = xor_permute(after(jnp.stack([far, both]), *before_far), "tensor", 4, 2)
    pair = jnp.stack([near, after(first, *before_near)[1]])
    return [mine, first, xor_permute(pair, "tensor", 4, 1)]


def rows_to_device(pieces, nt):
    return [xor_permute(pieces[k], "tensor", nt, k) if k else pieces[k] for k in range(nt)]


T_AT, Q_AT, KEEP_AT, GIVE_AT, MINE_AT, MEMBER_AT = range(6)


def full_spec(shape):
    return pl.BlockSpec(shape, memory_space=pltpu.VMEM)


def align_kernel(nt, half, sub, flags_ref, place_ref, *refs):
    mine, first, second = refs[:3]
    outs = refs[3:]
    rows, width = mine.shape
    lane = lax.broadcasted_iota(jnp.int32, (rows, rows), 1)
    q = flags_ref[Q_AT]
    for k in range(half):
        start = pl.multiple_of((q ^ k) * sub, sub)
        place = jnp.concatenate(
            [place_ref[pl.ds(start + b * half * sub, sub), :] for b in range(nt)], axis=0
        )
        total = jnp.zeros((rows, width), jnp.float32)
        for m in range(nt):
            selector = jnp.where(place - m * rows == lane, 1.0, 0.0).astype(jnp.bfloat16)
            source = (mine[...], second[0], first[0], second[1])[m]
            total = total + jnp.dot(selector, source, preferred_element_type=jnp.float32)
        outs[k][...] = total.astype(jnp.bfloat16)


def align(flags, place, sources, half, sub):
    nt = 4
    rows, width = sources[0].shape
    piece = jax.ShapeDtypeStruct((rows, width), jnp.bfloat16)
    return pl.pallas_call(
        functools.partial(align_kernel, nt, half, sub),
        out_shape=[piece] * half,
        in_specs=[pl.BlockSpec(memory_space=pltpu.SMEM), full_spec(place.shape)]
        + [full_spec(source.shape) for source in sources],
        out_specs=[full_spec((rows, width))] * half,
        compiler_params=pltpu.CompilerParams(vmem_limit_bytes=BIG_VMEM),
        cost_estimate=SMALL_COST,
        name="align",
    )(flags, place, *sources)


def sums_kernel(half, tile, flags_ref, *refs):
    parts, sent_ref, kept_ref = refs[:half], refs[half], refs[half + 1]
    gives = [jnp.where(flags_ref[MEMBER_AT + k] == flags_ref[GIVE_AT], 1.0, 0.0) for k in range(half)]
    keeps = [jnp.where(flags_ref[MEMBER_AT + k] == flags_ref[KEEP_AT], 1.0, 0.0) for k in range(half)]

    @pl.loop(0, sent_ref.shape[0] // tile)
    def _(i):
        at = pl.ds(pl.multiple_of(i * tile, tile), tile)
        sent = kept = None
        for k in range(half):
            part = parts[k][at, :].astype(jnp.float32)
            sent = part * gives[k] if k == 0 else sent + part * gives[k]
            kept = part * keeps[k] if k == 0 else kept + part * keeps[k]
        sent_ref[at, :] = sent.astype(sent_ref.dtype)
        kept_ref[at, :] = kept


def sums(flags, parts):
    rows, width = parts[0].shape
    tile = min(32, rows)
    spec = full_spec((rows, width))
    return pl.pallas_call(
        functools.partial(sums_kernel, len(parts), tile),
        out_shape=[
            jax.ShapeDtypeStruct((rows, width), jnp.bfloat16),
            jax.ShapeDtypeStruct((rows, width), jnp.float32),
        ],
        in_specs=[pl.BlockSpec(memory_space=pltpu.SMEM)] + [spec] * len(parts),
        out_specs=[spec, spec],
        compiler_params=pltpu.CompilerParams(vmem_limit_bytes=BIG_VMEM),
        cost_estimate=SMALL_COST,
        name="sums",
    )(flags, *parts)


def mean_kernel(scale_ref, kept_ref, other_ref, *outs):
    sub = outs[0].shape[0]
    scale = scale_ref[0]
    for m, out in enumerate(outs):
        at = pl.ds(m * sub, sub)
        total = kept_ref[at, :] + other_ref[at, :].astype(jnp.float32)
        out[...] = (total * scale).astype(out.dtype)


def mean_of(scale, kept, other, nt):
    rows, width = kept.shape
    sub = rows // nt
    return pl.pallas_call(
        mean_kernel,
        out_shape=[jax.ShapeDtypeStruct((sub, width), jnp.bfloat16)] * nt,
        in_specs=[pl.BlockSpec(memory_space=pltpu.SMEM)] + [full_spec((rows, width))] * 2,
        out_specs=[full_spec((sub, width))] * nt,
        compiler_params=pltpu.CompilerParams(vmem_limit_bytes=BIG_VMEM),
        cost_estimate=SMALL_COST,
        name="mean",
    )(scale, kept, other)


def assemble_kernel(half, nt, spans, flags_ref, *refs):
    groups, out_ref = refs[:-1], refs[-1]
    sub = groups[0].shape[1]
    block = out_ref.shape[1] // nt
    mine = flags_ref[MINE_AT] != 0

    @pl.when(mine)
    def _():
        for k in range(half):
            at = pl.multiple_of((flags_ref[Q_AT] ^ k) * sub, sub)
            for m in range(nt):
                left = pl.multiple_of((flags_ref[T_AT] ^ m) * block, 128)
                for c, (off, width) in enumerate(spans):
                    out_ref[pl.ds(at, sub), pl.ds(left + off, width)] = groups[c * half + k][m]

    @pl.when(jnp.logical_not(mine))
    def _():
        out_ref[...] = jnp.zeros_like(out_ref)


def assemble(flags, gathered, spans, rows, model):
    half = len(gathered[0])
    nt = gathered[0][0].shape[0]
    groups = [piece for group in gathered for piece in group]
    return pl.pallas_call(
        functools.partial(assemble_kernel, half, nt, spans),
        out_shape=jax.ShapeDtypeStruct((rows, model), jnp.bfloat16),
        in_specs=[pl.BlockSpec(memory_space=pltpu.SMEM)]
        + [full_spec(piece.shape) for piece in groups],
        out_specs=full_spec((rows, model)),
        compiler_params=pltpu.CompilerParams(vmem_limit_bytes=BIG_VMEM),
        cost_estimate=SMALL_COST,
        name="assemble",
    )(flags, *groups)


class TwoClusters:
    def __init__(self, own, perm, cluster, owners, e, t, ne, nt):
        self.own, self.t, self.ne, self.nt = own, t, ne, nt
        rows, model = own.shape
        half = self.half = ne // 2
        self.sub = rows // half
        self.spans = chunks_of(model // nt)
        self.cluster, self.owners, self.e = cluster, owners, e
        q, side = e % half, e // half
        self.place = (((perm // rows) ^ t) * rows + perm % rows).reshape(-1, 1)
        experts = jnp.arange(ne, dtype=jnp.int32)
        near = (e ^ jnp.arange(half, dtype=jnp.int32))[:, None] == experts[None, :]
        member = jnp.sum(jnp.where(near, cluster[None, :], 0), axis=1)
        sides = owners // half
        keep = jnp.where(sides[0:1] == side, 0, 1)
        give = jnp.where(sides[0:1] != side, 0, 1)
        mine = jnp.where(jnp.where(keep == 0, owners[0:1], owners[1:2]) == e, 1, 0)
        self.flags = jnp.concatenate(
            [t.reshape(1), q.reshape(1), keep, give, mine, member]
        ).astype(jnp.int32)
        self.sizes = jnp.sum(
            (cluster[None, :] == jnp.arange(2, dtype=jnp.int32)[:, None]).astype(jnp.float32),
            axis=1,
        )
        self.scale = 1.0 / jnp.where(keep == 0, self.sizes[0:1], self.sizes[1:2])

    def columns(self, c, *earlier):
        return columns_in_two(self.own, self.t, *self.spans[c], *earlier)

    def send_aligned(self, sources, *earlier):
        sources = all_after(sources, *earlier)
        pieces = align(self.flags, self.place, sources, self.half, self.sub)
        sent = [
            xor_permute(piece, "expert", self.ne, k) if k else piece
            for k, piece in enumerate(pieces)
        ]
        return pieces[0], sent

    def back(self, pieces):
        return jnp.stack(rows_to_device(pieces, self.nt))

    def out(self, lines):
        return [
            xor_permute(lines, "expert", self.ne, k) if k else lines for k in range(self.half)
        ]

    def finish(self, gathered, arrived):
        rows, model = self.own.shape
        first = assemble(self.flags, gathered, self.spans, rows, model)
        sides = self.owners // self.half

        def second(args):
            first, arrived = args
            near = self.cluster[self.e ^ jnp.arange(self.half, dtype=jnp.int32)]
            again = []
            for parts in arrived:
                total = jnp.zeros(parts[0].shape, jnp.float32)
                for k in range(self.half):
                    total = total + jnp.where(near[k] == 1, parts[k].astype(jnp.float32), 0.0)
                other = xor_permute(total.astype(jnp.bfloat16), "expert", self.ne, self.half)
                scale = (1.0 / self.sizes[1]).reshape(1)
                again.append(self.out(self.back(mean_of(scale, total, other, self.nt))))
            mine = jnp.where(self.owners[1:2] == self.e, 1, 0).astype(jnp.int32)
            flags = jnp.concatenate(
                [self.flags[:MINE_AT], mine, self.flags[MINE_AT + 1 :]]
            )
            return first + assemble(flags, again, self.spans, rows, model)

        return lax.cond(
            sides[0] == sides[1], second, lambda args: args[0], (first, arrived)
        )


def merge_any(own, perm, cluster, owners, e, t, ne, nt):
    rows, model = own.shape
    block = model // nt
    clusters = owners.shape[0]
    sub = rows // ne
    placed = ((perm // rows) ^ t) * rows + perm % rows
    placed = placed.reshape(nt, ne, sub).transpose(1, 0, 2).reshape(-1)
    aligned = pick_rows(
        one_hot(placed, rows * nt), jnp.concatenate(columns_to_device(own, t, nt, 0, block))
    )
    arrived = lax.all_to_all(aligned, "expert", split_axis=0, concat_axis=0, tiled=True)
    arrived = arrived.reshape(ne, nt, sub, block)
    member = cluster[None, :] == jnp.arange(clusters, dtype=jnp.int32)[:, None]
    inverse = 1.0 / jnp.sum(member.astype(jnp.float32), axis=1)
    means = []
    for c in range(clusters):
        total = jnp.sum(
            jnp.where(member[c][:, None, None, None], arrived.astype(jnp.float32), 0.0), axis=0
        )
        means.append((total * inverse[c]).astype(jnp.bfloat16))
    back = jnp.stack(rows_to_device(jnp.stack(means, axis=1), nt))
    back = jnp.take(back, jnp.arange(nt, dtype=jnp.int32) ^ t, axis=0)
    lines = back.transpose(1, 2, 0, 3).reshape(clusters, sub, model)
    outgoing = jnp.zeros((ne, sub, model), jnp.bfloat16).at[owners].set(lines)
    return lax.all_to_all(
        outgoing.reshape(ne * sub, model), "expert", split_axis=0, concat_axis=0, tiled=True
    )


def on_device(
    tokens,
    routes,
    gate_values,
    probe_rows,
    gate_weight,
    up_weight,
    down_weight,
    hidden_perm,
    cluster,
    owners,
):
    ne = lax.axis_size("expert")
    nt = lax.axis_size("tensor")
    e = lax.axis_index("expert").astype(jnp.int32)
    t = lax.axis_index("tensor").astype(jnp.int32)
    tok_rows, top = routes.shape
    capacity = tok_rows * top * 5 // (4 * ne)
    own = down_weight[0]
    model = own.shape[1]
    block = model // nt

    perm = jnp.concatenate(gather_small(hidden_perm[0], nt))
    two = None
    if ne == 8 and nt == 4 and owners.shape[0] == 2:
        two = TwoClusters(own, perm, cluster, owners, e, t, ne, nt)

    flat = routes.reshape(-1)
    pairs = jnp.arange(flat.shape[0], dtype=jnp.int32)
    earlier = (flat[:, None] == flat[None, :]) & (pairs[None, :] < pairs[:, None])
    target = flat * capacity + jnp.sum(earlier.astype(jnp.int32), axis=1)
    target = target.reshape(tok_rows, top)
    slots = jnp.arange(ne * capacity, dtype=jnp.int32)
    selector = jnp.zeros((ne * capacity, tok_rows), jnp.bool_)
    for k in range(top):
        selector = selector | (slots[:, None] == target[:, k][None, :])
    outgoing = jnp.dot(
        selector.astype(jnp.bfloat16), tokens, preferred_element_type=jnp.float32
    ).astype(jnp.bfloat16)
    arrived = lax.all_to_all(outgoing, "expert", split_axis=0, concat_axis=0, tiled=True)
    routed = arrived.shape[0]
    stacked = jnp.concatenate([arrived, probe_rows], axis=0)
    if two is not None:
        last = len(two.spans) - 1
        source = two.columns(0)
        mark, sent = two.send_aligned(source)
        parts = [sent]
        stacked = after(stacked, source[1])
    even, order = gather_even(stacked, nt, *([] if two is None else [mark]))
    odd = xor_permute(even, "tensor", nt, 1)
    hidden = ffn((even, odd), order, gate_weight, up_weight, t)
    probe_hidden = hidden[routed:]
    send, keep = down(hidden, routed, own, t, nt)
    if two is not None:
        others, kept = [], []
        for c in range(last + 1):
            if c < last:
                source = two.columns(c + 1, (even,), (*parts[c][1:], send))
                mark, sent = two.send_aligned(source, mark)
                parts.append(sent)
            ready = all_after(parts[c], *(kept[-1:] if c else (send,)))
            given, own_sum = sums(two.flags, ready)
            others.append(xor_permute(given, "expert", ne, two.half))
            kept.append(own_sum)
        lines = two.back(mean_of(two.scale, kept[0], after(others[0], kept[-1]), nt))
        keep = after(keep, kept[-1])
    returned = sum_tensor(send, keep, nt)
    home = lax.all_to_all(returned, "expert", split_axis=0, concat_axis=0, tiled=True)
    chooser = (target.T.reshape(-1)[:, None] == slots[None, :]).astype(jnp.bfloat16)
    picked = jnp.dot(chooser, home, preferred_element_type=jnp.float32)
    picked = picked.reshape(top, tok_rows, block)
    mixed = jnp.sum(gate_values.T[:, :, None] * picked, axis=0).astype(jnp.bfloat16)

    everyone = lax.all_gather(probe_hidden, "expert", axis=0)
    at_owner = jnp.arange(ne, dtype=jnp.int32) == owners[cluster[e]]
    partner = jnp.sum(
        jnp.where(at_owner[:, None, None], everyone.astype(jnp.float32), 0.0), axis=0
    ).astype(jnp.bfloat16)
    partner_full = lax.all_gather(partner, "tensor", axis=1, tiled=True)
    correlation = (
        lax.dot_general(
            probe_hidden, partner_full, (((0,), (0,)), ((), ())), preferred_element_type=jnp.float32
        )
        / probe_hidden.shape[0]
    )
    if two is not None:
        gathered = [two.out(lines)]
        for c in range(1, len(two.spans)):
            means = mean_of(two.scale, kept[c], after(others[c], lines), nt)
            lines = after(two.back(means), returned)
            gathered.append(two.out(lines))
        gathered[-1][0] = after(gathered[-1][0], mixed, correlation)
        merged = two.finish(gathered, parts)
    else:
        merged = merge_any(own, perm, cluster, owners, e, t, ne, nt)
    return (mixed, correlation[None], merged[None])


def solution(mesh):
    in_specs = (
        P("expert", "tensor"),
        P("expert", None),
        P("expert", None),
        P(None, "tensor"),
        P("expert", None, "tensor"),
        P("expert", None, "tensor"),
        P("expert", "tensor", None),
        P("expert", "tensor"),
        P(),
        P(),
    )
    out_specs = (P("expert", "tensor"), P("expert", "tensor", None), P("expert", "tensor", None))
    return jax.shard_map(
        on_device, mesh=mesh, in_specs=in_specs, out_specs=out_specs, check_vma=False
    )
```

```python
import functools

import jax
import jax.numpy as jnp
from jax import lax
from jax.experimental import pallas as pl
from jax.experimental.pallas import tpu as pltpu
from jax.sharding import PartitionSpec as P


def xor_permute(value, axis, size, k):
    return lax.ppermute(value, axis, [(i, i ^ k) for i in range(size)])


def gather_small(value, size):
    held = {0: value}
    bit = size // 2
    while bit:
        for k in sorted(held):
            held[k ^ bit] = xor_permute(held[k], "tensor", size, bit)
        bit //= 2
    return [held[k] for k in range(size)]


def gather_even(value, size, *others):
    stack, order = value[None], [0]
    bit = size // 2
    while bit > 1:
        arrived = after(xor_permute(stack, "tensor", size, bit), *others)
        stack = jnp.concatenate([stack, arrived])
        order = order + [k ^ bit for k in order]
        bit //= 2
    return stack, order


def down_kernel(count, where_ref, rows_ref, weight_ref, send_ref, keep_ref):
    step = pl.program_id(0)
    part = jnp.dot(rows_ref[...], weight_ref[...], preferred_element_type=jnp.float32)

    @pl.when(step < count // 2)
    def _():
        send_ref[0] = part.astype(send_ref.dtype)

    @pl.when(step >= count // 2)
    def _():
        keep_ref[0] = part.astype(keep_ref.dtype)


def down(hidden, routed, own, t, count):
    units, model = own.shape
    block = model // count
    half = count // 2

    def column(i, where):
        return (0, where[0] ^ jnp.where(i < half, 2 * i + 1, 2 * (i - half)))

    shape = jax.ShapeDtypeStruct((half, routed, block), jnp.bfloat16)
    return pl.pallas_call(
        functools.partial(down_kernel, count),
        out_shape=[shape, shape],
        grid_spec=pltpu.PrefetchScalarGridSpec(
            num_scalar_prefetch=1,
            grid=(count,),
            in_specs=[
                pl.BlockSpec((routed, units), lambda i, where: (0, 0)),
                pl.BlockSpec((units, block), column),
            ],
            out_specs=[
                pl.BlockSpec(
                    (1, routed, block), lambda i, where: (jnp.minimum(i, half - 1), 0, 0)
                ),
                pl.BlockSpec(
                    (1, routed, block), lambda i, where: (jnp.maximum(i - half, 0), 0, 0)
                ),
            ],
        ),
        compiler_params=pltpu.CompilerParams(vmem_limit_bytes=BIG_VMEM),
        cost_estimate=SMALL_COST,
        name="down",
    )(t.reshape(1).astype(jnp.int32), hidden, own)


def sum_tensor(send, keep, size):
    bit = 1
    while bit < size:
        if send.shape[0] == 1:
            send, keep = send[0], keep[0]
        arrived = xor_permute(send, "tensor", size, bit)
        total = keep.astype(jnp.float32) + arrived.astype(jnp.float32)
        bit *= 2
        if bit < size:
            send, keep = total[1::2].astype(jnp.bfloat16), total[0::2]
    return total.astype(jnp.bfloat16)


SMALL_COST = pl.CostEstimate(flops=1024, bytes_accessed=1024, transcendentals=0)
BIG_VMEM = 48 * 1024 * 1024


def all_after(values, *others):
    return list(lax.optimization_barrier((*values, *others))[: len(values)])


def ffn_kernel(order, where_ref, even_ref, odd_ref, gate_ref, up_ref, out_ref, gate_sum, up_sum):
    step = pl.program_id(0)
    count = 2 * len(order)

    @pl.when(step == 0)
    def _():
        gate_sum[...] = jnp.zeros_like(gate_sum)
        up_sum[...] = jnp.zeros_like(up_sum)

    for place, k in enumerate(order):
        for odd, stack in enumerate((even_ref, odd_ref)):

            @pl.when(step == k + odd)
            def _(place=place, stack=stack):
                rows = stack[place]
                gate_sum[...] += jnp.dot(rows, gate_ref[0], preferred_element_type=jnp.float32)
                up_sum[...] += jnp.dot(rows, up_ref[0], preferred_element_type=jnp.float32)

    @pl.when(step == count - 1)
    def _():
        gate = gate_sum[...]
        out_ref[...] = (gate / (1.0 + jnp.exp(-gate)) * up_sum[...]).astype(out_ref.dtype)


def ffn(stacks, order, gate_weight, up_weight, t):
    n, rows, width = stacks[0].shape
    units = gate_weight.shape[2]
    weight_spec = pl.BlockSpec((1, width, units), lambda k, where: (0, where[0] ^ k, 0))
    return pl.pallas_call(
        functools.partial(ffn_kernel, order),
        out_shape=jax.ShapeDtypeStruct((rows, units), jnp.bfloat16),
        grid_spec=pltpu.PrefetchScalarGridSpec(
            num_scalar_prefetch=1,
            grid=(2 * n,),
            in_specs=[pl.BlockSpec((n, rows, width), lambda k, where: (0, 0, 0))] * 2
            + [weight_spec, weight_spec],
            out_specs=pl.BlockSpec((rows, units), lambda k, where: (0, 0)),
            scratch_shapes=[pltpu.VMEM((rows, units), jnp.float32)] * 2,
        ),
        compiler_params=pltpu.CompilerParams(vmem_limit_bytes=BIG_VMEM),
        cost_estimate=SMALL_COST,
        name="ffn",
    )(t.reshape(1).astype(jnp.int32), *stacks, gate_weight, up_weight)


def chunks_of(width):
    lanes = 128
    if width % lanes or width < 2 * lanes:
        return [(0, width)]
    first = (width // lanes + 1) // 2 * lanes
    return [(0, first), (first, width - first)]


def one_hot(positions, count):
    selector = (positions[:, None] == jnp.arange(count, dtype=jnp.int32)[None, :]).astype(
        jnp.bfloat16
    )
    return lax.optimization_barrier(selector)


def pick_rows(selector, source):
    return jnp.dot(selector, source, preferred_element_type=jnp.float32).astype(jnp.bfloat16)


def after(value, *others):
    if not others:
        return value
    return lax.optimization_barrier((value,) + others)[0]


def columns_to_device(own, t, nt, off, width):
    block = own.shape[1] // nt
    found = []
    for k in range(nt):
        piece = lax.dynamic_slice(own, (0, (t ^ k) * block + off), (own.shape[0], width))
        found.append(xor_permute(piece, "tensor", nt, k) if k else piece)
    return found


def columns_in_two(own, t, off, width, *earlier):
    block = own.shape[1] // 4
    mine, near, far, both = [
        lax.dynamic_slice(own, (0, (t ^ k) * block + off), (own.shape[0], width)) for k in range(4)
    ]
    before_far, before_near = earlier or ((), ())
    first = xor_permute(after(jnp.stack([far, both]), *before_far), "tensor", 4, 2)
    pair = jnp.stack([near, after(first, *before_near)[1]])
    return [mine, first, xor_permute(pair, "tensor", 4, 1)]


def rows_to_device(pieces, nt):
    return [xor_permute(pieces[k], "tensor", nt, k) if k else pieces[k] for k in range(nt)]


T_AT, Q_AT, KEEP_AT, GIVE_AT, MINE_AT, MEMBER_AT = range(6)


def full_spec(shape):
    return pl.BlockSpec(shape, memory_space=pltpu.VMEM)


def align_kernel(nt, half, sub, flags_ref, place_ref, *refs):
    mine, first, second = refs[:3]
    outs = refs[3:]
    rows, width = mine.shape
    lane = lax.broadcasted_iota(jnp.int32, (rows, rows), 1)
    q = flags_ref[Q_AT]
    for k in range(half):
        start = pl.multiple_of((q ^ k) * sub, sub)
        place = jnp.concatenate(
            [place_ref[pl.ds(start + b * half * sub, sub), :] for b in range(nt)], axis=0
        )
        total = jnp.zeros((rows, width), jnp.float32)
        for m in range(nt):
            selector = jnp.where(place - m * rows == lane, 1.0, 0.0).astype(jnp.bfloat16)
            source = (mine[...], second[0], first[0], second[1])[m]
            total = total + jnp.dot(selector, source, preferred_element_type=jnp.float32)
        outs[k][...] = total.astype(jnp.bfloat16)


def align(flags, place, sources, half, sub):
    nt = 4
    rows, width = sources[0].shape
    piece = jax.ShapeDtypeStruct((rows, width), jnp.bfloat16)
    return pl.pallas_call(
        functools.partial(align_kernel, nt, half, sub),
        out_shape=[piece] * half,
        in_specs=[pl.BlockSpec(memory_space=pltpu.SMEM), full_spec(place.shape)]
        + [full_spec(source.shape) for source in sources],
        out_specs=[full_spec((rows, width))] * half,
        compiler_params=pltpu.CompilerParams(vmem_limit_bytes=BIG_VMEM),
        cost_estimate=SMALL_COST,
        name="align",
    )(flags, place, *sources)


def sums_kernel(half, tile, flags_ref, *refs):
    parts, sent_ref, kept_ref = refs[:half], refs[half], refs[half + 1]
    gives = [jnp.where(flags_ref[MEMBER_AT + k] == flags_ref[GIVE_AT], 1.0, 0.0) for k in range(half)]
    keeps = [jnp.where(flags_ref[MEMBER_AT + k] == flags_ref[KEEP_AT], 1.0, 0.0) for k in range(half)]

    @pl.loop(0, sent_ref.shape[0] // tile)
    def _(i):
        at = pl.ds(pl.multiple_of(i * tile, tile), tile)
        sent = kept = None
        for k in range(half):
            part = parts[k][at, :].astype(jnp.float32)
            sent = part * gives[k] if k == 0 else sent + part * gives[k]
            kept = part * keeps[k] if k == 0 else kept + part * keeps[k]
        sent_ref[at, :] = sent.astype(sent_ref.dtype)
        kept_ref[at, :] = kept


def sums(flags, parts):
    rows, width = parts[0].shape
    tile = min(32, rows)
    spec = full_spec((rows, width))
    return pl.pallas_call(
        functools.partial(sums_kernel, len(parts), tile),
        out_shape=[
            jax.ShapeDtypeStruct((rows, width), jnp.bfloat16),
            jax.ShapeDtypeStruct((rows, width), jnp.float32),
        ],
        in_specs=[pl.BlockSpec(memory_space=pltpu.SMEM)] + [spec] * len(parts),
        out_specs=[spec, spec],
        compiler_params=pltpu.CompilerParams(vmem_limit_bytes=BIG_VMEM),
        cost_estimate=SMALL_COST,
        name="sums",
    )(flags, *parts)


def mean_kernel(scale_ref, kept_ref, other_ref, mine_ref, near_ref, far_ref):
    sub = mine_ref.shape[0]
    scale = scale_ref[0]
    for m in range(4):
        at = pl.ds(m * sub, sub)
        total = kept_ref[at, :] + other_ref[at, :].astype(jnp.float32)
        value = (total * scale).astype(mine_ref.dtype)
        if m < 2:
            (mine_ref, near_ref)[m][...] = value
        else:
            far_ref[m - 2] = value


def mean_of(scale, kept, other):
    rows, width = kept.shape
    one, two = (rows // 4, width), (2, rows // 4, width)
    return pl.pallas_call(
        mean_kernel,
        out_shape=[jax.ShapeDtypeStruct(shape, jnp.bfloat16) for shape in (one, one, two)],
        in_specs=[pl.BlockSpec(memory_space=pltpu.SMEM)] + [full_spec((rows, width))] * 2,
        out_specs=[full_spec(one), full_spec(one), full_spec(two)],
        compiler_params=pltpu.CompilerParams(vmem_limit_bytes=BIG_VMEM),
        cost_estimate=SMALL_COST,
        name="mean",
    )(scale, kept, other)


def assemble_kernel(half, nt, spans, flags_ref, *refs):
    groups, out_ref = refs[:-1], refs[-1]
    sub = groups[0].shape[1]
    block = out_ref.shape[1] // nt
    mine = flags_ref[MINE_AT] != 0

    @pl.when(mine)
    def _():
        for k in range(half):
            at = pl.multiple_of((flags_ref[Q_AT] ^ k) * sub, sub)
            for m in range(nt):
                left = pl.multiple_of((flags_ref[T_AT] ^ m) * block, 128)
                for c, (off, width) in enumerate(spans):
                    out_ref[pl.ds(at, sub), pl.ds(left + off, width)] = groups[c * half + k][m]

    @pl.when(jnp.logical_not(mine))
    def _():
        out_ref[...] = jnp.zeros_like(out_ref)


def assemble(flags, gathered, spans, rows, model):
    half = len(gathered[0])
    nt = gathered[0][0].shape[0]
    groups = [piece for group in gathered for piece in group]
    return pl.pallas_call(
        functools.partial(assemble_kernel, half, nt, spans),
        out_shape=jax.ShapeDtypeStruct((rows, model), jnp.bfloat16),
        in_specs=[pl.BlockSpec(memory_space=pltpu.SMEM)]
        + [full_spec(piece.shape) for piece in groups],
        out_specs=full_spec((rows, model)),
        compiler_params=pltpu.CompilerParams(vmem_limit_bytes=BIG_VMEM),
        cost_estimate=SMALL_COST,
        name="assemble",
    )(flags, *groups)


class TwoClusters:
    def __init__(self, own, perm, cluster, owners, e, t, ne, nt):
        self.own, self.t, self.ne, self.nt = own, t, ne, nt
        rows, model = own.shape
        half = self.half = ne // 2
        self.sub = rows // half
        self.spans = chunks_of(model // nt)
        self.cluster, self.owners, self.e = cluster, owners, e
        q, side = e % half, e // half
        self.place = (((perm // rows) ^ t) * rows + perm % rows).reshape(-1, 1)
        experts = jnp.arange(ne, dtype=jnp.int32)
        near = (e ^ jnp.arange(half, dtype=jnp.int32))[:, None] == experts[None, :]
        member = jnp.sum(jnp.where(near, cluster[None, :], 0), axis=1)
        sides = owners // half
        keep = jnp.where(sides[0:1] == side, 0, 1)
        give = jnp.where(sides[0:1] != side, 0, 1)
        mine = jnp.where(jnp.where(keep == 0, owners[0:1], owners[1:2]) == e, 1, 0)
        self.flags = jnp.concatenate(
            [t.reshape(1), q.reshape(1), keep, give, mine, member]
        ).astype(jnp.int32)
        self.sizes = jnp.sum(
            (cluster[None, :] == jnp.arange(2, dtype=jnp.int32)[:, None]).astype(jnp.float32),
            axis=1,
        )
        self.scale = 1.0 / jnp.where(keep == 0, self.sizes[0:1], self.sizes[1:2])

    def columns(self, c, *earlier):
        return columns_in_two(self.own, self.t, *self.spans[c], *earlier)

    def send_aligned(self, sources, *earlier):
        sources = all_after(sources, *earlier)
        pieces = align(self.flags, self.place, sources, self.half, self.sub)
        sent = [
            xor_permute(piece, "expert", self.ne, k) if k else piece
            for k, piece in enumerate(pieces)
        ]
        return pieces[0], sent

    def back(self, pieces):
        mine, near, far = pieces
        first = xor_permute(far, "tensor", 4, 2)
        second = xor_permute(jnp.stack([near, first[1]]), "tensor", 4, 1)
        return jnp.stack([mine, second[0], first[0], second[1]])

    def out(self, lines):
        return [
            xor_permute(lines, "expert", self.ne, k) if k else lines for k in range(self.half)
        ]

    def finish(self, gathered, arrived):
        rows, model = self.own.shape
        first = assemble(self.flags, gathered, self.spans, rows, model)
        sides = self.owners // self.half

        def second(args):
            first, arrived = args
            near = self.cluster[self.e ^ jnp.arange(self.half, dtype=jnp.int32)]
            again = []
            for parts in arrived:
                total = jnp.zeros(parts[0].shape, jnp.float32)
                for k in range(self.half):
                    total = total + jnp.where(near[k] == 1, parts[k].astype(jnp.float32), 0.0)
                other = xor_permute(total.astype(jnp.bfloat16), "expert", self.ne, self.half)
                scale = (1.0 / self.sizes[1]).reshape(1)
                again.append(self.out(self.back(mean_of(scale, total, other))))
            mine = jnp.where(self.owners[1:2] == self.e, 1, 0).astype(jnp.int32)
            flags = jnp.concatenate(
                [self.flags[:MINE_AT], mine, self.flags[MINE_AT + 1 :]]
            )
            return first + assemble(flags, again, self.spans, rows, model)

        return lax.cond(
            sides[0] == sides[1], second, lambda args: args[0], (first, arrived)
        )


def merge_any(own, perm, cluster, owners, e, t, ne, nt):
    rows, model = own.shape
    block = model // nt
    clusters = owners.shape[0]
    sub = rows // ne
    placed = ((perm // rows) ^ t) * rows + perm % rows
    placed = placed.reshape(nt, ne, sub).transpose(1, 0, 2).reshape(-1)
    aligned = pick_rows(
        one_hot(placed, rows * nt), jnp.concatenate(columns_to_device(own, t, nt, 0, block))
    )
    arrived = lax.all_to_all(aligned, "expert", split_axis=0, concat_axis=0, tiled=True)
    arrived = arrived.reshape(ne, nt, sub, block)
    member = cluster[None, :] == jnp.arange(clusters, dtype=jnp.int32)[:, None]
    inverse = 1.0 / jnp.sum(member.astype(jnp.float32), axis=1)
    means = []
    for c in range(clusters):
        total = jnp.sum(
            jnp.where(member[c][:, None, None, None], arrived.astype(jnp.float32), 0.0), axis=0
        )
        means.append((total * inverse[c]).astype(jnp.bfloat16))
    back = jnp.stack(rows_to_device(jnp.stack(means, axis=1), nt))
    back = jnp.take(back, jnp.arange(nt, dtype=jnp.int32) ^ t, axis=0)
    lines = back.transpose(1, 2, 0, 3).reshape(clusters, sub, model)
    outgoing = jnp.zeros((ne, sub, model), jnp.bfloat16).at[owners].set(lines)
    return lax.all_to_all(
        outgoing.reshape(ne * sub, model), "expert", split_axis=0, concat_axis=0, tiled=True
    )


def on_device(
    tokens,
    routes,
    gate_values,
    probe_rows,
    gate_weight,
    up_weight,
    down_weight,
    hidden_perm,
    cluster,
    owners,
):
    ne = lax.axis_size("expert")
    nt = lax.axis_size("tensor")
    e = lax.axis_index("expert").astype(jnp.int32)
    t = lax.axis_index("tensor").astype(jnp.int32)
    tok_rows, top = routes.shape
    capacity = tok_rows * top * 5 // (4 * ne)
    own = down_weight[0]
    model = own.shape[1]
    block = model // nt

    perm = jnp.concatenate(gather_small(hidden_perm[0], nt))
    two = None
    if ne == 8 and nt == 4 and owners.shape[0] == 2:
        two = TwoClusters(own, perm, cluster, owners, e, t, ne, nt)

    flat = routes.reshape(-1)
    pairs = jnp.arange(flat.shape[0], dtype=jnp.int32)
    earlier = (flat[:, None] == flat[None, :]) & (pairs[None, :] < pairs[:, None])
    target = flat * capacity + jnp.sum(earlier.astype(jnp.int32), axis=1)
    target = target.reshape(tok_rows, top)
    slots = jnp.arange(ne * capacity, dtype=jnp.int32)
    selector = jnp.zeros((ne * capacity, tok_rows), jnp.bool_)
    for k in range(top):
        selector = selector | (slots[:, None] == target[:, k][None, :])
    outgoing = jnp.dot(
        selector.astype(jnp.bfloat16), tokens, preferred_element_type=jnp.float32
    ).astype(jnp.bfloat16)
    arrived = lax.all_to_all(outgoing, "expert", split_axis=0, concat_axis=0, tiled=True)
    routed = arrived.shape[0]
    stacked = jnp.concatenate([arrived, probe_rows], axis=0)
    if two is not None:
        last = len(two.spans) - 1
        source = two.columns(0)
        mark, sent = two.send_aligned(source)
        parts = [sent]
        stacked = after(stacked, source[1])
    even, order = gather_even(stacked, nt, *([] if two is None else [mark]))
    odd = xor_permute(even, "tensor", nt, 1)
    hidden = ffn((even, odd), order, gate_weight, up_weight, t)
    probe_hidden = hidden[routed:]
    send, keep = down(hidden, routed, own, t, nt)
    if two is not None:
        others, kept = [], []
        for c in range(last + 1):
            if c < last:
                source = two.columns(c + 1, (even,), (*parts[c][1:], send))
                mark, sent = two.send_aligned(source, mark)
                parts.append(sent)
            ready = all_after(parts[c], *((others[-1],) if c else (send,)))
            given, own_sum = sums(two.flags, ready)
            others.append(xor_permute(given, "expert", ne, two.half))
            kept.append(own_sum)
            if not c:
                returned = sum_tensor(send, after(keep, others[0]), nt)
        lines = two.back(mean_of(two.scale, kept[0], after(others[0], kept[-1])))
    else:
        returned = sum_tensor(send, keep, nt)
    home = lax.all_to_all(returned, "expert", split_axis=0, concat_axis=0, tiled=True)
    chooser = (target.T.reshape(-1)[:, None] == slots[None, :]).astype(jnp.bfloat16)
    picked = jnp.dot(chooser, home, preferred_element_type=jnp.float32)
    picked = picked.reshape(top, tok_rows, block)
    mixed = jnp.sum(gate_values.T[:, :, None] * picked, axis=0).astype(jnp.bfloat16)

    everyone = lax.all_gather(probe_hidden, "expert", axis=0)
    at_owner = jnp.arange(ne, dtype=jnp.int32) == owners[cluster[e]]
    partner = jnp.sum(
        jnp.where(at_owner[:, None, None], everyone.astype(jnp.float32), 0.0), axis=0
    ).astype(jnp.bfloat16)
    partner_full = lax.all_gather(partner, "tensor", axis=1, tiled=True)
    correlation = (
        lax.dot_general(
            probe_hidden, partner_full, (((0,), (0,)), ((), ())), preferred_element_type=jnp.float32
        )
        / probe_hidden.shape[0]
    )
    if two is not None:
        gathered = [two.out(lines)]
        for c in range(1, len(two.spans)):
            means = mean_of(two.scale, kept[c], after(others[c], returned, *gathered[-1][1:]))
            lines = after(two.back(means), returned)
            gathered.append(two.out(lines))
        gathered[-1][0] = after(gathered[-1][0], mixed, correlation)
        merged = two.finish(gathered, parts)
    else:
        merged = merge_any(own, perm, cluster, owners, e, t, ne, nt)
    return (mixed, correlation[None], merged[None])


def solution(mesh):
    in_specs = (
        P("expert", "tensor"),
        P("expert", None),
        P("expert", None),
        P(None, "tensor"),
        P("expert", None, "tensor"),
        P("expert", None, "tensor"),
        P("expert", "tensor", None),
        P("expert", "tensor"),
        P(),
        P(),
    )
    out_specs = (P("expert", "tensor"), P("expert", "tensor", None), P("expert", "tensor", None))
    return jax.shard_map(
        on_device, mesh=mesh, in_specs=in_specs, out_specs=out_specs, check_vma=False
    )
```

```python
import functools

import jax
import jax.numpy as jnp
from jax import lax
from jax.experimental import pallas as pl
from jax.experimental.pallas import tpu as pltpu
from jax.sharding import PartitionSpec as P


def xor_permute(value, axis, size, k):
    return lax.ppermute(value, axis, [(i, i ^ k) for i in range(size)])


def gather_small(value, size):
    held = {0: value}
    bit = size // 2
    while bit:
        for k in sorted(held):
            held[k ^ bit] = xor_permute(held[k], "tensor", size, bit)
        bit //= 2
    return [held[k] for k in range(size)]


def gather_even(value, size, *others):
    stack, order = value[None], [0]
    bit = size // 2
    while bit > 1:
        arrived = after(xor_permute(stack, "tensor", size, bit), *others)
        stack = jnp.concatenate([stack, arrived])
        order = order + [k ^ bit for k in order]
        bit //= 2
    return stack, order


def down_kernel(count, where_ref, rows_ref, weight_ref, send_ref, keep_ref):
    step = pl.program_id(0)
    part = jnp.dot(rows_ref[...], weight_ref[...], preferred_element_type=jnp.float32)

    @pl.when(step < count // 2)
    def _():
        send_ref[0] = part.astype(send_ref.dtype)

    @pl.when(step >= count // 2)
    def _():
        keep_ref[0] = part.astype(keep_ref.dtype)


def down(hidden, routed, own, t, count):
    units, model = own.shape
    block = model // count
    half = count // 2

    def column(i, where):
        return (0, where[0] ^ jnp.where(i < half, 2 * i + 1, 2 * (i - half)))

    shape = jax.ShapeDtypeStruct((half, routed, block), jnp.bfloat16)
    return pl.pallas_call(
        functools.partial(down_kernel, count),
        out_shape=[shape, shape],
        grid_spec=pltpu.PrefetchScalarGridSpec(
            num_scalar_prefetch=1,
            grid=(count,),
            in_specs=[
                pl.BlockSpec((routed, units), lambda i, where: (0, 0)),
                pl.BlockSpec((units, block), column),
            ],
            out_specs=[
                pl.BlockSpec(
                    (1, routed, block), lambda i, where: (jnp.minimum(i, half - 1), 0, 0)
                ),
                pl.BlockSpec(
                    (1, routed, block), lambda i, where: (jnp.maximum(i - half, 0), 0, 0)
                ),
            ],
        ),
        compiler_params=pltpu.CompilerParams(vmem_limit_bytes=BIG_VMEM),
        cost_estimate=SMALL_COST,
        name="down",
    )(t.reshape(1).astype(jnp.int32), hidden, own)


def sum_tensor(send, keep, size):
    bit = 1
    while bit < size:
        if send.shape[0] == 1:
            send, keep = send[0], keep[0]
        arrived = xor_permute(send, "tensor", size, bit)
        total = keep.astype(jnp.float32) + arrived.astype(jnp.float32)
        bit *= 2
        if bit < size:
            send, keep = total[1::2].astype(jnp.bfloat16), total[0::2]
    return total.astype(jnp.bfloat16)


SMALL_COST = pl.CostEstimate(flops=1024, bytes_accessed=1024, transcendentals=0)
BIG_VMEM = 48 * 1024 * 1024


def all_after(values, *others):
    return list(lax.optimization_barrier((*values, *others))[: len(values)])


def ffn_kernel(order, where_ref, even_ref, odd_ref, gate_ref, up_ref, out_ref, gate_sum, up_sum):
    step = pl.program_id(0)
    count = 2 * len(order)

    @pl.when(step == 0)
    def _():
        gate_sum[...] = jnp.zeros_like(gate_sum)
        up_sum[...] = jnp.zeros_like(up_sum)

    for place, k in enumerate(order):
        for odd, stack in enumerate((even_ref, odd_ref)):

            @pl.when(step == k + odd)
            def _(place=place, stack=stack):
                rows = stack[place]
                gate_sum[...] += jnp.dot(rows, gate_ref[0], preferred_element_type=jnp.float32)
                up_sum[...] += jnp.dot(rows, up_ref[0], preferred_element_type=jnp.float32)

    @pl.when(step == count - 1)
    def _():
        gate = gate_sum[...]
        out_ref[...] = (gate / (1.0 + jnp.exp(-gate)) * up_sum[...]).astype(out_ref.dtype)


def ffn(stacks, order, gate_weight, up_weight, t):
    n, rows, width = stacks[0].shape
    units = gate_weight.shape[2]
    weight_spec = pl.BlockSpec((1, width, units), lambda k, where: (0, where[0] ^ k, 0))
    return pl.pallas_call(
        functools.partial(ffn_kernel, order),
        out_shape=jax.ShapeDtypeStruct((rows, units), jnp.bfloat16),
        grid_spec=pltpu.PrefetchScalarGridSpec(
            num_scalar_prefetch=1,
            grid=(2 * n,),
            in_specs=[pl.BlockSpec((n, rows, width), lambda k, where: (0, 0, 0))] * 2
            + [weight_spec, weight_spec],
            out_specs=pl.BlockSpec((rows, units), lambda k, where: (0, 0)),
            scratch_shapes=[pltpu.VMEM((rows, units), jnp.float32)] * 2,
        ),
        compiler_params=pltpu.CompilerParams(vmem_limit_bytes=BIG_VMEM),
        cost_estimate=SMALL_COST,
        name="ffn",
    )(t.reshape(1).astype(jnp.int32), *stacks, gate_weight, up_weight)


def chunks_of(width):
    lanes = 128
    if width % lanes or width < 2 * lanes:
        return [(0, width)]
    first = (width // lanes + 1) // 2 * lanes
    return [(0, first), (first, width - first)]


def one_hot(positions, count):
    selector = (positions[:, None] == jnp.arange(count, dtype=jnp.int32)[None, :]).astype(
        jnp.bfloat16
    )
    return lax.optimization_barrier(selector)


def pick_rows(selector, source):
    return jnp.dot(selector, source, preferred_element_type=jnp.float32).astype(jnp.bfloat16)


def after(value, *others):
    if not others:
        return value
    return lax.optimization_barrier((value,) + others)[0]


def columns_to_device(own, t, nt, off, width):
    block = own.shape[1] // nt
    found = []
    for k in range(nt):
        piece = lax.dynamic_slice(own, (0, (t ^ k) * block + off), (own.shape[0], width))
        found.append(xor_permute(piece, "tensor", nt, k) if k else piece)
    return found


def columns_in_two(own, t, off, width, *earlier):
    block = own.shape[1] // 4
    mine, near, far, both = [
        lax.dynamic_slice(own, (0, (t ^ k) * block + off), (own.shape[0], width)) for k in range(4)
    ]
    before_far, before_near = earlier or ((), ())
    first = xor_permute(after(jnp.stack([far, both]), *before_far), "tensor", 4, 2)
    pair = jnp.stack([near, after(first, *before_near)[1]])
    return [mine, first, xor_permute(pair, "tensor", 4, 1)]


def rows_to_device(pieces, nt):
    return [xor_permute(pieces[k], "tensor", nt, k) if k else pieces[k] for k in range(nt)]


T_AT, Q_AT, KEEP_AT, GIVE_AT, MINE_AT, MEMBER_AT = range(6)


def full_spec(shape):
    return pl.BlockSpec(shape, memory_space=pltpu.VMEM)


def align_kernel(nt, half, sub, flags_ref, place_ref, *refs):
    mine, first, second = refs[:3]
    outs = refs[3:]
    rows, width = mine.shape
    lane = lax.broadcasted_iota(jnp.int32, (rows, rows), 1)
    q = flags_ref[Q_AT]
    for k in range(half):
        start = pl.multiple_of((q ^ k) * sub, sub)
        place = jnp.concatenate(
            [place_ref[pl.ds(start + b * half * sub, sub), :] for b in range(nt)], axis=0
        )
        total = jnp.zeros((rows, width), jnp.float32)
        for m in range(nt):
            selector = jnp.where(place - m * rows == lane, 1.0, 0.0).astype(jnp.bfloat16)
            source = (mine[...], second[0], first[0], second[1])[m]
            total = total + jnp.dot(selector, source, preferred_element_type=jnp.float32)
        outs[k][...] = total.astype(jnp.bfloat16)


def align(flags, place, sources, half, sub):
    nt = 4
    rows, width = sources[0].shape
    piece = jax.ShapeDtypeStruct((rows, width), jnp.bfloat16)
    return pl.pallas_call(
        functools.partial(align_kernel, nt, half, sub),
        out_shape=[piece] * half,
        in_specs=[pl.BlockSpec(memory_space=pltpu.SMEM), full_spec(place.shape)]
        + [full_spec(source.shape) for source in sources],
        out_specs=[full_spec((rows, width))] * half,
        compiler_params=pltpu.CompilerParams(vmem_limit_bytes=BIG_VMEM),
        cost_estimate=SMALL_COST,
        name="align",
    )(flags, place, *sources)


def sums_kernel(half, tile, flags_ref, *refs):
    parts, sent_ref, kept_ref = refs[:half], refs[half], refs[half + 1]
    gives = [jnp.where(flags_ref[MEMBER_AT + k] == flags_ref[GIVE_AT], 1.0, 0.0) for k in range(half)]
    keeps = [jnp.where(flags_ref[MEMBER_AT + k] == flags_ref[KEEP_AT], 1.0, 0.0) for k in range(half)]

    @pl.loop(0, sent_ref.shape[0] // tile)
    def _(i):
        at = pl.ds(pl.multiple_of(i * tile, tile), tile)
        sent = kept = None
        for k in range(half):
            part = parts[k][at, :].astype(jnp.float32)
            sent = part * gives[k] if k == 0 else sent + part * gives[k]
            kept = part * keeps[k] if k == 0 else kept + part * keeps[k]
        sent_ref[at, :] = sent.astype(sent_ref.dtype)
        kept_ref[at, :] = kept


def sums(flags, parts):
    rows, width = parts[0].shape
    tile = min(32, rows)
    spec = full_spec((rows, width))
    return pl.pallas_call(
        functools.partial(sums_kernel, len(parts), tile),
        out_shape=[
            jax.ShapeDtypeStruct((rows, width), jnp.bfloat16),
            jax.ShapeDtypeStruct((rows, width), jnp.float32),
        ],
        in_specs=[pl.BlockSpec(memory_space=pltpu.SMEM)] + [spec] * len(parts),
        out_specs=[spec, spec],
        compiler_params=pltpu.CompilerParams(vmem_limit_bytes=BIG_VMEM),
        cost_estimate=SMALL_COST,
        name="sums",
    )(flags, *parts)


def mean_kernel(scale_ref, kept_ref, other_ref, mine_ref, near_ref, far_ref):
    sub = mine_ref.shape[0]
    scale = scale_ref[0]
    for m in range(4):
        at = pl.ds(m * sub, sub)
        total = kept_ref[at, :] + other_ref[at, :].astype(jnp.float32)
        value = (total * scale).astype(mine_ref.dtype)
        if m < 2:
            (mine_ref, near_ref)[m][...] = value
        else:
            far_ref[m - 2] = value


def mean_of(scale, kept, other):
    rows, width = kept.shape
    one, two = (rows // 4, width), (2, rows // 4, width)
    return pl.pallas_call(
        mean_kernel,
        out_shape=[jax.ShapeDtypeStruct(shape, jnp.bfloat16) for shape in (one, one, two)],
        in_specs=[pl.BlockSpec(memory_space=pltpu.SMEM)] + [full_spec((rows, width))] * 2,
        out_specs=[full_spec(one), full_spec(one), full_spec(two)],
        compiler_params=pltpu.CompilerParams(vmem_limit_bytes=BIG_VMEM),
        cost_estimate=SMALL_COST,
        name="mean",
    )(scale, kept, other)


def assemble_kernel(half, nt, spans, flags_ref, *refs):
    groups, out_ref = refs[:-1], refs[-1]
    sub = groups[0].shape[1]
    block = out_ref.shape[1] // nt
    mine = flags_ref[MINE_AT] != 0

    @pl.when(mine)
    def _():
        for k in range(half):
            at = pl.multiple_of((flags_ref[Q_AT] ^ k) * sub, sub)
            for m in range(nt):
                left = pl.multiple_of((flags_ref[T_AT] ^ m) * block, 128)
                for c, (off, width) in enumerate(spans):
                    out_ref[pl.ds(at, sub), pl.ds(left + off, width)] = groups[c * half + k][m]

    @pl.when(jnp.logical_not(mine))
    def _():
        out_ref[...] = jnp.zeros_like(out_ref)


def assemble(flags, gathered, spans, rows, model):
    half = len(gathered[0])
    nt = gathered[0][0].shape[0]
    groups = [piece for group in gathered for piece in group]
    return pl.pallas_call(
        functools.partial(assemble_kernel, half, nt, spans),
        out_shape=jax.ShapeDtypeStruct((rows, model), jnp.bfloat16),
        in_specs=[pl.BlockSpec(memory_space=pltpu.SMEM)]
        + [full_spec(piece.shape) for piece in groups],
        out_specs=full_spec((rows, model)),
        compiler_params=pltpu.CompilerParams(vmem_limit_bytes=BIG_VMEM),
        cost_estimate=SMALL_COST,
        name="assemble",
    )(flags, *groups)


class TwoClusters:
    def __init__(self, own, perm, cluster, owners, e, t, ne, nt):
        self.own, self.t, self.ne, self.nt = own, t, ne, nt
        rows, model = own.shape
        half = self.half = ne // 2
        self.sub = rows // half
        self.spans = chunks_of(model // nt)
        self.cluster, self.owners, self.e = cluster, owners, e
        q, side = e % half, e // half
        self.place = (((perm // rows) ^ t) * rows + perm % rows).reshape(-1, 1)
        experts = jnp.arange(ne, dtype=jnp.int32)
        near = (e ^ jnp.arange(half, dtype=jnp.int32))[:, None] == experts[None, :]
        member = jnp.sum(jnp.where(near, cluster[None, :], 0), axis=1)
        sides = owners // half
        keep = jnp.where(sides[0:1] == side, 0, 1)
        give = jnp.where(sides[0:1] != side, 0, 1)
        mine = jnp.where(jnp.where(keep == 0, owners[0:1], owners[1:2]) == e, 1, 0)
        self.flags = jnp.concatenate(
            [t.reshape(1), q.reshape(1), keep, give, mine, member]
        ).astype(jnp.int32)
        self.sizes = jnp.sum(
            (cluster[None, :] == jnp.arange(2, dtype=jnp.int32)[:, None]).astype(jnp.float32),
            axis=1,
        )
        self.scale = 1.0 / jnp.where(keep == 0, self.sizes[0:1], self.sizes[1:2])

    def columns(self, c, *earlier):
        return columns_in_two(self.own, self.t, *self.spans[c], *earlier)

    def send_aligned(self, sources, *earlier):
        sources = all_after(sources, *earlier)
        pieces = align(self.flags, self.place, sources, self.half, self.sub)
        sent = [
            xor_permute(piece, "expert", self.ne, k) if k else piece
            for k, piece in enumerate(pieces)
        ]
        return pieces[0], sent

    def back(self, pieces):
        mine, near, far = pieces
        first = xor_permute(far, "tensor", 4, 2)
        second = xor_permute(jnp.stack([near, first[1]]), "tensor", 4, 1)
        return jnp.stack([mine, second[0], first[0], second[1]])

    def out(self, lines):
        return [
            xor_permute(lines, "expert", self.ne, k) if k else lines for k in range(self.half)
        ]

    def finish(self, gathered, arrived):
        rows, model = self.own.shape
        first = assemble(self.flags, gathered, self.spans, rows, model)
        sides = self.owners // self.half

        def second(args):
            first, arrived = args
            near = self.cluster[self.e ^ jnp.arange(self.half, dtype=jnp.int32)]
            again = []
            for parts in arrived:
                total = jnp.zeros(parts[0].shape, jnp.float32)
                for k in range(self.half):
                    total = total + jnp.where(near[k] == 1, parts[k].astype(jnp.float32), 0.0)
                other = xor_permute(total.astype(jnp.bfloat16), "expert", self.ne, self.half)
                scale = (1.0 / self.sizes[1]).reshape(1)
                again.append(self.out(self.back(mean_of(scale, total, other))))
            mine = jnp.where(self.owners[1:2] == self.e, 1, 0).astype(jnp.int32)
            flags = jnp.concatenate(
                [self.flags[:MINE_AT], mine, self.flags[MINE_AT + 1 :]]
            )
            return first + assemble(flags, again, self.spans, rows, model)

        return lax.cond(
            sides[0] == sides[1], second, lambda args: args[0], (first, arrived)
        )


def merge_any(own, perm, cluster, owners, e, t, ne, nt):
    rows, model = own.shape
    block = model // nt
    clusters = owners.shape[0]
    sub = rows // ne
    placed = ((perm // rows) ^ t) * rows + perm % rows
    placed = placed.reshape(nt, ne, sub).transpose(1, 0, 2).reshape(-1)
    aligned = pick_rows(
        one_hot(placed, rows * nt), jnp.concatenate(columns_to_device(own, t, nt, 0, block))
    )
    arrived = lax.all_to_all(aligned, "expert", split_axis=0, concat_axis=0, tiled=True)
    arrived = arrived.reshape(ne, nt, sub, block)
    member = cluster[None, :] == jnp.arange(clusters, dtype=jnp.int32)[:, None]
    inverse = 1.0 / jnp.sum(member.astype(jnp.float32), axis=1)
    means = []
    for c in range(clusters):
        total = jnp.sum(
            jnp.where(member[c][:, None, None, None], arrived.astype(jnp.float32), 0.0), axis=0
        )
        means.append((total * inverse[c]).astype(jnp.bfloat16))
    back = jnp.stack(rows_to_device(jnp.stack(means, axis=1), nt))
    back = jnp.take(back, jnp.arange(nt, dtype=jnp.int32) ^ t, axis=0)
    lines = back.transpose(1, 2, 0, 3).reshape(clusters, sub, model)
    outgoing = jnp.zeros((ne, sub, model), jnp.bfloat16).at[owners].set(lines)
    return lax.all_to_all(
        outgoing.reshape(ne * sub, model), "expert", split_axis=0, concat_axis=0, tiled=True
    )


def on_device(
    tokens,
    routes,
    gate_values,
    probe_rows,
    gate_weight,
    up_weight,
    down_weight,
    hidden_perm,
    cluster,
    owners,
):
    ne = lax.axis_size("expert")
    nt = lax.axis_size("tensor")
    e = lax.axis_index("expert").astype(jnp.int32)
    t = lax.axis_index("tensor").astype(jnp.int32)
    tok_rows, top = routes.shape
    capacity = tok_rows * top * 5 // (4 * ne)
    own = down_weight[0]
    model = own.shape[1]
    block = model // nt

    perm = jnp.concatenate(gather_small(hidden_perm[0], nt))
    two = None
    if ne == 8 and nt == 4 and owners.shape[0] == 2:
        two = TwoClusters(own, perm, cluster, owners, e, t, ne, nt)

    flat = routes.reshape(-1)
    pairs = jnp.arange(flat.shape[0], dtype=jnp.int32)
    earlier = (flat[:, None] == flat[None, :]) & (pairs[None, :] < pairs[:, None])
    target = flat * capacity + jnp.sum(earlier.astype(jnp.int32), axis=1)
    target = target.reshape(tok_rows, top)
    slots = jnp.arange(ne * capacity, dtype=jnp.int32)
    selector = jnp.zeros((ne * capacity, tok_rows), jnp.bool_)
    for k in range(top):
        selector = selector | (slots[:, None] == target[:, k][None, :])
    outgoing = jnp.dot(
        selector.astype(jnp.bfloat16), tokens, preferred_element_type=jnp.float32
    ).astype(jnp.bfloat16)
    arrived = lax.all_to_all(outgoing, "expert", split_axis=0, concat_axis=0, tiled=True)
    routed = arrived.shape[0]
    stacked = jnp.concatenate([arrived, probe_rows], axis=0)
    if two is not None:
        last = len(two.spans) - 1
        source = two.columns(0)
        mark, sent = two.send_aligned(source)
        parts = [sent]
        stacked = after(stacked, source[1])
    even, order = gather_even(stacked, nt, *([] if two is None else [mark]))
    odd = xor_permute(even, "tensor", nt, 1)
    hidden = ffn((even, odd), order, gate_weight, up_weight, t)
    probe_hidden = hidden[routed:]
    everyone = lax.all_gather(probe_hidden, "expert", axis=0)
    at_owner = jnp.arange(ne, dtype=jnp.int32) == owners[cluster[e]]
    partner = jnp.sum(
        jnp.where(at_owner[:, None, None], everyone.astype(jnp.float32), 0.0), axis=0
    ).astype(jnp.bfloat16)

    def correlate(partner):
        partner_full = lax.all_gather(partner, "tensor", axis=1, tiled=True)
        found = lax.dot_general(
            probe_hidden, partner_full, (((0,), (0,)), ((), ())), preferred_element_type=jnp.float32
        )
        return found / probe_hidden.shape[0]

    send, keep = down(hidden, routed, own, t, nt)
    if two is not None:
        others, kept = [], []
        for c in range(last + 1):
            if c < last:
                source = two.columns(c + 1, (even,), (*parts[c][1:], send))
                mark, sent = two.send_aligned(source, mark)
                parts.append(sent)
            ready = all_after(parts[c], *((others[-1], returned, correlation) if c else (send,)))
            given, own_sum = sums(two.flags, ready)
            others.append(xor_permute(given, "expert", ne, two.half))
            kept.append(own_sum)
            if not c:
                returned = sum_tensor(send, after(keep, mark), nt)
                correlation = correlate(after(partner, own_sum))
        lines = two.back(mean_of(two.scale, kept[0], after(others[0], kept[-1])))
        lines = after(lines, others[-1])
    else:
        returned = sum_tensor(send, keep, nt)
        correlation = correlate(partner)
    home = lax.all_to_all(returned, "expert", split_axis=0, concat_axis=0, tiled=True)
    chooser = (target.T.reshape(-1)[:, None] == slots[None, :]).astype(jnp.bfloat16)
    picked = jnp.dot(chooser, home, preferred_element_type=jnp.float32)
    picked = picked.reshape(top, tok_rows, block)
    mixed = jnp.sum(gate_values.T[:, :, None] * picked, axis=0).astype(jnp.bfloat16)

    if two is not None:
        gathered = [two.out(lines)]
        for c in range(1, len(two.spans)):
            means = mean_of(two.scale, kept[c], others[c])
            lines = two.back(means)
            gathered.append(two.out(lines))
        gathered[-1][0] = after(gathered[-1][0], mixed)
        merged = two.finish(gathered, parts)
    else:
        merged = merge_any(own, perm, cluster, owners, e, t, ne, nt)
    return (mixed, correlation[None], merged[None])


def solution(mesh):
    in_specs = (
        P("expert", "tensor"),
        P("expert", None),
        P("expert", None),
        P(None, "tensor"),
        P("expert", None, "tensor"),
        P("expert", None, "tensor"),
        P("expert", "tensor", None),
        P("expert", "tensor"),
        P(),
        P(),
    )
    out_specs = (P("expert", "tensor"), P("expert", "tensor", None), P("expert", "tensor", None))
    return jax.shard_map(
        on_device, mesh=mesh, in_specs=in_specs, out_specs=out_specs, check_vma=False
    )
```

```python
import functools

import jax
import jax.numpy as jnp
from jax import lax
from jax.experimental import pallas as pl
from jax.experimental.pallas import tpu as pltpu
from jax.sharding import PartitionSpec as P


def xor_permute(value, axis, size, k):
    return lax.ppermute(value, axis, [(i, i ^ k) for i in range(size)])


def gather_small(value, size):
    held = {0: value}
    bit = size // 2
    while bit:
        for k in sorted(held):
            held[k ^ bit] = xor_permute(held[k], "tensor", size, bit)
        bit //= 2
    return [held[k] for k in range(size)]


def gather_even(value, size, *others):
    stack, order = value[None], [0]
    bit = size // 2
    while bit > 1:
        arrived = after(xor_permute(stack, "tensor", size, bit), *others)
        stack = jnp.concatenate([stack, arrived])
        order = order + [k ^ bit for k in order]
        bit //= 2
    return stack, order


def down_kernel(count, where_ref, rows_ref, weight_ref, send_ref, keep_ref):
    step = pl.program_id(0)
    part = jnp.dot(rows_ref[...], weight_ref[...], preferred_element_type=jnp.float32)

    @pl.when(step < count // 2)
    def _():
        send_ref[0] = part.astype(send_ref.dtype)

    @pl.when(step >= count // 2)
    def _():
        keep_ref[0] = part.astype(keep_ref.dtype)


def down(hidden, routed, own, t, count):
    units, model = own.shape
    block = model // count
    half = count // 2

    def column(i, where):
        return (0, where[0] ^ jnp.where(i < half, 2 * i + 1, 2 * (i - half)))

    shape = jax.ShapeDtypeStruct((half, routed, block), jnp.bfloat16)
    return pl.pallas_call(
        functools.partial(down_kernel, count),
        out_shape=[shape, shape],
        grid_spec=pltpu.PrefetchScalarGridSpec(
            num_scalar_prefetch=1,
            grid=(count,),
            in_specs=[
                pl.BlockSpec((routed, units), lambda i, where: (0, 0)),
                pl.BlockSpec((units, block), column),
            ],
            out_specs=[
                pl.BlockSpec(
                    (1, routed, block), lambda i, where: (jnp.minimum(i, half - 1), 0, 0)
                ),
                pl.BlockSpec(
                    (1, routed, block), lambda i, where: (jnp.maximum(i - half, 0), 0, 0)
                ),
            ],
        ),
        compiler_params=pltpu.CompilerParams(vmem_limit_bytes=BIG_VMEM),
        cost_estimate=SMALL_COST,
        name="down",
    )(t.reshape(1).astype(jnp.int32), hidden, own)


def sum_tensor(send, keep, size):
    bit = 1
    while bit < size:
        if send.shape[0] == 1:
            send, keep = send[0], keep[0]
        arrived = xor_permute(send, "tensor", size, bit)
        total = keep.astype(jnp.float32) + arrived.astype(jnp.float32)
        bit *= 2
        if bit < size:
            send, keep = total[1::2].astype(jnp.bfloat16), total[0::2]
    return total.astype(jnp.bfloat16)


SMALL_COST = pl.CostEstimate(flops=1024, bytes_accessed=1024, transcendentals=0)
BIG_VMEM = 48 * 1024 * 1024


def all_after(values, *others):
    return list(lax.optimization_barrier((*values, *others))[: len(values)])


def ffn_kernel(order, where_ref, even_ref, odd_ref, gate_ref, up_ref, out_ref, gate_sum, up_sum):
    step = pl.program_id(0)
    count = 2 * len(order)

    @pl.when(step == 0)
    def _():
        gate_sum[...] = jnp.zeros_like(gate_sum)
        up_sum[...] = jnp.zeros_like(up_sum)

    for place, k in enumerate(order):
        for odd, stack in enumerate((even_ref, odd_ref)):

            @pl.when(step == k + odd)
            def _(place=place, stack=stack):
                rows = stack[place]
                gate_sum[...] += jnp.dot(rows, gate_ref[0], preferred_element_type=jnp.float32)
                up_sum[...] += jnp.dot(rows, up_ref[0], preferred_element_type=jnp.float32)

    @pl.when(step == count - 1)
    def _():
        gate = gate_sum[...]
        out_ref[...] = (gate / (1.0 + jnp.exp(-gate)) * up_sum[...]).astype(out_ref.dtype)


def ffn(stacks, order, gate_weight, up_weight, t):
    n, rows, width = stacks[0].shape
    units = gate_weight.shape[2]
    weight_spec = pl.BlockSpec((1, width, units), lambda k, where: (0, where[0] ^ k, 0))
    return pl.pallas_call(
        functools.partial(ffn_kernel, order),
        out_shape=jax.ShapeDtypeStruct((rows, units), jnp.bfloat16),
        grid_spec=pltpu.PrefetchScalarGridSpec(
            num_scalar_prefetch=1,
            grid=(2 * n,),
            in_specs=[pl.BlockSpec((n, rows, width), lambda k, where: (0, 0, 0))] * 2
            + [weight_spec, weight_spec],
            out_specs=pl.BlockSpec((rows, units), lambda k, where: (0, 0)),
            scratch_shapes=[pltpu.VMEM((rows, units), jnp.float32)] * 2,
        ),
        compiler_params=pltpu.CompilerParams(vmem_limit_bytes=BIG_VMEM),
        cost_estimate=SMALL_COST,
        name="ffn",
    )(t.reshape(1).astype(jnp.int32), *stacks, gate_weight, up_weight)


def chunks_of(width):
    lanes = 128
    if width % lanes or width < 2 * lanes:
        return [(0, width)]
    first = (width // lanes + 1) // 2 * lanes
    return [(0, first), (first, width - first)]


def one_hot(positions, count):
    selector = (positions[:, None] == jnp.arange(count, dtype=jnp.int32)[None, :]).astype(
        jnp.bfloat16
    )
    return lax.optimization_barrier(selector)


def pick_rows(selector, source):
    return jnp.dot(selector, source, preferred_element_type=jnp.float32).astype(jnp.bfloat16)


def after(value, *others):
    if not others:
        return value
    return lax.optimization_barrier((value,) + others)[0]


def columns_to_device(own, t, nt, off, width):
    block = own.shape[1] // nt
    found = []
    for k in range(nt):
        piece = lax.dynamic_slice(own, (0, (t ^ k) * block + off), (own.shape[0], width))
        found.append(xor_permute(piece, "tensor", nt, k) if k else piece)
    return found


def columns_in_two(own, t, off, width, *earlier):
    block = own.shape[1] // 4
    mine, near, far, both = [
        lax.dynamic_slice(own, (0, (t ^ k) * block + off), (own.shape[0], width)) for k in range(4)
    ]
    before_far, before_near = earlier or ((), ())
    first = xor_permute(after(jnp.stack([far, both]), *before_far), "tensor", 4, 2)
    pair = jnp.stack([near, after(first, *before_near)[1]])
    return [mine, first, xor_permute(pair, "tensor", 4, 1)]


def rows_to_device(pieces, nt):
    return [xor_permute(pieces[k], "tensor", nt, k) if k else pieces[k] for k in range(nt)]


T_AT, Q_AT, KEEP_AT, GIVE_AT, MINE_AT, MEMBER_AT = range(6)


def full_spec(shape):
    return pl.BlockSpec(shape, memory_space=pltpu.VMEM)


def align_kernel(nt, half, sub, flags_ref, place_ref, *refs):
    mine, first, second = refs[:3]
    outs = refs[3:]
    rows, width = mine.shape
    lane = lax.broadcasted_iota(jnp.int32, (rows, rows), 1)
    q = flags_ref[Q_AT]
    for k in range(half):
        start = pl.multiple_of((q ^ k) * sub, sub)
        place = jnp.concatenate(
            [place_ref[pl.ds(start + b * half * sub, sub), :] for b in range(nt)], axis=0
        )
        total = jnp.zeros((rows, width), jnp.float32)
        for m in range(nt):
            selector = jnp.where(place - m * rows == lane, 1.0, 0.0).astype(jnp.bfloat16)
            source = (mine[...], second[0], first[0], second[1])[m]
            total = total + jnp.dot(selector, source, preferred_element_type=jnp.float32)
        outs[k][...] = total.astype(jnp.bfloat16)


def align(flags, place, sources, half, sub):
    nt = 4
    rows, width = sources[0].shape
    piece = jax.ShapeDtypeStruct((rows, width), jnp.bfloat16)
    return pl.pallas_call(
        functools.partial(align_kernel, nt, half, sub),
        out_shape=[piece] * half,
        in_specs=[pl.BlockSpec(memory_space=pltpu.SMEM), full_spec(place.shape)]
        + [full_spec(source.shape) for source in sources],
        out_specs=[full_spec((rows, width))] * half,
        compiler_params=pltpu.CompilerParams(vmem_limit_bytes=BIG_VMEM),
        cost_estimate=SMALL_COST,
        name="align",
    )(flags, place, *sources)


def sums_kernel(half, tile, flags_ref, *refs):
    parts, sent_ref, kept_ref = refs[:half], refs[half], refs[half + 1]
    gives = [jnp.where(flags_ref[MEMBER_AT + k] == flags_ref[GIVE_AT], 1.0, 0.0) for k in range(half)]
    keeps = [jnp.where(flags_ref[MEMBER_AT + k] == flags_ref[KEEP_AT], 1.0, 0.0) for k in range(half)]

    @pl.loop(0, sent_ref.shape[0] // tile)
    def _(i):
        at = pl.ds(pl.multiple_of(i * tile, tile), tile)
        sent = kept = None
        for k in range(half):
            part = parts[k][at, :].astype(jnp.float32)
            sent = part * gives[k] if k == 0 else sent + part * gives[k]
            kept = part * keeps[k] if k == 0 else kept + part * keeps[k]
        sent_ref[at, :] = sent.astype(sent_ref.dtype)
        kept_ref[at, :] = kept


def sums(flags, parts):
    rows, width = parts[0].shape
    tile = min(32, rows)
    spec = full_spec((rows, width))
    return pl.pallas_call(
        functools.partial(sums_kernel, len(parts), tile),
        out_shape=[
            jax.ShapeDtypeStruct((rows, width), jnp.bfloat16),
            jax.ShapeDtypeStruct((rows, width), jnp.float32),
        ],
        in_specs=[pl.BlockSpec(memory_space=pltpu.SMEM)] + [spec] * len(parts),
        out_specs=[spec, spec],
        compiler_params=pltpu.CompilerParams(vmem_limit_bytes=BIG_VMEM),
        cost_estimate=SMALL_COST,
        name="sums",
    )(flags, *parts)


def mean_kernel(scale_ref, kept_ref, other_ref, mine_ref, near_ref, far_ref):
    sub = mine_ref.shape[0]
    scale = scale_ref[0]
    for m in range(4):
        at = pl.ds(m * sub, sub)
        total = kept_ref[at, :] + other_ref[at, :].astype(jnp.float32)
        value = (total * scale).astype(mine_ref.dtype)
        if m < 2:
            (mine_ref, near_ref)[m][...] = value
        else:
            far_ref[m - 2] = value


def mean_of(scale, kept, other):
    rows, width = kept.shape
    one, two = (rows // 4, width), (2, rows // 4, width)
    return pl.pallas_call(
        mean_kernel,
        out_shape=[jax.ShapeDtypeStruct(shape, jnp.bfloat16) for shape in (one, one, two)],
        in_specs=[pl.BlockSpec(memory_space=pltpu.SMEM)] + [full_spec((rows, width))] * 2,
        out_specs=[full_spec(one), full_spec(one), full_spec(two)],
        compiler_params=pltpu.CompilerParams(vmem_limit_bytes=BIG_VMEM),
        cost_estimate=SMALL_COST,
        name="mean",
    )(scale, kept, other)


def assemble_kernel(half, nt, spans, flags_ref, *refs):
    groups, out_ref = refs[:-1], refs[-1]
    sub = groups[0].shape[1]
    block = out_ref.shape[1] // nt
    mine = flags_ref[MINE_AT] != 0

    @pl.when(mine)
    def _():
        for k in range(half):
            at = pl.multiple_of((flags_ref[Q_AT] ^ k) * sub, sub)
            for m in range(nt):
                left = pl.multiple_of((flags_ref[T_AT] ^ m) * block, 128)
                for c, (off, width) in enumerate(spans):
                    out_ref[pl.ds(at, sub), pl.ds(left + off, width)] = groups[c * half + k][m]

    @pl.when(jnp.logical_not(mine))
    def _():
        out_ref[...] = jnp.zeros_like(out_ref)


def assemble(flags, gathered, spans, rows, model):
    half = len(gathered[0])
    nt = gathered[0][0].shape[0]
    groups = [piece for group in gathered for piece in group]
    return pl.pallas_call(
        functools.partial(assemble_kernel, half, nt, spans),
        out_shape=jax.ShapeDtypeStruct((rows, model), jnp.bfloat16),
        in_specs=[pl.BlockSpec(memory_space=pltpu.SMEM)]
        + [full_spec(piece.shape) for piece in groups],
        out_specs=full_spec((rows, model)),
        compiler_params=pltpu.CompilerParams(vmem_limit_bytes=BIG_VMEM),
        cost_estimate=SMALL_COST,
        name="assemble",
    )(flags, *groups)


class TwoClusters:
    def __init__(self, own, perm, cluster, owners, e, t, ne, nt):
        self.own, self.t, self.ne, self.nt = own, t, ne, nt
        rows, model = own.shape
        half = self.half = ne // 2
        self.sub = rows // half
        self.spans = chunks_of(model // nt)
        self.cluster, self.owners, self.e = cluster, owners, e
        q, side = e % half, e // half
        self.place = (((perm // rows) ^ t) * rows + perm % rows).reshape(-1, 1)
        experts = jnp.arange(ne, dtype=jnp.int32)
        near = (e ^ jnp.arange(half, dtype=jnp.int32))[:, None] == experts[None, :]
        member = jnp.sum(jnp.where(near, cluster[None, :], 0), axis=1)
        sides = owners // half
        keep = jnp.where(sides[0:1] == side, 0, 1)
        give = jnp.where(sides[0:1] != side, 0, 1)
        mine = jnp.where(jnp.where(keep == 0, owners[0:1], owners[1:2]) == e, 1, 0)
        self.flags = jnp.concatenate(
            [t.reshape(1), q.reshape(1), keep, give, mine, member]
        ).astype(jnp.int32)
        self.sizes = jnp.sum(
            (cluster[None, :] == jnp.arange(2, dtype=jnp.int32)[:, None]).astype(jnp.float32),
            axis=1,
        )
        self.scale = 1.0 / jnp.where(keep == 0, self.sizes[0:1], self.sizes[1:2])

    def columns(self, c, *earlier):
        return columns_in_two(self.own, self.t, *self.spans[c], *earlier)

    def send_aligned(self, sources, *earlier):
        sources = all_after(sources, *earlier)
        pieces = align(self.flags, self.place, sources, self.half, self.sub)
        sent = [
            xor_permute(piece, "expert", self.ne, k) if k else piece
            for k, piece in enumerate(pieces)
        ]
        return pieces[0], sent

    def back(self, pieces):
        mine, near, far = pieces
        first = xor_permute(far, "tensor", 4, 2)
        second = xor_permute(jnp.stack([near, first[1]]), "tensor", 4, 1)
        return jnp.stack([mine, second[0], first[0], second[1]])

    def out(self, lines):
        return [
            xor_permute(lines, "expert", self.ne, k) if k else lines for k in range(self.half)
        ]

    def finish(self, gathered, arrived):
        rows, model = self.own.shape
        first = assemble(self.flags, gathered, self.spans, rows, model)
        sides = self.owners // self.half

        def second(args):
            first, arrived = args
            near = self.cluster[self.e ^ jnp.arange(self.half, dtype=jnp.int32)]
            again = []
            for parts in arrived:
                total = jnp.zeros(parts[0].shape, jnp.float32)
                for k in range(self.half):
                    total = total + jnp.where(near[k] == 1, parts[k].astype(jnp.float32), 0.0)
                other = xor_permute(total.astype(jnp.bfloat16), "expert", self.ne, self.half)
                scale = (1.0 / self.sizes[1]).reshape(1)
                again.append(self.out(self.back(mean_of(scale, total, other))))
            mine = jnp.where(self.owners[1:2] == self.e, 1, 0).astype(jnp.int32)
            flags = jnp.concatenate(
                [self.flags[:MINE_AT], mine, self.flags[MINE_AT + 1 :]]
            )
            return first + assemble(flags, again, self.spans, rows, model)

        return lax.cond(
            sides[0] == sides[1], second, lambda args: args[0], (first, arrived)
        )


def merge_any(own, perm, cluster, owners, e, t, ne, nt):
    rows, model = own.shape
    block = model // nt
    clusters = owners.shape[0]
    sub = rows // ne
    placed = ((perm // rows) ^ t) * rows + perm % rows
    placed = placed.reshape(nt, ne, sub).transpose(1, 0, 2).reshape(-1)
    aligned = pick_rows(
        one_hot(placed, rows * nt), jnp.concatenate(columns_to_device(own, t, nt, 0, block))
    )
    arrived = lax.all_to_all(aligned, "expert", split_axis=0, concat_axis=0, tiled=True)
    arrived = arrived.reshape(ne, nt, sub, block)
    member = cluster[None, :] == jnp.arange(clusters, dtype=jnp.int32)[:, None]
    inverse = 1.0 / jnp.sum(member.astype(jnp.float32), axis=1)
    means = []
    for c in range(clusters):
        total = jnp.sum(
            jnp.where(member[c][:, None, None, None], arrived.astype(jnp.float32), 0.0), axis=0
        )
        means.append((total * inverse[c]).astype(jnp.bfloat16))
    back = jnp.stack(rows_to_device(jnp.stack(means, axis=1), nt))
    back = jnp.take(back, jnp.arange(nt, dtype=jnp.int32) ^ t, axis=0)
    lines = back.transpose(1, 2, 0, 3).reshape(clusters, sub, model)
    outgoing = jnp.zeros((ne, sub, model), jnp.bfloat16).at[owners].set(lines)
    return lax.all_to_all(
        outgoing.reshape(ne * sub, model), "expert", split_axis=0, concat_axis=0, tiled=True
    )


def on_device(
    tokens,
    routes,
    gate_values,
    probe_rows,
    gate_weight,
    up_weight,
    down_weight,
    hidden_perm,
    cluster,
    owners,
):
    ne = lax.axis_size("expert")
    nt = lax.axis_size("tensor")
    e = lax.axis_index("expert").astype(jnp.int32)
    t = lax.axis_index("tensor").astype(jnp.int32)
    tok_rows, top = routes.shape
    capacity = tok_rows * top * 5 // (4 * ne)
    own = down_weight[0]
    model = own.shape[1]
    block = model // nt

    perm = jnp.concatenate(gather_small(hidden_perm[0], nt))
    two = None
    if ne == 8 and nt == 4 and owners.shape[0] == 2:
        two = TwoClusters(own, perm, cluster, owners, e, t, ne, nt)

    flat = routes.reshape(-1)
    pairs = jnp.arange(flat.shape[0], dtype=jnp.int32)
    earlier = (flat[:, None] == flat[None, :]) & (pairs[None, :] < pairs[:, None])
    target = flat * capacity + jnp.sum(earlier.astype(jnp.int32), axis=1)
    target = target.reshape(tok_rows, top)
    slots = jnp.arange(ne * capacity, dtype=jnp.int32)
    selector = jnp.zeros((ne * capacity, tok_rows), jnp.bool_)
    for k in range(top):
        selector = selector | (slots[:, None] == target[:, k][None, :])
    outgoing = jnp.dot(
        selector.astype(jnp.bfloat16), tokens, preferred_element_type=jnp.float32
    ).astype(jnp.bfloat16)
    arrived = lax.all_to_all(outgoing, "expert", split_axis=0, concat_axis=0, tiled=True)
    routed = arrived.shape[0]
    stacked = jnp.concatenate([arrived, probe_rows], axis=0)
    if two is not None:
        last = len(two.spans) - 1
        source = two.columns(0)
        mark, sent = two.send_aligned(source)
        parts = [sent]
        stacked = after(stacked, source[1])
    even, order = gather_even(stacked, nt, *([] if two is None else [mark]))
    odd = xor_permute(even, "tensor", nt, 1)
    hidden = ffn((even, odd), order, gate_weight, up_weight, t)
    probe_hidden = hidden[routed:]
    everyone = lax.all_gather(probe_hidden, "expert", axis=0)
    at_owner = jnp.arange(ne, dtype=jnp.int32) == owners[cluster[e]]
    partner = jnp.sum(
        jnp.where(at_owner[:, None, None], everyone.astype(jnp.float32), 0.0), axis=0
    ).astype(jnp.bfloat16)

    def correlate(partner):
        partner_full = lax.all_gather(partner, "tensor", axis=1, tiled=True)
        found = lax.dot_general(
            probe_hidden, partner_full, (((0,), (0,)), ((), ())), preferred_element_type=jnp.float32
        )
        return found / probe_hidden.shape[0]

    send, keep = down(hidden, routed, own, t, nt)
    if two is not None:
        others, kept = [], []
        for c in range(last + 1):
            if c < last:
                source = two.columns(c + 1, (even,), (*parts[c][1:], send))
                mark, sent = two.send_aligned(source, mark)
                parts.append(sent)
            ready = all_after(parts[c], *((others[-1], returned) if c else (send,)))
            given, own_sum = sums(two.flags, ready)
            others.append(xor_permute(given, "expert", ne, two.half))
            kept.append(own_sum)
            if not c:
                returned = sum_tensor(send, after(keep, mark), nt)
        lines = two.back(mean_of(two.scale, kept[0], after(others[0], kept[-1])))
        lines = after(lines, others[-1])
    else:
        returned = sum_tensor(send, keep, nt)
        correlation = correlate(partner)
    home = lax.all_to_all(returned, "expert", split_axis=0, concat_axis=0, tiled=True)
    chooser = (target.T.reshape(-1)[:, None] == slots[None, :]).astype(jnp.bfloat16)
    picked = jnp.dot(chooser, home, preferred_element_type=jnp.float32)
    picked = picked.reshape(top, tok_rows, block)
    mixed = jnp.sum(gate_values.T[:, :, None] * picked, axis=0).astype(jnp.bfloat16)

    if two is not None:
        gathered = [two.out(lines)]
        for c in range(1, len(two.spans)):
            means = mean_of(two.scale, kept[c], others[c])
            lines = two.back(means)
            gathered.append(two.out(lines))
        correlation = correlate(after(partner, lines))
        gathered[-1][0] = after(gathered[-1][0], mixed, correlation)
        merged = two.finish(gathered, parts)
    else:
        merged = merge_any(own, perm, cluster, owners, e, t, ne, nt)
    return (mixed, correlation[None], merged[None])


def solution(mesh):
    in_specs = (
        P("expert", "tensor"),
        P("expert", None),
        P("expert", None),
        P(None, "tensor"),
        P("expert", None, "tensor"),
        P("expert", None, "tensor"),
        P("expert", "tensor", None),
        P("expert", "tensor"),
        P(),
        P(),
    )
    out_specs = (P("expert", "tensor"), P("expert", "tensor", None), P("expert", "tensor", None))
    return jax.shard_map(
        on_device, mesh=mesh, in_specs=in_specs, out_specs=out_specs, check_vma=False
    )
```

```python
import functools

import jax
import jax.numpy as jnp
from jax import lax
from jax.experimental import pallas as pl
from jax.experimental.pallas import tpu as pltpu
from jax.sharding import PartitionSpec as P


def xor_permute(value, axis, size, k):
    return lax.ppermute(value, axis, [(i, i ^ k) for i in range(size)])


def gather_small(value, size):
    held = {0: value}
    bit = size // 2
    while bit:
        for k in sorted(held):
            held[k ^ bit] = xor_permute(held[k], "tensor", size, bit)
        bit //= 2
    return [held[k] for k in range(size)]


def gather_even(value, size, *others):
    stack, order = value[None], [0]
    bit = size // 2
    while bit > 1:
        arrived = after(xor_permute(stack, "tensor", size, bit), *others)
        stack = jnp.concatenate([stack, arrived])
        order = order + [k ^ bit for k in order]
        bit //= 2
    return stack, order


def down_kernel(count, where_ref, rows_ref, weight_ref, send_ref, keep_ref):
    step = pl.program_id(0)
    part = jnp.dot(rows_ref[...], weight_ref[...], preferred_element_type=jnp.float32)

    @pl.when(step < count // 2)
    def _():
        send_ref[0] = part.astype(send_ref.dtype)

    @pl.when(step >= count // 2)
    def _():
        keep_ref[0] = part.astype(keep_ref.dtype)


def down(hidden, routed, own, t, count):
    units, model = own.shape
    block = model // count
    half = count // 2

    def column(i, where):
        return (0, where[0] ^ jnp.where(i < half, 2 * i + 1, 2 * (i - half)))

    shape = jax.ShapeDtypeStruct((half, routed, block), jnp.bfloat16)
    return pl.pallas_call(
        functools.partial(down_kernel, count),
        out_shape=[shape, shape],
        grid_spec=pltpu.PrefetchScalarGridSpec(
            num_scalar_prefetch=1,
            grid=(count,),
            in_specs=[
                pl.BlockSpec((routed, units), lambda i, where: (0, 0)),
                pl.BlockSpec((units, block), column),
            ],
            out_specs=[
                pl.BlockSpec(
                    (1, routed, block), lambda i, where: (jnp.minimum(i, half - 1), 0, 0)
                ),
                pl.BlockSpec(
                    (1, routed, block), lambda i, where: (jnp.maximum(i - half, 0), 0, 0)
                ),
            ],
        ),
        compiler_params=pltpu.CompilerParams(vmem_limit_bytes=BIG_VMEM),
        cost_estimate=SMALL_COST,
        name="down",
    )(t.reshape(1).astype(jnp.int32), hidden, own)


def sum_tensor(send, keep, size):
    bit = 1
    while bit < size:
        if send.shape[0] == 1:
            send, keep = send[0], keep[0]
        arrived = xor_permute(send, "tensor", size, bit)
        total = keep.astype(jnp.float32) + arrived.astype(jnp.float32)
        bit *= 2
        if bit < size:
            send, keep = total[1::2].astype(jnp.bfloat16), total[0::2]
    return total.astype(jnp.bfloat16)


SMALL_COST = pl.CostEstimate(flops=1024, bytes_accessed=1024, transcendentals=0)
BIG_VMEM = 48 * 1024 * 1024


def all_after(values, *others):
    return list(lax.optimization_barrier((*values, *others))[: len(values)])


def ffn_kernel(order, where_ref, even_ref, odd_ref, gate_ref, up_ref, out_ref, gate_sum, up_sum):
    step = pl.program_id(0)
    count = 2 * len(order)

    @pl.when(step == 0)
    def _():
        gate_sum[...] = jnp.zeros_like(gate_sum)
        up_sum[...] = jnp.zeros_like(up_sum)

    for place, k in enumerate(order):
        for odd, stack in enumerate((even_ref, odd_ref)):

            @pl.when(step == k + odd)
            def _(place=place, stack=stack):
                rows = stack[place]
                gate_sum[...] += jnp.dot(rows, gate_ref[0], preferred_element_type=jnp.float32)
                up_sum[...] += jnp.dot(rows, up_ref[0], preferred_element_type=jnp.float32)

    @pl.when(step == count - 1)
    def _():
        gate = gate_sum[...]
        out_ref[...] = (gate / (1.0 + jnp.exp(-gate)) * up_sum[...]).astype(out_ref.dtype)


def ffn(stacks, order, gate_weight, up_weight, t):
    n, rows, width = stacks[0].shape
    units = gate_weight.shape[2]
    weight_spec = pl.BlockSpec((1, width, units), lambda k, where: (0, where[0] ^ k, 0))
    return pl.pallas_call(
        functools.partial(ffn_kernel, order),
        out_shape=jax.ShapeDtypeStruct((rows, units), jnp.bfloat16),
        grid_spec=pltpu.PrefetchScalarGridSpec(
            num_scalar_prefetch=1,
            grid=(2 * n,),
            in_specs=[pl.BlockSpec((n, rows, width), lambda k, where: (0, 0, 0))] * 2
            + [weight_spec, weight_spec],
            out_specs=pl.BlockSpec((rows, units), lambda k, where: (0, 0)),
            scratch_shapes=[pltpu.VMEM((rows, units), jnp.float32)] * 2,
        ),
        compiler_params=pltpu.CompilerParams(vmem_limit_bytes=BIG_VMEM),
        cost_estimate=SMALL_COST,
        name="ffn",
    )(t.reshape(1).astype(jnp.int32), *stacks, gate_weight, up_weight)


def chunks_of(width):
    lanes = 128
    if width % lanes or width < 2 * lanes:
        return [(0, width)]
    first = (width // lanes + 1) // 2 * lanes
    return [(0, first), (first, width - first)]


def one_hot(positions, count):
    selector = (positions[:, None] == jnp.arange(count, dtype=jnp.int32)[None, :]).astype(
        jnp.bfloat16
    )
    return lax.optimization_barrier(selector)


def pick_rows(selector, source):
    return jnp.dot(selector, source, preferred_element_type=jnp.float32).astype(jnp.bfloat16)


def after(value, *others):
    if not others:
        return value
    return lax.optimization_barrier((value,) + others)[0]


def columns_to_device(own, t, nt, off, width):
    block = own.shape[1] // nt
    found = []
    for k in range(nt):
        piece = lax.dynamic_slice(own, (0, (t ^ k) * block + off), (own.shape[0], width))
        found.append(xor_permute(piece, "tensor", nt, k) if k else piece)
    return found


def columns_in_two(own, t, off, width, *earlier):
    block = own.shape[1] // 4
    mine, near, far, both = [
        lax.dynamic_slice(own, (0, (t ^ k) * block + off), (own.shape[0], width)) for k in range(4)
    ]
    before_far, before_near = earlier or ((), ())
    first = xor_permute(after(jnp.stack([far, both]), *before_far), "tensor", 4, 2)
    pair = jnp.stack([near, after(first, *before_near)[1]])
    return [mine, first, xor_permute(pair, "tensor", 4, 1)]


def rows_to_device(pieces, nt):
    return [xor_permute(pieces[k], "tensor", nt, k) if k else pieces[k] for k in range(nt)]


T_AT, Q_AT, KEEP_AT, GIVE_AT, MINE_AT, MEMBER_AT = range(6)


def full_spec(shape):
    return pl.BlockSpec(shape, memory_space=pltpu.VMEM)


def align_kernel(nt, half, sub, flags_ref, place_ref, *refs):
    mine, first, second = refs[:3]
    outs = refs[3:]
    rows, width = mine.shape
    lane = lax.broadcasted_iota(jnp.int32, (rows, rows), 1)
    q = flags_ref[Q_AT]
    for k in range(half):
        start = pl.multiple_of((q ^ k) * sub, sub)
        place = jnp.concatenate(
            [place_ref[pl.ds(start + b * half * sub, sub), :] for b in range(nt)], axis=0
        )
        total = jnp.zeros((rows, width), jnp.float32)
        for m in range(nt):
            selector = jnp.where(place - m * rows == lane, 1.0, 0.0).astype(jnp.bfloat16)
            source = (mine[...], second[0], first[0], second[1])[m]
            total = total + jnp.dot(selector, source, preferred_element_type=jnp.float32)
        outs[k][...] = total.astype(jnp.bfloat16)


def align(flags, place, sources, half, sub):
    nt = 4
    rows, width = sources[0].shape
    piece = jax.ShapeDtypeStruct((rows, width), jnp.bfloat16)
    return pl.pallas_call(
        functools.partial(align_kernel, nt, half, sub),
        out_shape=[piece] * half,
        in_specs=[pl.BlockSpec(memory_space=pltpu.SMEM), full_spec(place.shape)]
        + [full_spec(source.shape) for source in sources],
        out_specs=[full_spec((rows, width))] * half,
        compiler_params=pltpu.CompilerParams(vmem_limit_bytes=BIG_VMEM),
        cost_estimate=SMALL_COST,
        name="align",
    )(flags, place, *sources)


def sums_kernel(half, tile, flags_ref, *refs):
    parts, sent_ref, kept_ref = refs[:half], refs[half], refs[half + 1]
    gives = [jnp.where(flags_ref[MEMBER_AT + k] == flags_ref[GIVE_AT], 1.0, 0.0) for k in range(half)]
    keeps = [jnp.where(flags_ref[MEMBER_AT + k] == flags_ref[KEEP_AT], 1.0, 0.0) for k in range(half)]

    @pl.loop(0, sent_ref.shape[0] // tile)
    def _(i):
        at = pl.ds(pl.multiple_of(i * tile, tile), tile)
        sent = kept = None
        for k in range(half):
            part = parts[k][at, :].astype(jnp.float32)
            sent = part * gives[k] if k == 0 else sent + part * gives[k]
            kept = part * keeps[k] if k == 0 else kept + part * keeps[k]
        sent_ref[at, :] = sent.astype(sent_ref.dtype)
        kept_ref[at, :] = kept


def sums(flags, parts):
    rows, width = parts[0].shape
    tile = min(32, rows)
    spec = full_spec((rows, width))
    return pl.pallas_call(
        functools.partial(sums_kernel, len(parts), tile),
        out_shape=[
            jax.ShapeDtypeStruct((rows, width), jnp.bfloat16),
            jax.ShapeDtypeStruct((rows, width), jnp.float32),
        ],
        in_specs=[pl.BlockSpec(memory_space=pltpu.SMEM)] + [spec] * len(parts),
        out_specs=[spec, spec],
        compiler_params=pltpu.CompilerParams(vmem_limit_bytes=BIG_VMEM),
        cost_estimate=SMALL_COST,
        name="sums",
    )(flags, *parts)


def mean_kernel(scale_ref, kept_ref, other_ref, mine_ref, near_ref, far_ref):
    sub = mine_ref.shape[0]
    scale = scale_ref[0]
    for m in range(4):
        at = pl.ds(m * sub, sub)
        total = kept_ref[at, :] + other_ref[at, :].astype(jnp.float32)
        value = (total * scale).astype(mine_ref.dtype)
        if m < 2:
            (mine_ref, near_ref)[m][...] = value
        else:
            far_ref[m - 2] = value


def mean_of(scale, kept, other):
    rows, width = kept.shape
    one, two = (rows // 4, width), (2, rows // 4, width)
    return pl.pallas_call(
        mean_kernel,
        out_shape=[jax.ShapeDtypeStruct(shape, jnp.bfloat16) for shape in (one, one, two)],
        in_specs=[pl.BlockSpec(memory_space=pltpu.SMEM)] + [full_spec((rows, width))] * 2,
        out_specs=[full_spec(one), full_spec(one), full_spec(two)],
        compiler_params=pltpu.CompilerParams(vmem_limit_bytes=BIG_VMEM),
        cost_estimate=SMALL_COST,
        name="mean",
    )(scale, kept, other)


def assemble_kernel(half, nt, spans, flags_ref, *refs):
    groups, out_ref = refs[:-1], refs[-1]
    sub = groups[0].shape[1]
    block = out_ref.shape[1] // nt
    mine = flags_ref[MINE_AT] != 0

    @pl.when(mine)
    def _():
        for k in range(half):
            at = pl.multiple_of((flags_ref[Q_AT] ^ k) * sub, sub)
            for m in range(nt):
                left = pl.multiple_of((flags_ref[T_AT] ^ m) * block, 128)
                for c, (off, width) in enumerate(spans):
                    out_ref[pl.ds(at, sub), pl.ds(left + off, width)] = groups[c * half + k][m]

    @pl.when(jnp.logical_not(mine))
    def _():
        out_ref[...] = jnp.zeros_like(out_ref)


def assemble(flags, gathered, spans, rows, model):
    half = len(gathered[0])
    nt = gathered[0][0].shape[0]
    groups = [piece for group in gathered for piece in group]
    return pl.pallas_call(
        functools.partial(assemble_kernel, half, nt, spans),
        out_shape=jax.ShapeDtypeStruct((rows, model), jnp.bfloat16),
        in_specs=[pl.BlockSpec(memory_space=pltpu.SMEM)]
        + [full_spec(piece.shape) for piece in groups],
        out_specs=full_spec((rows, model)),
        compiler_params=pltpu.CompilerParams(vmem_limit_bytes=BIG_VMEM),
        cost_estimate=SMALL_COST,
        name="assemble",
    )(flags, *groups)


class TwoClusters:
    def __init__(self, own, perm, cluster, owners, e, t, ne, nt):
        self.own, self.t, self.ne, self.nt = own, t, ne, nt
        rows, model = own.shape
        half = self.half = ne // 2
        self.sub = rows // half
        self.spans = chunks_of(model // nt)
        self.cluster, self.owners, self.e = cluster, owners, e
        q, side = e % half, e // half
        self.place = (((perm // rows) ^ t) * rows + perm % rows).reshape(-1, 1)
        experts = jnp.arange(ne, dtype=jnp.int32)
        near = (e ^ jnp.arange(half, dtype=jnp.int32))[:, None] == experts[None, :]
        member = jnp.sum(jnp.where(near, cluster[None, :], 0), axis=1)
        sides = owners // half
        keep = jnp.where(sides[0:1] == side, 0, 1)
        give = jnp.where(sides[0:1] != side, 0, 1)
        mine = jnp.where(jnp.where(keep == 0, owners[0:1], owners[1:2]) == e, 1, 0)
        self.flags = jnp.concatenate(
            [t.reshape(1), q.reshape(1), keep, give, mine, member]
        ).astype(jnp.int32)
        self.sizes = jnp.sum(
            (cluster[None, :] == jnp.arange(2, dtype=jnp.int32)[:, None]).astype(jnp.float32),
            axis=1,
        )
        self.scale = 1.0 / jnp.where(keep == 0, self.sizes[0:1], self.sizes[1:2])

    def columns(self, c, *earlier):
        return columns_in_two(self.own, self.t, *self.spans[c], *earlier)

    def send_aligned(self, sources, *earlier):
        sources = all_after(sources, *earlier)
        pieces = align(self.flags, self.place, sources, self.half, self.sub)
        sent = [
            xor_permute(piece, "expert", self.ne, k) if k else piece
            for k, piece in enumerate(pieces)
        ]
        return pieces[0], sent

    def back(self, pieces):
        mine, near, far = pieces
        first = xor_permute(far, "tensor", 4, 2)
        second = xor_permute(jnp.stack([near, first[1]]), "tensor", 4, 1)
        return jnp.stack([mine, second[0], first[0], second[1]])

    def out(self, lines):
        return [
            xor_permute(lines, "expert", self.ne, k) if k else lines for k in range(self.half)
        ]

    def finish(self, gathered, arrived):
        rows, model = self.own.shape
        first = assemble(self.flags, gathered, self.spans, rows, model)
        sides = self.owners // self.half

        def second(args):
            first, arrived = args
            near = self.cluster[self.e ^ jnp.arange(self.half, dtype=jnp.int32)]
            again = []
            for parts in arrived:
                total = jnp.zeros(parts[0].shape, jnp.float32)
                for k in range(self.half):
                    total = total + jnp.where(near[k] == 1, parts[k].astype(jnp.float32), 0.0)
                other = xor_permute(total.astype(jnp.bfloat16), "expert", self.ne, self.half)
                scale = (1.0 / self.sizes[1]).reshape(1)
                again.append(self.out(self.back(mean_of(scale, total, other))))
            mine = jnp.where(self.owners[1:2] == self.e, 1, 0).astype(jnp.int32)
            flags = jnp.concatenate(
                [self.flags[:MINE_AT], mine, self.flags[MINE_AT + 1 :]]
            )
            return first + assemble(flags, again, self.spans, rows, model)

        return lax.cond(
            sides[0] == sides[1], second, lambda args: args[0], (first, arrived)
        )


def merge_any(own, perm, cluster, owners, e, t, ne, nt):
    rows, model = own.shape
    block = model // nt
    clusters = owners.shape[0]
    sub = rows // ne
    placed = ((perm // rows) ^ t) * rows + perm % rows
    placed = placed.reshape(nt, ne, sub).transpose(1, 0, 2).reshape(-1)
    aligned = pick_rows(
        one_hot(placed, rows * nt), jnp.concatenate(columns_to_device(own, t, nt, 0, block))
    )
    arrived = lax.all_to_all(aligned, "expert", split_axis=0, concat_axis=0, tiled=True)
    arrived = arrived.reshape(ne, nt, sub, block)
    member = cluster[None, :] == jnp.arange(clusters, dtype=jnp.int32)[:, None]
    inverse = 1.0 / jnp.sum(member.astype(jnp.float32), axis=1)
    means = []
    for c in range(clusters):
        total = jnp.sum(
            jnp.where(member[c][:, None, None, None], arrived.astype(jnp.float32), 0.0), axis=0
        )
        means.append((total * inverse[c]).astype(jnp.bfloat16))
    back = jnp.stack(rows_to_device(jnp.stack(means, axis=1), nt))
    back = jnp.take(back, jnp.arange(nt, dtype=jnp.int32) ^ t, axis=0)
    lines = back.transpose(1, 2, 0, 3).reshape(clusters, sub, model)
    outgoing = jnp.zeros((ne, sub, model), jnp.bfloat16).at[owners].set(lines)
    return lax.all_to_all(
        outgoing.reshape(ne * sub, model), "expert", split_axis=0, concat_axis=0, tiled=True
    )


def on_device(
    tokens,
    routes,
    gate_values,
    probe_rows,
    gate_weight,
    up_weight,
    down_weight,
    hidden_perm,
    cluster,
    owners,
):
    ne = lax.axis_size("expert")
    nt = lax.axis_size("tensor")
    e = lax.axis_index("expert").astype(jnp.int32)
    t = lax.axis_index("tensor").astype(jnp.int32)
    tok_rows, top = routes.shape
    capacity = tok_rows * top * 5 // (4 * ne)
    own = down_weight[0]
    model = own.shape[1]
    block = model // nt

    perm = jnp.concatenate(gather_small(hidden_perm[0], nt))
    two = None
    if ne == 8 and nt == 4 and owners.shape[0] == 2:
        two = TwoClusters(own, perm, cluster, owners, e, t, ne, nt)

    flat = routes.reshape(-1)
    pairs = jnp.arange(flat.shape[0], dtype=jnp.int32)
    earlier = (flat[:, None] == flat[None, :]) & (pairs[None, :] < pairs[:, None])
    target = flat * capacity + jnp.sum(earlier.astype(jnp.int32), axis=1)
    target = target.reshape(tok_rows, top)
    slots = jnp.arange(ne * capacity, dtype=jnp.int32)
    selector = jnp.zeros((ne * capacity, tok_rows), jnp.bool_)
    for k in range(top):
        selector = selector | (slots[:, None] == target[:, k][None, :])
    outgoing = jnp.dot(
        selector.astype(jnp.bfloat16), tokens, preferred_element_type=jnp.float32
    ).astype(jnp.bfloat16)
    arrived = lax.all_to_all(outgoing, "expert", split_axis=0, concat_axis=0, tiled=True)
    routed = arrived.shape[0]
    stacked = jnp.concatenate([arrived, probe_rows], axis=0)
    if two is not None:
        last = len(two.spans) - 1
        source = two.columns(0)
        mark, sent = two.send_aligned(source)
        parts = [sent]
        stacked = after(stacked, source[1])
    even, order = gather_even(stacked, nt, *([] if two is None else [mark]))
    odd = xor_permute(even, "tensor", nt, 1)
    hidden = ffn((even, odd), order, gate_weight, up_weight, t)
    probe_hidden = hidden[routed:]
    everyone = lax.all_gather(probe_hidden, "expert", axis=0)
    at_owner = jnp.arange(ne, dtype=jnp.int32) == owners[cluster[e]]
    partner = jnp.sum(
        jnp.where(at_owner[:, None, None], everyone.astype(jnp.float32), 0.0), axis=0
    ).astype(jnp.bfloat16)

    def correlate(partner):
        partner_full = lax.all_gather(partner, "tensor", axis=1, tiled=True)
        found = lax.dot_general(
            probe_hidden, partner_full, (((0,), (0,)), ((), ())), preferred_element_type=jnp.float32
        )
        return found / probe_hidden.shape[0]

    send, keep = down(hidden, routed, own, t, nt)
    if two is not None:
        others, kept = [], []
        for c in range(last + 1):
            if c < last:
                source = two.columns(c + 1, (even,), (*parts[c][1:], send))
                mark, sent = two.send_aligned(source, mark)
                parts.append(sent)
            ready = all_after(parts[c], *((others[-1], returned) if c else (send,)))
            given, own_sum = sums(two.flags, ready)
            others.append(xor_permute(given, "expert", ne, two.half))
            kept.append(own_sum)
            if not c:
                returned = sum_tensor(send, after(keep, mark), nt)
        lines = two.back(mean_of(two.scale, kept[0], after(others[0], kept[-1])))
    else:
        returned = sum_tensor(send, keep, nt)
        correlation = correlate(partner)
    home = lax.all_to_all(returned, "expert", split_axis=0, concat_axis=0, tiled=True)
    chooser = (target.T.reshape(-1)[:, None] == slots[None, :]).astype(jnp.bfloat16)
    picked = jnp.dot(chooser, home, preferred_element_type=jnp.float32)
    picked = picked.reshape(top, tok_rows, block)
    mixed = jnp.sum(gate_values.T[:, :, None] * picked, axis=0).astype(jnp.bfloat16)

    if two is not None:
        gathered = [two.out(lines)]
        for c in range(1, len(two.spans)):
            means = mean_of(two.scale, kept[c], after(others[c], *gathered[-1][1:]))
            lines = two.back(means)
            gathered.append(two.out(lines))
        correlation = correlate(after(partner, lines))
        gathered[-1][0] = after(gathered[-1][0], mixed, correlation)
        merged = two.finish(gathered, parts)
    else:
        merged = merge_any(own, perm, cluster, owners, e, t, ne, nt)
    return (mixed, correlation[None], merged[None])


def solution(mesh):
    in_specs = (
        P("expert", "tensor"),
        P("expert", None),
        P("expert", None),
        P(None, "tensor"),
        P("expert", None, "tensor"),
        P("expert", None, "tensor"),
        P("expert", "tensor", None),
        P("expert", "tensor"),
        P(),
        P(),
    )
    out_specs = (P("expert", "tensor"), P("expert", "tensor", None), P("expert", "tensor", None))
    return jax.shard_map(
        on_device, mesh=mesh, in_specs=in_specs, out_specs=out_specs, check_vma=False
    )
```

```python
import functools

import jax
import jax.numpy as jnp
from jax import lax
from jax.experimental import pallas as pl
from jax.experimental.pallas import tpu as pltpu
from jax.sharding import PartitionSpec as P


def xor_permute(value, axis, size, k):
    return lax.ppermute(value, axis, [(i, i ^ k) for i in range(size)])


def gather_tensor(value, size):
    held = {0: value}
    bit = size // 2
    while bit:
        for k in sorted(held):
            held[k ^ bit] = xor_permute(held[k], "tensor", size, bit)
        bit //= 2
    return [held[k] for k in range(size)]


def scatter_tensor(parts, size):
    held = dict(enumerate(parts))
    bit = 1
    while bit < size:
        for k in sorted(held):
            if k & bit:
                arrived = xor_permute(
                    held.pop(k).astype(jnp.bfloat16), "tensor", size, bit
                )
                held[k ^ bit] = held[k ^ bit] + arrived.astype(jnp.float32)
        bit *= 2
    return held[0]


def ffn_kernel(count, where_ref, *refs):
    parts = refs[:count]
    gate_ref, up_ref, out_ref, gate_sum, up_sum = refs[count:]
    step = pl.program_id(0)

    @pl.when(step == 0)
    def _():
        gate_sum[...] = jnp.zeros_like(gate_sum)
        up_sum[...] = jnp.zeros_like(up_sum)

    for k in range(count):

        @pl.when(step == k)
        def _(k=k):
            rows = parts[k][...]
            gate_sum[...] += jnp.dot(rows, gate_ref[0], preferred_element_type=jnp.float32)
            up_sum[...] += jnp.dot(rows, up_ref[0], preferred_element_type=jnp.float32)

    @pl.when(step == count - 1)
    def _():
        gate = gate_sum[...]
        out_ref[...] = (gate / (1.0 + jnp.exp(-gate)) * up_sum[...]).astype(out_ref.dtype)


def ffn(parts, gate_weight, up_weight, t):
    count = len(parts)
    rows, width = parts[0].shape
    units = gate_weight.shape[2]
    weight_spec = pl.BlockSpec((1, width, units), lambda k, where: (0, where[0] ^ k, 0))
    return pl.pallas_call(
        functools.partial(ffn_kernel, count),
        out_shape=jax.ShapeDtypeStruct((rows, units), jnp.bfloat16),
        grid_spec=pltpu.PrefetchScalarGridSpec(
            num_scalar_prefetch=1,
            grid=(count,),
            in_specs=[pl.BlockSpec((rows, width), lambda k, where: (0, 0))] * count
            + [weight_spec, weight_spec],
            out_specs=pl.BlockSpec((rows, units), lambda k, where: (0, 0)),
            scratch_shapes=[pltpu.VMEM((rows, units), jnp.float32)] * 2,
        ),
        compiler_params=pltpu.CompilerParams(vmem_limit_bytes=48 * 1024 * 1024),
        cost_estimate=pl.CostEstimate(
            flops=4 * rows * width * count * units,
            bytes_accessed=2 * (2 * width * count * units + rows * width * count + rows * units),
            transcendentals=rows * units,
        ),
        name="ffn",
    )(t.reshape(1).astype(jnp.int32), *parts, gate_weight, up_weight)


def chunks_of(width):
    lanes = 128
    if width % lanes or width < 2 * lanes:
        return [(0, width)]
    first = (width // lanes + 1) // 2 * lanes
    return [(0, first), (first, width - first)]


def one_hot(positions, count):
    selector = (positions[:, None] == jnp.arange(count, dtype=jnp.int32)[None, :]).astype(
        jnp.bfloat16
    )
    return lax.optimization_barrier(selector)


def pick_rows(selector, source):
    return jnp.dot(selector, source, preferred_element_type=jnp.float32).astype(jnp.bfloat16)


def after(value, *others):
    return lax.optimization_barrier((value,) + others)[0]


def columns_to_device(own, t, nt, off, width):
    block = own.shape[1] // nt
    found = []
    for k in range(nt):
        piece = lax.dynamic_slice(own, (0, (t ^ k) * block + off), (own.shape[0], width))
        found.append(xor_permute(piece, "tensor", nt, k) if k else piece)
    return jnp.concatenate(found, axis=0)


def rows_to_device(pieces, nt):
    return [xor_permute(pieces[k], "tensor", nt, k) if k else pieces[k] for k in range(nt)]


def merge_two(own, perm, cluster, owners, e, t, ne, nt, beside):
    rows, model = own.shape
    half = ne // 2
    block = model // nt
    sub = rows // half
    q, side = e % half, e // half
    placed = ((perm // rows) ^ t) * rows + perm % rows
    placed = placed.reshape(nt, half, sub)
    member = cluster[(e ^ jnp.arange(half, dtype=jnp.int32))]
    inverse = 1.0 / jnp.sum(
        (cluster[None, :] == jnp.arange(2, dtype=jnp.int32)[:, None]).astype(jnp.float32), axis=1
    )
    owner_side = owners // half
    keep = jnp.where(owner_side[0] == side, 0, 1)
    give = jnp.where(owner_side[0] != side, 0, 1)
    spans = chunks_of(block)
    order = [(q ^ k) for k in range(half)]
    selectors = [
        one_hot(lax.dynamic_index_in_dim(placed, j, 1, keepdims=False).reshape(-1), rows * nt)
        for j in order
    ]

    partials = []
    for off, width in spans:
        source = columns_to_device(own, t, nt, off, width)
        arrived = [None] * half
        for k in list(range(1, half)) + [0]:
            aligned = pick_rows(selectors[k], source)
            arrived[k] = xor_permute(aligned, "expert", ne, k) if k else aligned
        partials.append(arrived)

    def partial_of(arrived, which):
        total = jnp.zeros(arrived[0].shape, jnp.float32)
        for k in range(half):
            total = total + jnp.where(member[k] == which, arrived[k].astype(jnp.float32), 0.0)
        return total

    def finish(partials, kept, given, beside=()):
        gathered = []
        for place, (arrived, (off, width)) in enumerate(zip(partials, spans)):
            sent = partial_of(arrived, given).astype(jnp.bfloat16)
            if place == 0 and beside:
                sent = after(sent, beside[0])
            other = xor_permute(sent, "expert", ne, half)
            mean = (
                (partial_of(arrived, kept) + other.astype(jnp.float32)) * inverse[kept]
            ).astype(jnp.bfloat16)
            lines = jnp.stack(rows_to_device(mean.reshape(nt, sub, width), nt))
            if place == len(spans) - 1 and beside:
                lines = after(lines, beside[1])
            gathered.append(
                [xor_permute(lines, "expert", ne, k) if k else lines for k in range(half)]
            )
        mine = owners[kept] == e
        order_t = jnp.arange(nt, dtype=jnp.int32) ^ t
        out = []
        for j in range(half):
            wide = []
            for group in gathered:
                chosen = group[0]
                for k in range(1, half):
                    chosen = jnp.where((q ^ j) == k, group[k], chosen)
                wide.append(chosen)
            out.append(jnp.concatenate(wide, axis=2))
        joined = jnp.stack(out)
        ordered = []
        for b in range(nt):
            chosen = joined[:, 0]
            for k in range(1, nt):
                chosen = jnp.where(order_t[b] == k, joined[:, k], chosen)
            ordered.append(chosen)
        whole = jnp.concatenate(ordered, axis=2).reshape(rows, model)
        return jnp.where(mine, whole, jnp.zeros_like(whole))

    first = finish(partials, keep, give, beside)

    def second(args):
        first, partials = args
        return first + finish(partials, 1, 1)

    return lax.cond(
        owner_side[0] == owner_side[1], second, lambda args: args[0], (first, partials)
    )


def merge_any(own, perm, cluster, owners, e, t, ne, nt, beside):
    rows, model = own.shape
    block = model // nt
    clusters = owners.shape[0]
    sub = rows // ne
    placed = ((perm // rows) ^ t) * rows + perm % rows
    placed = placed.reshape(nt, ne, sub).transpose(1, 0, 2).reshape(-1)
    aligned = pick_rows(
        one_hot(placed, rows * nt), columns_to_device(own, t, nt, 0, block)
    )
    arrived = lax.all_to_all(aligned, "expert", split_axis=0, concat_axis=0, tiled=True)
    arrived = arrived.reshape(ne, nt, sub, block)
    member = cluster[None, :] == jnp.arange(clusters, dtype=jnp.int32)[:, None]
    inverse = 1.0 / jnp.sum(member.astype(jnp.float32), axis=1)
    means = []
    for c in range(clusters):
        total = jnp.sum(
            jnp.where(member[c][:, None, None, None], arrived.astype(jnp.float32), 0.0), axis=0
        )
        means.append((total * inverse[c]).astype(jnp.bfloat16))
    back = jnp.stack(rows_to_device(jnp.stack(means, axis=1), nt))
    back = jnp.take(back, jnp.arange(nt, dtype=jnp.int32) ^ t, axis=0)
    lines = back.transpose(1, 2, 0, 3).reshape(clusters, sub, model)
    outgoing = jnp.zeros((ne, sub, model), jnp.bfloat16).at[owners].set(lines)
    return lax.all_to_all(
        outgoing.reshape(ne * sub, model), "expert", split_axis=0, concat_axis=0, tiled=True
    )


def on_device(
    tokens,
    routes,
    gate_values,
    probe_rows,
    gate_weight,
    up_weight,
    down_weight,
    hidden_perm,
    cluster,
    owners,
):
    ne = lax.axis_size("expert")
    nt = lax.axis_size("tensor")
    e = lax.axis_index("expert").astype(jnp.int32)
    t = lax.axis_index("tensor").astype(jnp.int32)
    tok_rows, top = routes.shape
    capacity = tok_rows * top * 5 // (4 * ne)
    own = down_weight[0]
    model = own.shape[1]
    block = model // nt

    perm = jnp.concatenate(gather_tensor(hidden_perm[0], nt))

    flat = routes.reshape(-1)
    pairs = jnp.arange(flat.shape[0], dtype=jnp.int32)
    earlier = (flat[:, None] == flat[None, :]) & (pairs[None, :] < pairs[:, None])
    target = flat * capacity + jnp.sum(earlier.astype(jnp.int32), axis=1)
    target = target.reshape(tok_rows, top)
    slots = jnp.arange(ne * capacity, dtype=jnp.int32)
    selector = jnp.zeros((ne * capacity, tok_rows), jnp.bool_)
    for k in range(top):
        selector = selector | (slots[:, None] == target[:, k][None, :])
    outgoing = jnp.dot(
        selector.astype(jnp.bfloat16), tokens, preferred_element_type=jnp.float32
    ).astype(jnp.bfloat16)
    arrived = lax.all_to_all(outgoing, "expert", split_axis=0, concat_axis=0, tiled=True)
    routed = arrived.shape[0]
    stacked = jnp.concatenate([arrived, probe_rows], axis=0)
    hidden = ffn(gather_tensor(stacked, nt), gate_weight, up_weight, t)
    routed_hidden, probe_hidden = hidden[:routed], hidden[routed:]

    parts = [
        jnp.dot(
            routed_hidden,
            lax.dynamic_slice(own, (0, (t ^ k) * block), (own.shape[0], block)),
            preferred_element_type=jnp.float32,
        )
        for k in range(nt)
    ]
    returned = scatter_tensor(parts, nt).astype(jnp.bfloat16)
    home = lax.all_to_all(returned, "expert", split_axis=0, concat_axis=0, tiled=True)
    chooser = (target.T.reshape(-1)[:, None] == slots[None, :]).astype(jnp.bfloat16)
    picked = jnp.dot(chooser, home, preferred_element_type=jnp.float32)
    picked = picked.reshape(top, tok_rows, block)
    mixed = jnp.sum(gate_values.T[:, :, None] * picked, axis=0).astype(jnp.bfloat16)

    merge = merge_two if ne == 8 and owners.shape[0] == 2 else merge_any
    merged = merge(own, perm, cluster, owners, e, t, ne, nt, (hidden, returned))

    everyone = lax.all_gather(probe_hidden, "expert", axis=0)
    partner = lax.dynamic_index_in_dim(everyone, owners[cluster[e]], 0, keepdims=False)
    partner_full = lax.all_gather(partner, "tensor", axis=1, tiled=True)
    correlation = (
        lax.dot_general(
            probe_hidden, partner_full, (((0,), (0,)), ((), ())), preferred_element_type=jnp.float32
        )
        / probe_hidden.shape[0]
    )
    return (mixed, correlation[None], merged[None])


def solution(mesh):
    in_specs = (
        P("expert", "tensor"),
        P("expert", None),
        P("expert", None),
        P(None, "tensor"),
        P("expert", None, "tensor"),
        P("expert", None, "tensor"),
        P("expert", "tensor", None),
        P("expert", "tensor"),
        P(),
        P(),
    )
    out_specs = (P("expert", "tensor"), P("expert", "tensor", None), P("expert", "tensor", None))
    return jax.shard_map(
        on_device, mesh=mesh, in_specs=in_specs, out_specs=out_specs, check_vma=False
    )
```
